256 devices in a mesh: dp: 32 (over x, y, core), proto: 8 (over z).
Axes of the slice: x: 4, y: 4, z: 8, core: 2. Of those that a mesh axis runs over, the one named last changes fastest.
Arguments:
- student_crops: bfloat16 [4096, 256], P('dp'), may hold values from -0.6 to 0.6
- teacher_crops: bfloat16 [4096, 256], P('dp'), may hold values from -5 to 5
- student_patches: bfloat16 [32768, 256], P('dp'), may hold values from -0.6 to 0.6
- teacher_patches: bfloat16 [32768, 256], P('dp'), may hold values from -5 to 5
- patch_mask: int32 [128, 96], P('dp'), may hold values from 0 to 255, as said below
- student_protos: bfloat16 [256, 65536], P(None, 'proto'), may hold values from -0.6 to 0.6
- teacher_protos: bfloat16 [256, 65536], P(None, 'proto'), may hold values from -5 to 5
Outputs:
- proto_grad: float32 [256, 65536], P('dp', 'proto')
- crop_grad: float32 [4096, 256], P(('dp', 'proto'))
- patch_grad: float32 [32768, 256], P(('dp', 'proto'))
The draws below stay inside these ranges and needn't reach their ends.
Inputs may be any that keep to these rules, and one draw needn't show every extreme that they name: `patch_mask`: each row holds 96 different patch positions of one image.
All inputs are finite; a program needn't handle non-finite values.
Results may differ from the reference program's by a relative error of at most 0.0052.
Values sent between devices are 32-bit elements; how exact they have to be, the bound alone decides.
No kernel may reach another device: no remote copies, remote signals or barrier semaphores. Data moves between devices by JAX's collectives and lax.ppermute only.
A program may use at most 128 MiB of HBM per device.

```python
import jax
import jax.numpy as jnp
from jax import lax

B = 256
K = 65536
CROPS_DEV = 128
IMG_DEV = 4
PATCHES = 256
MASKED = 96
ITERS = 3
CROPS = 4096
IMAGES = 128


centre_count = 16


def shared_centres(key):
    centres = jax.random.truncated_normal(jax.random.fold_in(key, 1), -3.0, 3.0, (centre_count, B), jnp.float32)
    labels = jax.random.permutation(jax.random.fold_in(key, 2), centre_count).astype(jnp.int32)
    return (centres, labels)


def shard_homes(labels, rows, per_shard):
    shard = jnp.arange(rows, dtype=jnp.int32) // per_shard
    return labels[shard % centre_count]


def column_groups():
    index = jnp.arange(K, dtype=jnp.int32)
    bounds = jnp.arange(1, centre_count, dtype=jnp.int32)
    above = index[:, None] * (centre_count * centre_count) >= (bounds * bounds)[None, :] * K
    return jnp.sum(above.astype(jnp.int32), axis=1)


def clustered_rows(key, home, centres, noise, lower, upper):
    keys = jax.random.split(key, 2)
    rows = home.shape[0]
    beside = (home + 1) % centre_count
    mixing = jax.random.uniform(keys[0], (rows, 1), jnp.float32, 0.3, 0.7)
    strength = jax.random.uniform(keys[1], (rows, 1), jnp.float32, lower, upper)
    direction = mixing * centres[home] + (1.0 - mixing) * centres[beside]
    return strength * direction + jnp.sqrt(1.0 - strength * strength) * noise


def drawn_columns(key, centres, noise, lower, upper):
    group = column_groups()
    strength = jax.random.uniform(key, (1, K), jnp.float32, lower, upper)
    return strength * centres.T[:, group] + jnp.sqrt(1.0 - strength * strength) * noise


def spread_factor(key, shape):
    return jnp.exp(jax.random.uniform(key, shape, jnp.float32, -0.6931472, 0.6931472))


def draw_teacher_crops(key, part):
    centres, labels = shared_centres(key)
    key = jax.random.fold_in(key, 11)
    noise_key, row_key = jax.random.split(key)
    home = shard_homes(labels, CROPS, CROPS_DEV)
    noise = jax.random.truncated_normal(noise_key, -3.0, 3.0, (CROPS, B), jnp.float32)
    values = clustered_rows(row_key, home, centres, noise, 0.5, 0.75)
    return values.astype(jnp.bfloat16)


def draw_teacher_patches(key, part):
    centres, labels = shared_centres(key)
    key = jax.random.fold_in(key, 12)
    noise_key, row_key = jax.random.split(key)
    count = IMAGES * PATCHES
    home = shard_homes(labels, count, IMG_DEV * PATCHES)
    noise = jax.random.truncated_normal(noise_key, -3.0, 3.0, (count, B), jnp.float32)
    values = clustered_rows(row_key, home, centres, noise, 0.5, 0.75)
    return values.astype(jnp.bfloat16)


def draw_student_crops(key, part):
    centres, labels = shared_centres(key)
    key = jax.random.fold_in(key, 14)
    noise_key, row_key, scale_key = jax.random.split(key, 3)
    home = shard_homes(labels, CROPS, CROPS_DEV)
    factor = spread_factor(scale_key, (CROPS, 1)) * 0.0625
    noise = jax.random.truncated_normal(noise_key, -3.0, 3.0, (CROPS, B), jnp.float32)
    values = clustered_rows(row_key, home, centres, noise, 0.65, 0.85)
    return (factor * values).astype(jnp.bfloat16)


def draw_student_patches(key, part):
    centres, labels = shared_centres(key)
    key = jax.random.fold_in(key, 15)
    noise_key, row_key, scale_key = jax.random.split(key, 3)
    count = IMAGES * PATCHES
    home = shard_homes(labels, count, IMG_DEV * PATCHES)
    factor = spread_factor(scale_key, (count, 1)) * 0.0625
    noise = jax.random.truncated_normal(noise_key, -3.0, 3.0, (count, B), jnp.float32)
    values = clustered_rows(row_key, home, centres, noise, 0.65, 0.85)
    return (factor * values).astype(jnp.bfloat16)


def draw_teacher_protos(key, part):
    centres, labels = shared_centres(key)
    key = jax.random.fold_in(key, 13)
    noise_key, column_key = jax.random.split(key)
    noise = jax.random.truncated_normal(noise_key, -3.0, 3.0, (B, K), jnp.float32)
    values = drawn_columns(column_key, centres, noise, 0.5, 0.75)
    return values.astype(jnp.bfloat16)


def draw_student_protos(key, part):
    centres, labels = shared_centres(key)
    key = jax.random.fold_in(key, 16)
    noise_key, column_key, scale_key = jax.random.split(key, 3)
    factor = spread_factor(scale_key, (1, K)) * 0.0625
    noise = jax.random.truncated_normal(noise_key, -3.0, 3.0, (B, K), jnp.float32)
    values = drawn_columns(column_key, centres, noise, 0.65, 0.85)
    return (factor * values).astype(jnp.bfloat16)


def draw_patch_mask(key, part):
    key = jax.random.fold_in(key, 7)
    scores = jax.random.randint(key, (IMAGES, PATCHES), 0, 4194304)
    scores = scores * PATCHES + jnp.arange(PATCHES, dtype=jnp.int32)[None, :]
    order = jnp.argsort(scores, axis=1)
    return order[:, :MASKED].astype(jnp.int32)


def setup_inputs(seed: int = 0) -> dict:
    seeds = jax.random.split(jax.random.key(seed), 8)
    return {
        "student_crops": draw_student_crops(jax.random.fold_in(seeds[7], 71), 0),
        "teacher_crops": draw_teacher_crops(jax.random.fold_in(seeds[7], 71), 0),
        "student_patches": draw_student_patches(jax.random.fold_in(seeds[7], 71), 0),
        "teacher_patches": draw_teacher_patches(jax.random.fold_in(seeds[7], 71), 0),
        "patch_mask": draw_patch_mask(jax.random.fold_in(seeds[7], 71), 0),
        "student_protos": draw_student_protos(jax.random.fold_in(seeds[7], 71), 0),
        "teacher_protos": draw_teacher_protos(jax.random.fold_in(seeds[7], 71), 0),
    }


EPS = 1e-06
TEACHER_TEMP = 0.07
STUDENT_TEMP = 0.1
LOSS_SCALE = 256.0

def unit_rows(x):
    xf = x.astype(jnp.float32)
    inv = lax.rsqrt(lax.optimization_barrier(jnp.sum(xf * xf, axis=-1, keepdims=True)) + EPS)
    return (xf * inv, inv)

def unit_cols(w):
    wf = w.astype(jnp.float32)
    inv = lax.rsqrt(lax.optimization_barrier(jnp.sum(wf * wf, axis=0, keepdims=True)) + EPS)
    return (wf * inv, inv)

def block_rows(count):
    return 512 if count % 512 == 0 else count

def teacher_exp(feats, teacher_w):
    count = feats.shape[0]
    blk = block_rows(count)
    blocks = feats.reshape(count // blk, blk, feats.shape[1])
    return lax.map(lambda z: jnp.exp(jnp.dot(z, teacher_w, preferred_element_type=jnp.float32) / TEACHER_TEMP).astype(jnp.bfloat16), blocks)

def balanced_assignment(exponent_matrix):
    rowscale = jnp.ones(exponent_matrix.shape[:2], jnp.float32)
    colscale = jnp.ones((exponent_matrix.shape[2],), jnp.float32)
    for step in range(ITERS):
        parts = lax.map(lambda pair: lax.optimization_barrier(jnp.sum(pair[0][:, None] * pair[1].astype(jnp.float32), axis=0)), (rowscale, exponent_matrix))
        colscale = 1.0 / lax.optimization_barrier(jnp.sum(parts, axis=0))
        rowscale = 1.0 / lax.map(lambda eb: lax.optimization_barrier(jnp.sum(eb.astype(jnp.float32) * colscale[None, :], axis=1)), exponent_matrix)
    return (rowscale, colscale)

def head_pass(wsum, student, exponent_matrix, rowscale, colscale, student_w):
    blocks = student.reshape(exponent_matrix.shape[0], exponent_matrix.shape[1], student.shape[1])

    def step(carry, items):
        feats, eblock, rows = items
        score = jnp.dot(feats, student_w, preferred_element_type=jnp.float32) / STUDENT_TEMP
        total = lax.optimization_barrier(jnp.sum(jnp.exp(score), axis=1, keepdims=True))
        prob = jnp.exp(score - jnp.log(total))
        target = rows[:, None] * eblock.astype(jnp.float32) * colscale[None, :]
        grad = (LOSS_SCALE * (prob - target) / STUDENT_TEMP).astype(jnp.bfloat16)
        carry = carry + jnp.dot(feats.T, grad, preferred_element_type=jnp.float32)
        fgrad = jnp.dot(grad, student_w.T, preferred_element_type=jnp.float32)
        return (carry, fgrad)
    wsum, fgrad = lax.scan(step, wsum, (blocks, exponent_matrix, rowscale))
    return (wsum, fgrad.reshape(student.shape[0], student.shape[1]))

def norm_back(xf, inv, fgrad):
    return (fgrad - xf * lax.optimization_barrier(jnp.sum(xf * fgrad, axis=-1, keepdims=True))) * inv

def reference(student_crops, teacher_crops, student_patches, teacher_patches, patch_mask, student_protos, teacher_protos):
    images, masked = patch_mask.shape
    patches = student_patches.shape[0] // images
    flat = (jnp.arange(images, dtype=jnp.int32)[:, None] * patches + patch_mask).reshape(-1)
    crop_f, crop_inv = unit_rows(student_crops)
    student_dino = crop_f.astype(jnp.bfloat16)
    teacher_dino = unit_rows(teacher_crops)[0].astype(jnp.bfloat16)
    student_ibot = unit_rows(jnp.take(student_patches, flat, axis=0))[0].astype(jnp.bfloat16)
    teacher_ibot = unit_rows(jnp.take(teacher_patches, flat, axis=0))[0].astype(jnp.bfloat16)
    wnorm, winv = unit_cols(student_protos)
    student_w = wnorm.astype(jnp.bfloat16)
    teacher_w = unit_cols(teacher_protos)[0].astype(jnp.bfloat16)
    exponent_global = teacher_exp(teacher_dino, teacher_w)
    exponent_patchwise = teacher_exp(teacher_ibot, teacher_w)
    row_count_global, column_count_global = balanced_assignment(exponent_global)
    row_count_patchwise, column_count_patchwise = balanced_assignment(exponent_patchwise)
    wsum = jnp.zeros(student_protos.shape, jnp.float32)
    wsum, fgrad_dino = head_pass(wsum, student_dino, exponent_global, row_count_global, column_count_global, student_w)
    wsum, fgrad_ibot = head_pass(wsum, student_ibot, exponent_patchwise, row_count_patchwise, column_count_patchwise, student_w)
    coldot = lax.optimization_barrier(jnp.sum(wnorm * wsum, axis=0, keepdims=True))
    proto_grad = (wsum - wnorm * coldot) * winv
    crop_grad = norm_back(crop_f, crop_inv, fgrad_dino)
    dense = jnp.zeros(student_patches.shape, jnp.float32).at[flat].add(fgrad_ibot)
    patch_f, patch_inv = unit_rows(student_patches)
    patch_grad = norm_back(patch_f, patch_inv, dense)
    return (proto_grad, crop_grad, patch_grad)
```

```python
import functools

import jax
import jax.numpy as jnp
from jax import lax
from jax.experimental import pallas as pl
from jax.experimental.pallas import tpu as pltpu
from jax.sharding import Mesh, PartitionSpec as P

ITERS = 3
EPS = 1e-06
TEACHER_TEMP = 0.07
STUDENT_TEMP = 0.1
LOSS_SCALE = 256.0
GRAD_SCALE = LOSS_SCALE / STUDENT_TEMP
LOG2E = 1.4426950408889634

BN = 512
RB = 128
F32 = jnp.float32
BF16 = jnp.bfloat16
VMEM_LIMIT = 48 * 1024 * 1024


def params():
    return pltpu.CompilerParams(
        dimension_semantics=("arbitrary",), vmem_limit_bytes=VMEM_LIMIT
    )


def unit(x):
    xf = x.astype(F32)
    return xf * lax.rsqrt(jnp.sum(xf * xf, axis=-1, keepdims=True) + EPS)


def unit_cols(w):
    wf = w.astype(F32)
    inv = lax.rsqrt(jnp.sum(wf * wf, axis=0, keepdims=True) + EPS)
    return wf * inv, inv


def prep_kernel(images, patches, masked, crops, patch_rows, mask, out):
    count = crops.shape[0]
    out[:count, :] = unit(crops[...])
    for i in range(images):
        place = lax.broadcasted_iota(jnp.int32, (masked, patches), 1)
        chosen = (place == mask[i * masked : (i + 1) * masked, :]).astype(F32).astype(BF16)
        rows = jnp.dot(
            chosen, patch_rows[i * patches : (i + 1) * patches, :], preferred_element_type=F32
        )
        out[count + i * masked : count + (i + 1) * masked, :] = unit(rows)


def prep(crops, patch_rows, mask_col, images, masked):
    patches = patch_rows.shape[0] // images
    count = crops.shape[0] + images * masked
    return pl.pallas_call(
        functools.partial(prep_kernel, images, patches, masked),
        out_shape=jax.ShapeDtypeStruct((count, crops.shape[1]), F32),
        compiler_params=pltpu.CompilerParams(vmem_limit_bytes=VMEM_LIMIT),
    )(crops, patch_rows, mask_col)


def place_rows(core, own, other, dest):
    half = own.shape[0]
    first = pl.multiple_of(core * half, half)
    second = pl.multiple_of((1 - core) * half, half)
    dest[pl.ds(first, half), :] = own[...].astype(dest.dtype)
    dest[pl.ds(second, half), :] = other[...].astype(dest.dtype)


def row_groups(half, crops):
    groups = []
    for base in (0, half):
        groups.append((base, base + crops, 0))
        groups.append((base + crops, base + half, 1))
    return groups


def put_columns(step, heads, out):
    copies = out.shape[0]
    per_head = out.shape[1] // 2
    for head in range(2):
        for t in range(BN // 128):
            piece = heads[head][:, 128 * t : 128 * (t + 1)]
            out[:, pl.ds(head * per_head + step * (BN // 128) + t, 1), :] = jnp.broadcast_to(
                piece[None], (copies, 1, 128)
            )


def teacher_kernel(groups, idx, own, other, protos, expo, sums, feats):
    step = pl.program_id(0)

    @pl.when(step == 0)
    def _():
        place_rows(idx[0], own, other, feats)

    w = unit_cols(protos[...])[0].astype(BF16)
    heads = [jnp.zeros((1, BN), F32), jnp.zeros((1, BN), F32)]
    for start, stop, head in groups:
        score = jnp.dot(feats[start:stop, :], w, preferred_element_type=F32)
        e = jnp.exp2(score * (LOG2E / TEACHER_TEMP)).astype(BF16)
        expo[start:stop, :] = e
        heads[head] = heads[head] + jnp.sum(e.astype(F32), axis=0, keepdims=True)
    put_columns(step, heads, sums)


def teacher_pass(idx, own, other, protos, groups, columns, copies):
    half, width = own.shape
    steps = columns // BN
    return pl.pallas_call(
        functools.partial(teacher_kernel, groups),
        grid_spec=pltpu.PrefetchScalarGridSpec(
            num_scalar_prefetch=1,
            grid=(steps,),
            in_specs=[
                pl.BlockSpec((half, width), lambda j, idx: (0, 0)),
                pl.BlockSpec((half, width), lambda j, idx: (0, 0)),
                pl.BlockSpec((width, BN), lambda j, idx: (0, idx[0] * steps + j)),
            ],
            out_specs=[
                pl.BlockSpec((2 * half, BN), lambda j, idx: (0, j)),
                pl.BlockSpec((copies, 2 * columns // 128, 128), lambda j, idx: (0, 0, 0)),
            ],
            scratch_shapes=[pltpu.VMEM((2 * half, width), BF16)],
        ),
        out_shape=[
            jax.ShapeDtypeStruct((2 * half, columns), BF16),
            jax.ShapeDtypeStruct((copies, 2 * columns // 128, 128), F32),
        ],
        compiler_params=params(),
    )(idx, own, other, protos)


def denominator_kernel(steps, idx, own, other, protos, total, feats, acc):
    step = pl.program_id(0)

    @pl.when(step == 0)
    def _():
        place_rows(idx[0], own, other, feats)
        acc[...] = jnp.zeros_like(acc)

    w = unit_cols(protos[...])[0].astype(BF16)
    rows = feats.shape[0]
    for start in range(0, rows, 256):
        score = jnp.dot(feats[start : start + 256, :], w, preferred_element_type=F32)
        p = jnp.exp2(score * (LOG2E / STUDENT_TEMP))
        part = p[:, :128]
        for t in range(1, BN // 128):
            part = part + p[:, 128 * t : 128 * (t + 1)]
        acc[start : start + 256, :] += part

    @pl.when(step == steps - 1)
    def _():
        for t in range(rows // 128):
            turned = jnp.transpose(acc[128 * t : 128 * (t + 1), :])
            total[t : t + 1, :] = jnp.sum(turned, axis=0, keepdims=True)


def denominator_pass(idx, own, other, protos, columns):
    half, width = own.shape
    steps = columns // BN
    rows = 2 * half
    return pl.pallas_call(
        functools.partial(denominator_kernel, steps),
        grid_spec=pltpu.PrefetchScalarGridSpec(
            num_scalar_prefetch=1,
            grid=(steps,),
            in_specs=[
                pl.BlockSpec((half, width), lambda j, idx: (0, 0)),
                pl.BlockSpec((half, width), lambda j, idx: (0, 0)),
                pl.BlockSpec((width, BN), lambda j, idx: (0, idx[0] * steps + j)),
            ],
            out_specs=pl.BlockSpec((rows // 128, 128), lambda j, idx: (0, 0)),
            scratch_shapes=[pltpu.VMEM((rows, width), BF16), pltpu.VMEM((rows, 128), F32)],
        ),
        out_shape=jax.ShapeDtypeStruct((rows // 128, 128), F32),
        compiler_params=params(),
    )(idx, own, other, protos)


def row_kernel(per_half, crop_blocks, columns, extra, expo, colparts, *refs):
    if extra:
        total, out, colscale = refs
    else:
        out, colscale = refs
    step = pl.program_id(0)
    copies = out.shape[0]
    rows8 = expo.shape[0]
    per_head = columns // 128

    @pl.when(step == 0)
    def _():
        colscale[...] = 1.0 / jnp.sum(colparts[...], axis=0)
        if extra:
            count = total.shape[0]
            out[:, count:, :] = jnp.broadcast_to(total[...][None], (copies, count, 128))

    head = jnp.where(lax.rem(step, per_half) < crop_blocks, 0, 1)

    def chunk(k, acc):
        e = expo[:, pl.ds(pl.multiple_of(k * 128, 128), 128)].astype(F32)
        return acc + e * colscale[pl.ds(head * per_head + k, 1), :]

    acc = lax.fori_loop(0, per_head, chunk, jnp.zeros((rows8, 128), F32), unroll=8)
    sums = jnp.sum(jnp.transpose(acc), axis=0, keepdims=True)
    out[:, pl.ds(step, 1), :] = jnp.broadcast_to(sums[None], (copies, 1, 128))


def row_pass(expo, colparts, total, half, crops, copies):
    rows, columns = expo.shape
    sublanes = rows // 128
    extra = total is not None
    in_specs = [
        pl.BlockSpec((RB, columns), lambda i: (i, 0)),
        pl.BlockSpec(colparts.shape, lambda i: (0, 0, 0)),
    ]
    args = [expo, colparts]
    if extra:
        in_specs.append(pl.BlockSpec(total.shape, lambda i: (0, 0)))
        args.append(total)
    out_shape = (copies, sublanes * (2 if extra else 1), 128)
    return pl.pallas_call(
        functools.partial(row_kernel, half // RB, crops // RB, columns, extra),
        grid=(rows // RB,),
        in_specs=in_specs,
        out_specs=pl.BlockSpec(out_shape, lambda i: (0, 0, 0)),
        out_shape=jax.ShapeDtypeStruct(out_shape, F32),
        scratch_shapes=[pltpu.VMEM((2 * columns // 128, 128), F32)],
        compiler_params=params(),
    )(*args)


def spread_rows(values, dest):
    for t in range(values.shape[0]):
        line = jnp.broadcast_to(values[t : t + 1, :], (128, 128))
        dest[128 * t : 128 * (t + 1), :] = jnp.transpose(line)


def column_kernel(groups, expo, rowparts, out, rowscale):
    step = pl.program_id(0)
    rows = expo.shape[0]

    @pl.when(step == 0)
    def _():
        spread_rows(1.0 / jnp.sum(rowparts[:, : rows // 128, :], axis=0), rowscale)

    def group(start, stop):
        def body(i, acc):
            at = pl.multiple_of(start + i * 16, 16)
            e = expo[pl.ds(at, 16), :].astype(F32)
            r = rowscale[pl.ds(at, 16), :]
            m = e * jnp.concatenate([r] * (BN // 128), axis=1)
            return acc + (m[:8, :] + m[8:, :])

        acc = lax.fori_loop(0, (stop - start) // 16, body, jnp.zeros((8, BN), F32), unroll=8)
        return jnp.sum(acc, axis=0, keepdims=True)

    heads = [jnp.zeros((1, BN), F32), jnp.zeros((1, BN), F32)]
    for start, stop, head in groups:
        heads[head] = heads[head] + group(start, stop)
    put_columns(step, heads, out)


def column_pass(expo, rowparts, groups, copies):
    rows, columns = expo.shape
    out_shape = (copies, 2 * columns // 128, 128)
    return pl.pallas_call(
        functools.partial(column_kernel, groups),
        grid=(columns // BN,),
        in_specs=[
            pl.BlockSpec((rows, BN), lambda j: (0, j)),
            pl.BlockSpec(rowparts.shape, lambda j: (0, 0, 0)),
        ],
        out_specs=pl.BlockSpec(out_shape, lambda j: (0, 0, 0)),
        out_shape=jax.ShapeDtypeStruct(out_shape, F32),
        scratch_shapes=[pltpu.VMEM((rows, 128), F32)],
        compiler_params=params(),
    )(expo, rowparts)


def grad_kernel(groups, steps, nx, ny, idx, own, other, protos, expo, colparts, rowparts, totals, *refs):
    first = refs[:nx]
    second = refs[nx : nx + ny]
    fown, fother, winv_out, feats, feats_t, colscale, rowscale, shift, gbuf, wsum, facc = refs[nx + ny :]
    step = pl.program_id(0)
    rows, width = feats.shape
    half = rows // 2
    sub = rows // 128
    per_head = colscale.shape[0] // 2

    @pl.when(step == 0)
    def _():
        place_rows(idx[0], own, other, feats)
        feats_t[...] = jnp.transpose(feats[...].astype(F32)).astype(BF16)
        colscale[...] = 1.0 / jnp.sum(colparts[...], axis=0)
        spread_rows(GRAD_SCALE / jnp.sum(rowparts[:, :sub, :], axis=0), rowscale)
        denominators = jnp.sum(totals[:, sub : 2 * sub, :], axis=0)
        spread_rows(jnp.log2(GRAD_SCALE / denominators), shift)
        facc[...] = jnp.zeros_like(facc)

    wnorm, winv = unit_cols(protos[...])
    w = wnorm.astype(BF16)
    winv_out[...] = winv
    wide = BN // 128
    scales = []
    for head in range(2):
        base = head * per_head + step * wide
        scales.append(
            jnp.concatenate([colscale[pl.ds(base + t, 1), :] for t in range(wide)], axis=1)
        )
    for start, stop, head in groups:
        score = jnp.dot(feats[start:stop, :], w, preferred_element_type=F32)
        shifts = jnp.concatenate([shift[start:stop, :]] * wide, axis=1)
        prob = jnp.exp2(score * (LOG2E / STUDENT_TEMP) + shifts)
        rs = jnp.concatenate([rowscale[start:stop, :]] * wide, axis=1)
        target = rs * expo[start:stop, :].astype(F32) * scales[head]
        gbuf[start:stop, :] = (prob - target).astype(BF16)
    wsum[...] = jnp.dot(feats_t[...], gbuf[...], preferred_element_type=F32)
    facc[...] += lax.dot_general(
        gbuf[...], w, (((1,), (1,)), ((), ())), preferred_element_type=F32
    )
    coldot = jnp.broadcast_to(jnp.sum(wnorm * wsum[...], axis=0, keepdims=True), (8, BN))

    @pl.when(step < steps // 2)
    def _():
        part = width // nx
        for s in range(nx):
            at = pl.multiple_of(lax.rem(idx[1] + s, nx) * part, part)
            first[s][:part, :] = wsum[pl.ds(at, part), :]
            first[s][part:, :] = coldot

    @pl.when(step >= steps // 2)
    def _():
        part = width // (nx * ny)
        for s in range(ny):
            dest = lax.rem(idx[2] + s, ny)
            for q in range(nx):
                at = pl.multiple_of((q * ny + dest) * part, part)
                second[s][q * part : (q + 1) * part, :] = wsum[pl.ds(at, part), :]
            second[s][nx * part :, :] = coldot

    @pl.when(step == steps - 1)
    def _():
        mine = pl.multiple_of(idx[0] * half, half)
        theirs = pl.multiple_of((1 - idx[0]) * half, half)
        fown[...] = facc[pl.ds(mine, half), :]
        fother[...] = facc[pl.ds(theirs, half), :]


def grad_pass(idx, own, other, protos, expo, colparts, rowparts, totals, groups, nx, ny):
    half, width = own.shape
    rows, columns = expo.shape
    steps = columns // BN
    mid = steps // 2
    whole = lambda shape: pl.BlockSpec(shape, lambda j, idx: (0,) * len(shape))
    front = pl.BlockSpec((width // nx + 8, BN), lambda j, idx: (0, jnp.minimum(j, mid - 1)))
    back = pl.BlockSpec((width // ny + 8, BN), lambda j, idx: (0, jnp.maximum(j - mid, 0)))
    outs = pl.pallas_call(
        functools.partial(grad_kernel, groups, steps, nx, ny),
        grid_spec=pltpu.PrefetchScalarGridSpec(
            num_scalar_prefetch=1,
            grid=(steps,),
            in_specs=[
                whole((half, width)),
                whole((half, width)),
                pl.BlockSpec((width, BN), lambda j, idx: (0, idx[0] * steps + j)),
                pl.BlockSpec((rows, BN), lambda j, idx: (0, j)),
                whole(colparts.shape),
                whole(rowparts.shape),
                whole(totals.shape),
            ],
            out_specs=[front] * nx
            + [back] * ny
            + [
                whole((half, width)),
                whole((half, width)),
                pl.BlockSpec((1, BN), lambda j, idx: (0, j)),
            ],
            scratch_shapes=[
                pltpu.VMEM((rows, width), BF16),
                pltpu.VMEM((width, rows), BF16),
                pltpu.VMEM((2 * columns // 128, 128), F32),
                pltpu.VMEM((rows, 128), F32),
                pltpu.VMEM((rows, 128), F32),
                pltpu.VMEM((rows, BN), BF16),
                pltpu.VMEM((width, BN), F32),
                pltpu.VMEM((rows, width), F32),
            ],
        ),
        out_shape=[jax.ShapeDtypeStruct((width // nx + 8, columns // 2), F32)] * nx
        + [jax.ShapeDtypeStruct((width // ny + 8, columns // 2), F32)] * ny
        + [
            jax.ShapeDtypeStruct((half, width), F32),
            jax.ShapeDtypeStruct((half, width), F32),
            jax.ShapeDtypeStruct((1, columns), F32),
        ],
        compiler_params=params(),
    )(idx, own, other, protos, expo, colparts, rowparts, totals)
    return outs[:nx], outs[nx : nx + ny], outs[-3], outs[-2], outs[-1]


def cut_kernel(slot, n, count, part, idx, *refs):
    arrived = refs[:count]
    outs = refs[count : count + n]
    total = refs[count + n]
    value = arrived[0][...]
    for ref in arrived[1:]:
        value = value + ref[...]
    total[...] = value
    own = total.shape[0] - 8
    for s in range(n):
        at = pl.multiple_of(lax.rem(idx[slot] + s, n) * part, part)
        outs[s][:part, :] = total[pl.ds(at, part), :]
        outs[s][part:, :] = total[own:, :]


def cut_pass(idx, arrived, slot, n):
    rows, columns = arrived[0].shape
    part = (rows - 8) // n
    count = len(arrived)
    return pl.pallas_call(
        functools.partial(cut_kernel, slot, n, count, part),
        grid_spec=pltpu.PrefetchScalarGridSpec(
            num_scalar_prefetch=1,
            grid=(columns // BN,),
            in_specs=[pl.BlockSpec((rows, BN), lambda j, idx: (0, j))] * count,
            out_specs=[pl.BlockSpec((part + 8, BN), lambda j, idx: (0, j))] * n,
            scratch_shapes=[pltpu.VMEM((rows, BN), F32)],
        ),
        out_shape=[jax.ShapeDtypeStruct((part + 8, columns), F32)] * n,
        compiler_params=params(),
    )(idx, *arrived)


def proto_kernel(count_a, count_b, part, idx, *refs):
    a_refs = refs[:count_a]
    b_refs = refs[count_a : count_a + count_b]
    protos, winv, mine, theirs = refs[count_a + count_b :]
    columns = a_refs[0].shape[1]
    own = part // 2
    core = idx[0]
    for side, group in enumerate((a_refs, b_refs)):
        value = group[0][...]
        for ref in group[1:]:
            value = value + ref[...]
        span = slice(side * columns, (side + 1) * columns)
        inv = winv[:, span]
        wnorm = protos[:, span].astype(F32) * inv
        grad = (value[:part, :] - wnorm * value[part : part + 1, :]) * inv
        low = grad[:own, :]
        high = grad[own:, :]
        mine[:, span] = jnp.where(core == 0, low, high)
        theirs[:, span] = jnp.where(core == 0, high, low)


def proto_pass(idx, a_parts, b_parts, protos, winv):
    rows, columns = a_parts[0].shape
    part = rows - 8
    total = 2 * columns
    own = part // 2
    whole = lambda shape: pl.BlockSpec(shape, lambda i, idx: (0, 0))
    return pl.pallas_call(
        functools.partial(proto_kernel, len(a_parts), len(b_parts), part),
        grid_spec=pltpu.PrefetchScalarGridSpec(
            num_scalar_prefetch=1,
            grid=(1,),
            in_specs=[whole((rows, columns))] * (len(a_parts) + len(b_parts))
            + [pl.BlockSpec((part, total), lambda i, idx: (idx[4], idx[0])), whole((1, total))],
            out_specs=[whole((own, total))] * 2,
        ),
        out_shape=[jax.ShapeDtypeStruct((own, total), F32)] * 2,
        compiler_params=params(),
    )(idx, *a_parts, *b_parts, protos, winv)


def pack_kernel(nz, crops, masked, per_z, share, patches, mine, came, out):
    total = mine[...] + came[...]
    crop_share = crops // nz
    for z in range(nz):
        out[z, :crop_share, :] = total[z * crop_share : (z + 1) * crop_share, :]
        image = z * share // patches
        start = crops + image * masked
        out[z, crop_share:, :] = total[start : start + per_z * masked, :]


def pack_pass(mine, came, nz, crops, masked, per_z, share, patches):
    width = mine.shape[1]
    out_shape = (nz, crops // nz + per_z * masked, width)
    return pl.pallas_call(
        functools.partial(pack_kernel, nz, crops, masked, per_z, share, patches),
        out_shape=jax.ShapeDtypeStruct(out_shape, F32),
        compiler_params=pltpu.CompilerParams(vmem_limit_bytes=VMEM_LIMIT),
    )(mine, came)


def feature_kernel(nz, crop_share, masked, per_z, share, patches, idx, mask, parts, crops, rows, crop_out, patch_out, total, dense):
    value = parts[0]
    for z in range(1, nz):
        value = value + parts[z]
    total[...] = value
    dense[...] = jnp.zeros_like(dense)
    first_row = idx[3] * share
    first_image = first_row // patches
    offset = first_row - first_image * patches

    def place(m, _):
        image = m // masked
        at = mask[(first_image + image) * masked + m - image * masked] + image * patches - offset

        @pl.when(jnp.logical_and(at >= 0, at < share))
        def _():
            dense[pl.ds(at, 1), :] = total[pl.ds(crop_share + m, 1), :]

        return 0

    lax.fori_loop(0, per_z * masked, place, 0, unroll=4)

    def back(x, fgrad):
        xf = x.astype(F32)
        inv = lax.rsqrt(jnp.sum(xf * xf, axis=-1, keepdims=True) + EPS)
        u = xf * inv
        return (fgrad - u * jnp.sum(u * fgrad, axis=-1, keepdims=True)) * inv

    crop_out[...] = back(crops[...], total[:crop_share, :])
    patch_out[...] = back(rows[...], dense[...])


def feature_pass(idx, mask, parts, crops, patch_rows, nz, masked, per_z, patches):
    width = crops.shape[1]
    crop_share = crops.shape[0] // nz
    share = patch_rows.shape[0] // nz
    return pl.pallas_call(
        functools.partial(feature_kernel, nz, crop_share, masked, per_z, share, patches),
        grid_spec=pltpu.PrefetchScalarGridSpec(
            num_scalar_prefetch=2,
            grid=(1,),
            in_specs=[
                pl.BlockSpec(parts.shape, lambda i, idx, mask: (0, 0, 0)),
                pl.BlockSpec((crop_share, width), lambda i, idx, mask: (idx[3], 0)),
                pl.BlockSpec((share, width), lambda i, idx, mask: (idx[3], 0)),
            ],
            out_specs=[
                pl.BlockSpec((crop_share, width), lambda i, idx, mask: (0, 0)),
                pl.BlockSpec((share, width), lambda i, idx, mask: (0, 0)),
            ],
            scratch_shapes=[pltpu.VMEM(parts.shape[1:], F32), pltpu.VMEM((share, width), F32)],
        ),
        out_shape=[
            jax.ShapeDtypeStruct((crop_share, width), F32),
            jax.ShapeDtypeStruct((share, width), F32),
        ],
        compiler_params=params(),
    )(idx, mask, parts, crops, patch_rows)


def shifted(n, s):
    return [(i, (i + s) % n) for i in range(n)]


def local(
    sizes,
    student_crops,
    teacher_crops,
    student_patches,
    teacher_patches,
    patch_mask,
    student_protos,
    teacher_protos,
):
    nx, ny, nz = sizes
    images, masked = patch_mask.shape
    patches = student_patches.shape[0] // images
    width = student_crops.shape[1]
    crops = student_crops.shape[0]
    half = crops + images * masked
    columns = student_protos.shape[1] // 2
    groups = row_groups(half, crops)
    ix, iy, ic, iz = (lax.axis_index(a) for a in ("x", "y", "c", "z"))
    idx = jnp.stack([ic, ix, iy, iz, ix * ny + iy]).astype(jnp.int32)
    mask_col = patch_mask.reshape(-1, 1)
    swap = [(0, 1), (1, 0)]

    teacher = prep(teacher_crops, teacher_patches, mask_col, images, masked)
    teacher_other = lax.ppermute(teacher, "c", swap)
    student = prep(student_crops, student_patches, mask_col, images, masked)
    student_other = lax.ppermute(student, "c", swap)

    expo, sums = teacher_pass(
        idx, teacher, teacher_other, teacher_protos, groups, columns, nx * ny
    )
    total = None
    totals = None
    for step in range(ITERS):
        colparts = lax.all_to_all(sums, ("x", "y"), 0, 0)
        if step == 0:
            total = denominator_pass(idx, student, student_other, student_protos, columns)
        sums = row_pass(expo, colparts, total if step == 0 else None, half, crops, 2 * nz)
        rowparts = lax.all_to_all(sums, ("c", "z"), 0, 0)
        if step == 0:
            totals = rowparts
        if step < ITERS - 1:
            sums = column_pass(expo, rowparts, groups, nx * ny)

    a_out, b_out, f_mine, f_theirs, winv = grad_pass(
        idx,
        student,
        student_other,
        student_protos,
        expo,
        colparts,
        rowparts,
        totals,
        groups,
        nx,
        ny,
    )
    a_in = [a_out[0]] + [lax.ppermute(a_out[s], "x", shifted(nx, s)) for s in range(1, nx)]
    b_in = [b_out[0]] + [lax.ppermute(b_out[s], "y", shifted(ny, s)) for s in range(1, ny)]
    f_came = lax.ppermute(f_theirs, "c", swap)
    share = student_patches.shape[0] // nz
    per_z = max(1, share // patches)
    packed = pack_pass(f_mine, f_came, nz, crops, masked, per_z, share, patches)
    fparts = lax.all_to_all(packed, "z", 0, 0)
    crop_grad, patch_grad = feature_pass(
        idx,
        patch_mask.reshape(-1),
        fparts,
        student_crops,
        student_patches,
        nz,
        masked,
        per_z,
        patches,
    )
    a_cut = cut_pass(idx, a_in, 2, ny)
    a_in = [a_cut[0]] + [lax.ppermute(a_cut[s], "y", shifted(ny, s)) for s in range(1, ny)]
    b_cut = cut_pass(idx, b_in, 1, nx)
    b_in = [b_cut[0]] + [lax.ppermute(b_cut[s], "x", shifted(nx, s)) for s in range(1, nx)]
    mine, theirs = proto_pass(idx, a_in, b_in, student_protos, winv)
    came = lax.ppermute(theirs, "c", swap)
    proto_grad = jnp.where(
        ic == 0,
        jnp.concatenate([mine, came], axis=1),
        jnp.concatenate([came, mine], axis=1),
    )
    return (proto_grad, crop_grad, patch_grad)


def solution(mesh):
    dp, nz = mesh.devices.shape
    nx = 4 if dp == 32 else 2
    ny = dp // (2 * nx)
    grid = Mesh(mesh.devices.reshape(nx, ny, 2, nz), ("x", "y", "c", "z"))
    rows = ("x", "y", "c")
    in_specs = (
        P(rows, None),
        P(rows, None),
        P(rows, None),
        P(rows, None),
        P(rows, None),
        P(None, "z"),
        P(None, "z"),
    )
    out_specs = (P(rows, "z"), P(rows + ("z",), None), P(rows + ("z",), None))
    return jax.shard_map(
        functools.partial(local, (nx, ny, nz)),
        mesh=grid,
        in_specs=in_specs,
        out_specs=out_specs,
        check_vma=False,
    )
```

```python
import functools

import jax
import jax.numpy as jnp
from jax import lax
from jax.experimental import pallas as pl
from jax.experimental.pallas import tpu as pltpu
from jax.sharding import Mesh, PartitionSpec as P

ITERS = 3
EPS = 1e-06
TEACHER_TEMP = 0.07
STUDENT_TEMP = 0.1
LOSS_SCALE = 256.0
GRAD_SCALE = LOSS_SCALE / STUDENT_TEMP
LOG2E = 1.4426950408889634

BN = 512
F32 = jnp.float32
BF16 = jnp.bfloat16
VMEM_LIMIT = 26 * 1024 * 1024
SMEM = pl.BlockSpec(memory_space=pltpu.SMEM)
VMEM = pl.BlockSpec(memory_space=pltpu.VMEM)


def call(kernel, out_shape, args, scalars=0, scratch=(), flops=0, traffic=0):
    return pl.pallas_call(
        kernel,
        out_shape=out_shape,
        in_specs=[SMEM] * scalars + [VMEM] * (len(args) - scalars),
        scratch_shapes=list(scratch),
        compiler_params=pltpu.CompilerParams(vmem_limit_bytes=VMEM_LIMIT),
        cost_estimate=pl.CostEstimate(flops=flops, bytes_accessed=traffic, transcendentals=0),
    )(*args)


def array(shape, dtype=F32):
    return jax.ShapeDtypeStruct(shape, dtype)


def unit(x):
    xf = x.astype(F32)
    return xf * lax.rsqrt(jnp.sum(xf * xf, axis=-1, keepdims=True) + EPS)


def unit_cols(w):
    wf = w.astype(F32)
    inv = lax.rsqrt(jnp.sum(wf * wf, axis=0, keepdims=True) + EPS)
    return wf * inv, inv


def prep_kernel(crops, patch_rows, mask, out):
    images, masked = mask.shape
    patches = patch_rows.shape[0] // images
    count = crops.shape[0]
    out[:count, :] = unit(crops[...])
    for i in range(images):
        place = lax.broadcasted_iota(jnp.int32, (patches, masked), 0)
        chosen = (place == mask[i : i + 1, :]).astype(F32).astype(BF16)
        rows = lax.dot_general(
            chosen,
            patch_rows[i * patches : (i + 1) * patches, :],
            (((0,), (0,)), ((), ())),
            preferred_element_type=F32,
        )
        out[count + i * masked : count + (i + 1) * masked, :] = unit(rows)


def prep(crops, patch_rows, mask):
    count = crops.shape[0] + mask.size
    return call(prep_kernel, array((count, crops.shape[1])), [crops, patch_rows, mask])


def place_rows(core, crops, own, other, dest):
    half = own.shape[0]
    rest = half - crops
    for side, ref in ((core, own), (1 - core, other)):
        at = pl.multiple_of(side * crops, crops)
        dest[pl.ds(at, crops), :] = ref[:crops, :].astype(dest.dtype)
        at = pl.multiple_of(2 * crops + side * rest, 128)
        dest[pl.ds(at, rest), :] = ref[crops:, :].astype(dest.dtype)


def row_blocks(start, stop):
    return [(a, min(a + 256, stop)) for a in range(start, stop, 256)]


def proto_block(core, step, protos):
    columns = protos.shape[1] // 2
    at = pl.multiple_of(core * columns + step * BN, BN)
    return unit_cols(protos[:, pl.ds(at, BN)])


def put_columns(step, heads, out):
    copies = out.shape[0]
    per_head = out.shape[1] // 2
    for head in range(2):
        for t in range(BN // 128):
            piece = heads[head][:, 128 * t : 128 * (t + 1)]
            out[:, pl.ds(head * per_head + step * (BN // 128) + t, 1), :] = jnp.broadcast_to(
                piece[None], (copies, 1, 128)
            )


def get_columns(step, head, lines):
    base = head * (lines.shape[0] // 2) + step * (BN // 128)
    return jnp.concatenate([lines[pl.ds(base + t, 1), :] for t in range(BN // 128)], axis=1)


def line_up(values):
    return jnp.concatenate([values[t : t + 1, :] for t in range(values.shape[0])], axis=1)


def teacher_kernel(crops, idx, own, other, protos, expo, sums, feats):
    place_rows(idx[0], crops, own, other, feats)
    rows, columns = expo.shape

    def step(j, _):
        w = proto_block(idx[0], j, protos)[0].astype(BF16)
        at = pl.multiple_of(j * BN, BN)
        heads = []
        for first, last in ((0, 2 * crops), (2 * crops, rows)):
            part = jnp.zeros((1, BN), F32)
            for start, stop in row_blocks(first, last):
                score = jnp.dot(feats[start:stop, :], w, preferred_element_type=F32)
                e = jnp.exp2(score * (LOG2E / TEACHER_TEMP)).astype(BF16)
                expo[start:stop, pl.ds(at, BN)] = e
                part = part + jnp.sum(e.astype(F32), axis=0, keepdims=True)
            heads.append(part)
        put_columns(j, heads, sums)
        return 0

    lax.fori_loop(0, columns // BN, step, 0)


def teacher_pass(idx, own, other, protos, crops, copies):
    half, width = own.shape
    columns = protos.shape[1] // 2
    return call(
        functools.partial(teacher_kernel, crops),
        [array((2 * half, columns), BF16), array((copies, 2 * columns // 128, 128))],
        [idx, own, other, protos],
        scalars=1,
        scratch=[pltpu.VMEM((2 * half, width), BF16)],
        flops=4 * half * width * columns,
        traffic=4 * half * columns,
    )


def student_kernel(crops, idx, own, other, protos, expo, total, mix, turned, feats, acc):
    place_rows(idx[0], crops, own, other, feats)
    turned[...] = jnp.transpose(feats[...].astype(F32)).astype(BF16)
    acc[...] = jnp.zeros_like(acc)
    mix[...] = jnp.zeros_like(mix)
    rows, columns = expo.shape

    def step(j, _):
        w = proto_block(idx[0], j, protos)[0].astype(BF16)
        at = pl.multiple_of(j * BN, BN)
        for start, stop in row_blocks(0, rows):
            score = jnp.dot(feats[start:stop, :], w, preferred_element_type=F32)
            p = jnp.exp2(score * (LOG2E / STUDENT_TEMP))
            part = p[:, :128]
            for t in range(1, BN // 128):
                part = part + p[:, 128 * t : 128 * (t + 1)]
            acc[start:stop, :] += part
            p = p.astype(BF16)
            expo[start:stop, pl.ds(at, BN)] = p
            mix[start:stop, :] += lax.dot_general(
                p, w, (((1,), (1,)), ((), ())), preferred_element_type=F32
            )
        return 0

    lax.fori_loop(0, columns // BN, step, 0)
    for t in range(rows // 128):
        block = jnp.transpose(acc[128 * t : 128 * (t + 1), :])
        total[t : t + 1, :] = jnp.sum(block, axis=0, keepdims=True)


def student_pass(idx, own, other, protos, crops):
    half, width = own.shape
    columns = protos.shape[1] // 2
    rows = 2 * half
    return call(
        functools.partial(student_kernel, crops),
        [
            array((rows, columns), BF16),
            array((rows // 128, 128)),
            array((rows, width)),
            array((width, rows), BF16),
        ],
        [idx, own, other, protos],
        scalars=1,
        scratch=[pltpu.VMEM((rows, width), BF16), pltpu.VMEM((rows, 128), F32)],
        flops=4 * rows * width * columns,
        traffic=2 * rows * columns,
    )


def row_kernel(crops, extra, expo, colparts, *refs):
    if extra:
        total, out, colscale = refs
    else:
        out, colscale = refs
    copies = out.shape[0]
    rows, columns = expo.shape
    per_head = columns // 128
    colscale[...] = 1.0 / jnp.sum(colparts[...], axis=0)
    if extra:
        count = total.shape[0]
        out[:, count:, :] = jnp.broadcast_to(total[...][None], (copies, count, 128))

    def block(i, _):
        head = jnp.where(i < 2 * crops // 128, 0, 1)
        at = pl.multiple_of(i * 128, 128)

        def chunk(k, acc):
            e = expo[pl.ds(at, 128), pl.ds(pl.multiple_of(k * 128, 128), 128)].astype(F32)
            return acc + e * colscale[pl.ds(head * per_head + k, 1), :]

        acc = lax.fori_loop(0, per_head, chunk, jnp.zeros((128, 128), F32), unroll=8)
        sums = jnp.sum(jnp.transpose(acc), axis=0, keepdims=True)
        out[:, pl.ds(i, 1), :] = jnp.broadcast_to(sums[None], (copies, 1, 128))
        return 0

    lax.fori_loop(0, rows // 128, block, 0)


def row_pass(expo, colparts, total, crops, copies):
    rows, columns = expo.shape
    extra = total is not None
    return call(
        functools.partial(row_kernel, crops, extra),
        array((copies, rows // 128 * (2 if extra else 1), 128)),
        [expo, colparts] + ([total] if extra else []),
        scratch=[pltpu.VMEM((2 * columns // 128, 128), F32)],
        flops=2 * rows * columns,
        traffic=2 * rows * columns,
    )


def split3(v):
    high = v.astype(BF16)
    rest = v - high.astype(F32)
    middle = rest.astype(BF16)
    low = (rest - middle.astype(F32)).astype(BF16)
    pad = jnp.zeros((13, v.shape[1]), F32)
    parts = [high.astype(F32), middle.astype(F32), low.astype(F32), pad]
    return jnp.concatenate(parts, axis=0).astype(BF16)


def column_kernel(crops, expo, rowparts, out):
    rows, columns = expo.shape
    scale = line_up(1.0 / jnp.sum(rowparts[:, : rows // 128, :], axis=0))
    spans = [(0, 2 * crops), (2 * crops, rows)]
    lefts = [split3(scale[:, first:last]) for first, last in spans]
    for j in range(columns // BN):
        heads = []
        for left, (first, last) in zip(lefts, spans):
            sums = jnp.dot(
                left, expo[first:last, j * BN : (j + 1) * BN], preferred_element_type=F32
            )
            heads.append(sums[0:1, :] + sums[1:2, :] + sums[2:3, :])
        put_columns(j, heads, out)


def column_pass(expo, rowparts, crops, copies):
    rows, columns = expo.shape
    return call(
        functools.partial(column_kernel, crops),
        array((copies, 2 * columns // 128, 128)),
        [expo, rowparts],
        flops=2 * rows * columns,
        traffic=2 * rows * columns,
    )


def prob_kernel(turned, student_expo, totals, out):
    rows, columns = student_expo.shape
    sub = rows // 128
    scale = line_up(GRAD_SCALE / jnp.sum(totals[:, sub : 2 * sub, :], axis=0))
    left = (turned[...].astype(F32) * scale).astype(BF16)
    for j in range(columns // BN):
        span = slice(j * BN, (j + 1) * BN)
        out[:, span] = jnp.dot(left, student_expo[:, span], preferred_element_type=F32)


def prob_pass(turned, student_expo, totals):
    width = turned.shape[0]
    rows, columns = student_expo.shape
    return call(
        prob_kernel,
        array((width, columns)),
        [turned, student_expo, totals],
        flops=2 * rows * columns * width,
        traffic=2 * rows * columns,
    )


def weight_kernel(crops, idx, turned, expo, prob, protos, colparts, rowparts, out, winv_out, scales, left):
    rows, columns = expo.shape
    copies = out.shape[0]
    width = turned.shape[0]
    part = width // copies
    scales[...] = GRAD_SCALE / jnp.sum(colparts[...], axis=0)
    scale = line_up(1.0 / jnp.sum(rowparts[:, : rows // 128, :], axis=0))
    left[...] = (turned[...].astype(F32) * scale).astype(BF16)
    spans = [(0, 2 * crops), (2 * crops, rows)]
    tail = columns // 128 * part

    def step(j, _):
        at = pl.multiple_of(j * BN, BN)
        wsum = prob[:, pl.ds(at, BN)]
        for head, (first, last) in enumerate(spans):
            target = jnp.dot(
                left[:, first:last], expo[first:last, pl.ds(at, BN)], preferred_element_type=F32
            )
            wsum = wsum - target * get_columns(j, head, scales)
        wnorm, winv = proto_block(idx[0], j, protos)
        winv_out[:, pl.ds(at, BN)] = winv
        coldot = jnp.sum(wnorm * wsum, axis=0, keepdims=True)
        for t in range(BN // 128):
            lanes = slice(128 * t, 128 * (t + 1))
            row = pl.multiple_of((j * (BN // 128) + t) * part, part)
            for d in range(copies):
                out[d, pl.ds(row, part), :] = wsum[d * part : (d + 1) * part, lanes]
            out[:, pl.ds(tail + j * (BN // 128) + t, 1), :] = jnp.broadcast_to(
                coldot[:, lanes][None], (copies, 1, 128)
            )
        return 0

    lax.fori_loop(0, columns // BN, step, 0)


def weight_pass(idx, turned, expo, prob, protos, colparts, rowparts, crops, copies):
    width, rows = turned.shape
    columns = expo.shape[1]
    lines = columns // 128 * (width // copies + 1)
    return call(
        functools.partial(weight_kernel, crops),
        [array((copies, lines, 128)), array((1, columns))],
        [idx, turned, expo, prob, protos, colparts, rowparts],
        scalars=1,
        scratch=[
            pltpu.VMEM((2 * columns // 128, 128), F32),
            pltpu.VMEM((width, rows), BF16),
        ],
        flops=2 * rows * columns * width,
        traffic=2 * rows * columns,
    )


def proto_kernel(idx, parts, protos, winv, mine, theirs):
    columns = winv.shape[1]
    copies = parts.shape[0]
    part = protos.shape[0] // copies
    own = part // 2
    core = idx[0]
    tail = columns // 128 * part
    row = pl.multiple_of(idx[2] * part, part)
    for t in range(columns // 128):
        lanes = slice(128 * t, 128 * (t + 1))
        wsum = jnp.sum(parts[:, t * part : (t + 1) * part, :], axis=0)
        coldot = jnp.sum(parts[:, tail + t : tail + t + 1, :], axis=0)
        inv = winv[:, lanes]
        at = pl.multiple_of(core * columns + 128 * t, 128)
        wnorm = protos[pl.ds(row, part), pl.ds(at, 128)].astype(F32) * inv
        grad = (wsum - wnorm * coldot) * inv
        low = grad[:own, :]
        high = grad[own:, :]
        mine[:, lanes] = jnp.where(core == 0, low, high)
        theirs[:, lanes] = jnp.where(core == 0, high, low)


def proto_pass(idx, parts, protos, winv):
    own = protos.shape[0] // parts.shape[0] // 2
    columns = winv.shape[1]
    return call(
        proto_kernel,
        [array((own, columns)), array((own, columns))],
        [idx, parts, protos, winv],
        scalars=1,
    )


def target_kernel(crops, idx, expo, protos, colparts, out, scales):
    rows, columns = expo.shape
    scales[...] = 1.0 / jnp.sum(colparts[...], axis=0)
    out[...] = jnp.zeros_like(out)

    def step(j, _):
        wnorm = proto_block(idx[0], j, protos)[0]
        at = pl.multiple_of(j * BN, BN)
        for head, (first, last) in enumerate(((0, 2 * crops), (2 * crops, rows))):
            w = (wnorm * get_columns(j, head, scales)).astype(BF16)
            out[first:last, :] += lax.dot_general(
                expo[first:last, pl.ds(at, BN)],
                w,
                (((1,), (1,)), ((), ())),
                preferred_element_type=F32,
            )
        return 0

    lax.fori_loop(0, columns // BN, step, 0)


def target_pass(idx, expo, protos, colparts, crops):
    rows, columns = expo.shape
    width = protos.shape[0]
    return call(
        functools.partial(target_kernel, crops),
        array((rows, width)),
        [idx, expo, protos, colparts],
        scalars=1,
        scratch=[pltpu.VMEM((2 * columns // 128, 128), F32)],
        flops=2 * rows * columns * width,
        traffic=2 * rows * columns,
    )


def spread_row(line):
    return jnp.transpose(jnp.broadcast_to(line, (128, 128)))


def combine_kernel(crops, idx, mix, target, totals, rowparts, mine, theirs, buf):
    rows, width = mix.shape
    sub = rows // 128
    prob = GRAD_SCALE / jnp.sum(totals[:, sub : 2 * sub, :], axis=0)
    row = GRAD_SCALE / jnp.sum(rowparts[:, :sub, :], axis=0)
    for t in range(sub):
        span = slice(128 * t, 128 * (t + 1))
        p = jnp.concatenate([spread_row(prob[t : t + 1, :])] * (width // 128), axis=1)
        r = jnp.concatenate([spread_row(row[t : t + 1, :])] * (width // 128), axis=1)
        buf[span, :] = mix[span, :] * p - target[span, :] * r
    rest = rows // 2 - crops
    for side, ref in ((idx[0], mine), (1 - idx[0], theirs)):
        ref[:crops, :] = buf[pl.ds(pl.multiple_of(side * crops, crops), crops), :]
        ref[crops:, :] = buf[pl.ds(pl.multiple_of(2 * crops + side * rest, 128), rest), :]


def combine_pass(idx, mix, target, totals, rowparts, crops):
    rows, width = mix.shape
    return call(
        functools.partial(combine_kernel, crops),
        [array((rows // 2, width)), array((rows // 2, width))],
        [idx, mix, target, totals, rowparts],
        scalars=1,
        scratch=[pltpu.VMEM((rows, width), F32)],
    )


def pack_kernel(nz, crops, mine, came, out):
    half = mine.shape[0]
    chunk = half // nz
    share = crops // nz
    rest = chunk - share
    for z in range(nz):
        for src, dst, size in ((z * share, z * chunk, share), (crops + z * rest, z * chunk + share, rest)):
            out[dst : dst + size, :] = mine[src : src + size, :] + came[src : src + size, :]


def pack_pass(mine, came, nz, crops):
    return call(functools.partial(pack_kernel, nz, crops), array(mine.shape), [mine, came])


def feature_kernel(pair, patches, idx, mask, *refs):
    if pair:
        own, other, crops, rows, crop_out, patch_out, masked_rows, dense = refs
    else:
        own, crops, rows, crop_out, patch_out, masked_rows, dense = refs
    z = idx[1]
    masked = mask.shape[1]
    crop_share = crop_out.shape[0]
    share = patch_out.shape[0]
    rest = own.shape[0] - crop_share
    if pair:
        odd = lax.rem(z, 2)
        masked_rows[pl.ds(pl.multiple_of(odd * rest, 8), rest), :] = own[crop_share:, :]
        masked_rows[pl.ds(pl.multiple_of((1 - odd) * rest, 8), rest), :] = other[crop_share:, :]
    else:
        masked_rows[...] = own[crop_share:, :]
    dense[...] = jnp.zeros_like(dense)
    first_row = z * share
    first_image = first_row // patches
    offset = first_row - first_image * patches
    for image in range(masked_rows.shape[0] // masked):

        def place(m, _):
            at = mask[first_image + image, m] + image * patches - offset

            @pl.when(jnp.logical_and(at >= 0, at < share))
            def _():
                dense[pl.ds(at, 1), :] = masked_rows[pl.ds(image * masked + m, 1), :]

            return 0

        lax.fori_loop(0, masked, place, 0, unroll=4)

    def back(x, fgrad):
        xf = x.astype(F32)
        inv = lax.rsqrt(jnp.sum(xf * xf, axis=-1, keepdims=True) + EPS)
        u = xf * inv
        return (fgrad - u * jnp.sum(u * fgrad, axis=-1, keepdims=True)) * inv

    crop_at = pl.multiple_of(z * crop_share, 16)
    patch_at = pl.multiple_of(z * share, 128)
    crop_out[...] = back(crops[pl.ds(crop_at, crop_share), :], own[:crop_share, :])
    patch_out[...] = back(rows[pl.ds(patch_at, share), :], dense[...])


def feature_pass(idx, mask, pieces, crops, patch_rows, nz, patches):
    width = crops.shape[1]
    crop_share = crops.shape[0] // nz
    share = patch_rows.shape[0] // nz
    count = len(pieces) * (pieces[0].shape[0] - crop_share)
    return call(
        functools.partial(feature_kernel, len(pieces) == 2, patches),
        [array((crop_share, width)), array((share, width))],
        [idx, mask, *pieces, crops, patch_rows],
        scalars=2,
        scratch=[pltpu.VMEM((count, width), F32), pltpu.VMEM((share, width), F32)],
    )


def local(
    sizes,
    student_crops,
    teacher_crops,
    student_patches,
    teacher_patches,
    patch_mask,
    student_protos,
    teacher_protos,
):
    nx, ny, nz = sizes
    images, masked = patch_mask.shape
    patches = student_patches.shape[0] // images
    crops = student_crops.shape[0]
    ix, iy, ic, iz = (lax.axis_index(a) for a in ("x", "y", "c", "z"))
    idx = jnp.stack([ic, iz, ix * ny + iy]).astype(jnp.int32)
    swap = [(0, 1), (1, 0)]

    teacher = prep(teacher_crops, teacher_patches, patch_mask)
    teacher_other = lax.ppermute(teacher, "c", swap)
    student = prep(student_crops, student_patches, patch_mask)
    student_other = lax.ppermute(student, "c", swap)

    expo, sums = teacher_pass(idx, teacher, teacher_other, teacher_protos, crops, nx * ny)
    for step in range(ITERS):
        colparts = lax.all_to_all(sums, ("x", "y"), 0, 0)
        if step == 0:
            student_expo, total, mix, turned = student_pass(
                idx, student, student_other, student_protos, crops
            )
        sums = row_pass(expo, colparts, total if step == 0 else None, crops, 2 * nz)
        rowparts = lax.all_to_all(sums, ("c", "z"), 0, 0)
        if step == 0:
            totals = rowparts
        if step < ITERS - 1:
            sums = column_pass(expo, rowparts, crops, nx * ny)

    prob = prob_pass(turned, student_expo, totals)
    target = target_pass(idx, expo, student_protos, colparts, crops)
    outgoing, winv = weight_pass(
        idx, turned, expo, prob, student_protos, colparts, rowparts, crops, nx * ny
    )
    parts = lax.all_to_all(outgoing, ("x", "y"), 0, 0)
    f_mine, f_theirs = combine_pass(idx, mix, target, totals, rowparts, crops)
    f_came = lax.ppermute(f_theirs, "c", swap)
    packed = pack_pass(f_mine, f_came, nz, crops)
    own = lax.psum_scatter(packed, "z", scatter_dimension=0, tiled=True)
    pieces = [own]
    if student_patches.shape[0] // nz < patches:
        pieces.append(lax.ppermute(own, "z", [(i, i ^ 1) for i in range(nz)]))
    crop_grad, patch_grad = feature_pass(
        idx, patch_mask, pieces, student_crops, student_patches, nz, patches
    )
    mine, theirs = proto_pass(idx, parts, student_protos, winv)
    came = lax.ppermute(theirs, "c", swap)
    proto_grad = jnp.where(
        ic == 0,
        jnp.concatenate([mine, came], axis=1),
        jnp.concatenate([came, mine], axis=1),
    )
    return (proto_grad, crop_grad, patch_grad)


def solution(mesh):
    dp, nz = mesh.devices.shape
    nx = 4 if dp == 32 else 2
    ny = dp // (2 * nx)
    grid = Mesh(mesh.devices.reshape(nx, ny, 2, nz), ("x", "y", "c", "z"))
    rows = ("x", "y", "c")
    in_specs = (
        P(rows, None),
        P(rows, None),
        P(rows, None),
        P(rows, None),
        P(rows, None),
        P(None, "z"),
        P(None, "z"),
    )
    out_specs = (P(rows, "z"), P(rows + ("z",), None), P(rows + ("z",), None))
    return jax.shard_map(
        functools.partial(local, (nx, ny, nz)),
        mesh=grid,
        in_specs=in_specs,
        out_specs=out_specs,
        check_vma=False,
    )
```

```python
import functools

import jax
import jax.numpy as jnp
from jax import lax
from jax.experimental import pallas as pl
from jax.experimental.pallas import tpu as pltpu
from jax.sharding import Mesh, PartitionSpec as P

ITERS = 3
EPS = 1e-06
TEACHER_TEMP = 0.07
STUDENT_TEMP = 0.1
LOSS_SCALE = 256.0
GRAD_SCALE = LOSS_SCALE / STUDENT_TEMP
LOG2E = 1.4426950408889634

BN = 512
F32 = jnp.float32
BF16 = jnp.bfloat16
VMEM_LIMIT = 16 * 1024 * 1024
SMEM = pl.BlockSpec(memory_space=pltpu.SMEM)
VMEM = pl.BlockSpec(memory_space=pltpu.VMEM)
HBM = pl.BlockSpec(memory_space=pltpu.HBM)


def call(kernel, out_shape, args, specs="", scratch=(), flops=0, traffic=0):
    spaces = {"s": SMEM, "v": VMEM, "h": HBM}
    return pl.pallas_call(
        kernel,
        out_shape=out_shape,
        in_specs=[spaces[letter] for letter in specs],
        scratch_shapes=list(scratch),
        compiler_params=pltpu.CompilerParams(vmem_limit_bytes=VMEM_LIMIT),
        cost_estimate=pl.CostEstimate(flops=flops, bytes_accessed=traffic, transcendentals=0),
    )(*args)


def array(shape, dtype=F32):
    return jax.ShapeDtypeStruct(shape, dtype)


def stream(source, buf, sem, steps, body):
    def copy(j, slot):
        return pltpu.make_async_copy(source(j), buf.at[slot], sem.at[slot])

    copy(0, 0).start()

    def step(j, _):
        slot = lax.rem(j, 2)

        @pl.when(j + 1 < steps)
        def _():
            copy(j + 1, 1 - slot).start()

        copy(j, slot).wait()
        body(j, buf.at[slot])
        return 0

    lax.fori_loop(0, steps, step, 0)


def unit(x):
    xf = x.astype(F32)
    return xf * lax.rsqrt(jnp.sum(xf * xf, axis=-1, keepdims=True) + EPS)


def unit_cols(w):
    wf = w.astype(F32)
    inv = lax.rsqrt(jnp.sum(wf * wf, axis=0, keepdims=True) + EPS)
    return wf * inv, inv


def prep_kernel(tcrops, tpatch, scrops, spatch, mask, out, tc, tp, sc, sp, sem):
    images, masked = mask.shape
    patches = tp.shape[0] // images
    count = tc.shape[0]
    half = out.shape[0] // 2
    copies = [
        pltpu.make_async_copy(src, dst, sem.at[i])
        for i, (src, dst) in enumerate(((tcrops, tc), (tpatch, tp), (scrops, sc), (spatch, sp)))
    ]
    for copy in copies:
        copy.start()
    for side, (crops, patch_rows) in enumerate(((tc, tp), (sc, sp))):
        copies[2 * side].wait()
        copies[2 * side + 1].wait()
        base = side * half
        out[base : base + count, :] = unit(crops[...])
        for i in range(images):
            place = lax.broadcasted_iota(jnp.int32, (patches, masked), 0)
            chosen = (place == mask[i : i + 1, :]).astype(F32).astype(BF16)
            rows = lax.dot_general(
                chosen,
                patch_rows[i * patches : (i + 1) * patches, :],
                (((0,), (0,)), ((), ())),
                preferred_element_type=F32,
            )
            at = base + count + i * masked
            out[at : at + masked, :] = unit(rows)


def prep(tcrops, tpatch, scrops, spatch, mask):
    half = tcrops.shape[0] + mask.size
    return call(
        prep_kernel,
        array((2 * half, tcrops.shape[1])),
        [tcrops, tpatch, scrops, spatch, mask],
        "hhhhv",
        scratch=[pltpu.VMEM(a.shape, BF16) for a in (tcrops, tpatch, scrops, spatch)]
        + [pltpu.SemaphoreType.DMA((4,))],
    )


def place_rows(core, crops, base, half, own, other, dest):
    rest = half - crops
    for side, ref in ((core, own), (1 - core, other)):
        at = pl.multiple_of(side * crops, crops)
        dest[pl.ds(at, crops), :] = ref[base : base + crops, :].astype(dest.dtype)
        at = pl.multiple_of(2 * crops + side * rest, 128)
        dest[pl.ds(at, rest), :] = ref[base + crops : base + half, :].astype(dest.dtype)


def row_blocks(start, stop):
    return [(a, min(a + 256, stop)) for a in range(start, stop, 256)]


def proto_source(core, protos):
    columns = protos.shape[1] // 2
    return lambda j: protos.at[:, pl.ds(pl.multiple_of(core * columns + j * BN, BN), BN)]


def proto_scratch(width):
    return [pltpu.VMEM((2, width, BN), BF16), pltpu.SemaphoreType.DMA((2,))]


def put_columns(step, heads, out):
    copies = out.shape[0]
    per_head = out.shape[1] // 2
    for head in range(2):
        for t in range(BN // 128):
            piece = heads[head][:, 128 * t : 128 * (t + 1)]
            out[:, pl.ds(head * per_head + step * (BN // 128) + t, 1), :] = jnp.broadcast_to(
                piece[None], (copies, 1, 128)
            )


def get_columns(step, head, lines):
    base = head * (lines.shape[0] // 2) + step * (BN // 128)
    return jnp.concatenate([lines[pl.ds(base + t, 1), :] for t in range(BN // 128)], axis=1)


def line_up(values):
    return jnp.concatenate([values[t : t + 1, :] for t in range(values.shape[0])], axis=1)


def teacher_kernel(crops, idx, own, other, protos, expo, sums, feats, buf, sem):
    rows, columns = expo.shape
    place_rows(idx[0], crops, 0, rows // 2, own, other, feats)

    def step(j, block):
        w = unit_cols(block[...])[0].astype(BF16)
        at = pl.multiple_of(j * BN, BN)
        heads = []
        for first, last in ((0, 2 * crops), (2 * crops, rows)):
            part = jnp.zeros((1, BN), F32)
            for start, stop in row_blocks(first, last):
                score = jnp.dot(feats[start:stop, :], w, preferred_element_type=F32)
                e = jnp.exp2(score * (LOG2E / TEACHER_TEMP)).astype(BF16)
                expo[start:stop, pl.ds(at, BN)] = e
                part = part + jnp.sum(e.astype(F32), axis=0, keepdims=True)
            heads.append(part)
        put_columns(j, heads, sums)

    stream(proto_source(idx[0], protos), buf, sem, columns // BN, step)


def teacher_pass(idx, own, other, protos, crops, copies):
    rows, width = own.shape
    columns = protos.shape[1] // 2
    return call(
        functools.partial(teacher_kernel, crops),
        [array((rows, columns), BF16), array((copies, 2 * columns // 128, 128))],
        [idx, own, other, protos],
        "svvh",
        scratch=[pltpu.VMEM((rows, width), BF16)] + proto_scratch(width),
        flops=2 * rows * width * columns,
        traffic=2 * rows * columns,
    )


def student_kernel(crops, idx, own, other, protos, total, mix, feats, acc, buf, sem):
    rows = feats.shape[0]
    place_rows(idx[0], crops, rows // 2, rows // 2, own, other, feats)
    acc[...] = jnp.zeros_like(acc)
    mix[...] = jnp.zeros_like(mix)

    def step(j, block):
        w = unit_cols(block[...])[0].astype(BF16)
        for start, stop in row_blocks(0, rows):
            score = jnp.dot(feats[start:stop, :], w, preferred_element_type=F32)
            p = jnp.exp2(score * (LOG2E / STUDENT_TEMP))
            part = p[:, :128]
            for t in range(1, BN // 128):
                part = part + p[:, 128 * t : 128 * (t + 1)]
            acc[start:stop, :] += part
            mix[start:stop, :] += lax.dot_general(
                p.astype(BF16), w, (((1,), (1,)), ((), ())), preferred_element_type=F32
            )

    stream(proto_source(idx[0], protos), buf, sem, protos.shape[1] // 2 // BN, step)
    for t in range(rows // 128):
        block = jnp.transpose(acc[128 * t : 128 * (t + 1), :])
        total[t : t + 1, :] = jnp.sum(block, axis=0, keepdims=True)


def student_pass(idx, own, other, protos, crops):
    rows, width = own.shape
    columns = protos.shape[1] // 2
    return call(
        functools.partial(student_kernel, crops),
        [array((rows // 128, 128)), array((rows, width))],
        [idx, own, other, protos],
        "svvh",
        scratch=[pltpu.VMEM((rows, width), BF16), pltpu.VMEM((rows, 128), F32)]
        + proto_scratch(width),
        flops=4 * rows * width * columns,
        traffic=2 * width * columns,
    )


def sum_rows(crops, expo, colscale, out):
    copies = out.shape[0]
    rows, columns = expo.shape
    per_head = columns // 128

    def block(i, _):
        head = jnp.where(i < 2 * crops // 128, 0, 1)
        at = pl.multiple_of(i * 128, 128)

        def chunk(k, acc):
            e = expo[pl.ds(at, 128), pl.ds(pl.multiple_of(k * 128, 128), 128)].astype(F32)
            return acc + e * colscale[pl.ds(head * per_head + k, 1), :]

        acc = lax.fori_loop(0, per_head, chunk, jnp.zeros((128, 128), F32), unroll=8)
        sums = jnp.sum(jnp.transpose(acc), axis=0, keepdims=True)
        out[:, pl.ds(i, 1), :] = jnp.broadcast_to(sums[None], (copies, 1, 128))
        return 0

    lax.fori_loop(0, rows // 128, block, 0)


def row_kernel(crops, extra, expo, colparts, *refs):
    if extra:
        total, out, colscale = refs
        count = total.shape[0]
        out[:, count:, :] = jnp.broadcast_to(total[...][None], (out.shape[0], count, 128))
    else:
        out, colscale = refs
    colscale[...] = 1.0 / jnp.sum(colparts[...], axis=0)
    sum_rows(crops, expo, colscale, out)


def row_pass(expo, colparts, total, crops, copies):
    rows, columns = expo.shape
    extra = total is not None
    return call(
        functools.partial(row_kernel, crops, extra),
        array((copies, rows // 128 * (2 if extra else 1), 128)),
        [expo, colparts] + ([total] if extra else []),
        "vvv" if extra else "vv",
        scratch=[pltpu.VMEM((2 * columns // 128, 128), F32)],
        flops=2 * rows * columns,
        traffic=2 * rows * columns,
    )


def last_row_kernel(crops, idx, expo, colparts, protos, out, target, colscale, buf, sem):
    rows, columns = expo.shape
    colscale[...] = 1.0 / jnp.sum(colparts[...], axis=0)
    target[...] = jnp.zeros_like(target)

    def step(j, block):
        wnorm = unit_cols(block[...])[0]
        at = pl.multiple_of(j * BN, BN)
        for head, (first, last) in enumerate(((0, 2 * crops), (2 * crops, rows))):
            w = (wnorm * get_columns(j, head, colscale)).astype(BF16)
            target[first:last, :] += lax.dot_general(
                expo[first:last, pl.ds(at, BN)],
                w,
                (((1,), (1,)), ((), ())),
                preferred_element_type=F32,
            )

    stream(proto_source(idx[0], protos), buf, sem, columns // BN, step)
    sum_rows(crops, expo, colscale, out)


def last_row_pass(idx, expo, colparts, protos, crops, copies):
    rows, columns = expo.shape
    width = protos.shape[0]
    return call(
        functools.partial(last_row_kernel, crops),
        [array((copies, rows // 128, 128)), array((rows, width))],
        [idx, expo, colparts, protos],
        "svvh",
        scratch=[pltpu.VMEM((2 * columns // 128, 128), F32)] + proto_scratch(width),
        flops=2 * rows * columns * width,
        traffic=2 * rows * columns,
    )


def split3(v):
    high = v.astype(BF16)
    rest = v - high.astype(F32)
    middle = rest.astype(BF16)
    low = (rest - middle.astype(F32)).astype(BF16)
    pad = jnp.zeros((13, v.shape[1]), F32)
    parts = [high.astype(F32), middle.astype(F32), low.astype(F32), pad]
    return jnp.concatenate(parts, axis=0).astype(BF16)


def column_kernel(crops, expo, rowparts, out):
    rows, columns = expo.shape
    scale = line_up(1.0 / jnp.sum(rowparts[:, : rows // 128, :], axis=0))
    spans = [(0, 2 * crops), (2 * crops, rows)]
    lefts = [split3(scale[:, first:last]) for first, last in spans]
    for j in range(columns // BN):
        heads = []
        for left, (first, last) in zip(lefts, spans):
            sums = jnp.dot(
                left, expo[first:last, j * BN : (j + 1) * BN], preferred_element_type=F32
            )
            heads.append(sums[0:1, :] + sums[1:2, :] + sums[2:3, :])
        put_columns(j, heads, out)


def column_pass(expo, rowparts, crops, copies):
    rows, columns = expo.shape
    return call(
        functools.partial(column_kernel, crops),
        array((copies, 2 * columns // 128, 128)),
        [expo, rowparts],
        "vv",
        flops=2 * rows * columns,
        traffic=2 * rows * columns,
    )


def part_source(idx, ny, protos):
    columns = protos.shape[1] // 2
    part = columns // ny
    at = pl.multiple_of(idx[0] * columns + idx[3] * part, 128)
    return protos.at[:, pl.ds(at, part)]


def stream_rows(ny, base, half, own, other, buf, sem, body):
    def copy(step, slot):
        ref = own if step < ny else other
        return pltpu.make_async_copy(
            ref.at[step % ny, pl.ds(base, half), :], buf.at[slot], sem.at[slot]
        )

    copy(0, 0).start()
    for step in range(2 * ny):
        if step + 1 < 2 * ny:
            copy(step + 1, (step + 1) % 2).start()
        copy(step, step % 2).wait()
        body(step // ny, step % ny, buf.at[step % 2])


def wide_teacher_kernel(ny, crops, idx, own, other, protos, expo_d, expo_i, w, wbuf, buf, sem, wsem):
    half = buf.shape[1]
    rest = half - crops
    fetch = pltpu.make_async_copy(part_source(idx, ny, protos), wbuf, wsem)
    fetch.start()
    fetch.wait()
    w[...] = unit_cols(wbuf[...])[0].astype(BF16)

    def body(side, y, ref):
        place = 2 * y + jnp.where(idx[0] == side, 0, 1)
        feats = ref[...].astype(BF16)
        for start in range(0, half, 128):
            score = jnp.dot(feats[start : start + 128, :], w[...], preferred_element_type=F32)
            e = jnp.exp2(score * (LOG2E / TEACHER_TEMP)).astype(BF16)
            if start < crops:
                expo_d[pl.ds(pl.multiple_of(place * crops + start, 128), 128), :] = e
            else:
                at = pl.multiple_of(place * rest + start - crops, 128)
                expo_i[pl.ds(at, 128), :] = e

    stream_rows(ny, 0, half, own, other, buf, sem, body)


def wide_teacher_pass(idx, own, other, protos, crops):
    ny, rows, width = own.shape
    half = rows // 2
    part = protos.shape[1] // 2 // ny
    return call(
        functools.partial(wide_teacher_kernel, ny, crops),
        [array((2 * ny * crops, part), BF16), array((2 * ny * (half - crops), part), BF16)],
        [idx, own, other, protos],
        "shhh",
        scratch=[
            pltpu.VMEM((width, part), BF16),
            pltpu.VMEM((width, part), BF16),
            pltpu.VMEM((2, half, width), F32),
            pltpu.SemaphoreType.DMA((2,)),
            pltpu.SemaphoreType.DMA,
        ],
        flops=2 * 2 * ny * half * width * part,
        traffic=8 * ny * half * width,
    )


def wide_student_kernel(ny, crops, idx, own, other, protos, *refs):
    totals = refs[:ny]
    out, wnorm_out, turned_d, turned_i, w, wbuf, scale, left, expo, buf, sem, wsem = refs[ny:]
    half = buf.shape[1]
    rest = half - crops
    sub = totals[0].shape[0]
    fetch = pltpu.make_async_copy(part_source(idx, ny, protos), wbuf, wsem)
    fetch.start()
    for s in range(ny):
        y = lax.rem(idx[3] + ny - s, ny)
        scale[pl.ds(pl.multiple_of(y * sub, sub), sub), :] = GRAD_SCALE / totals[s][...]
    fetch.wait()
    wnorm_out[...] = unit_cols(wbuf[...])[0]
    w[...] = wnorm_out[...].astype(BF16)
    out[...] = jnp.zeros_like(out)

    def body(side, y, ref):
        core = jnp.where(idx[0] == side, 0, 1)
        place = 2 * y + core
        feats = ref[...].astype(BF16)
        turned = jnp.transpose(feats.astype(F32))
        turned_d[:, pl.ds(pl.multiple_of(place * crops, 128), crops)] = turned[:, :crops].astype(BF16)
        turned_i[:, pl.ds(pl.multiple_of(place * rest, 128), rest)] = turned[:, crops:].astype(BF16)
        lines = [scale[pl.ds(y * sub + core * (crops // 128) + t, 1), :] for t in range(crops // 128)]
        first = y * sub + 2 * crops // 128 + core * (rest // 128)
        lines += [scale[pl.ds(first + t, 1), :] for t in range(rest // 128)]
        left[...] = (turned * jnp.concatenate(lines, axis=1)).astype(BF16)
        for start in range(0, half, 128):
            score = jnp.dot(feats[start : start + 128, :], w[...], preferred_element_type=F32)
            expo[start : start + 128, :] = jnp.exp2(score * (LOG2E / STUDENT_TEMP)).astype(BF16)
        out[...] += jnp.dot(left[...], expo[...], preferred_element_type=F32)

    stream_rows(ny, half, half, own, other, buf, sem, body)


def wide_student_pass(idx, own, other, protos, totals, crops):
    ny, rows, width = own.shape
    half = rows // 2
    part = protos.shape[1] // 2 // ny
    return call(
        functools.partial(wide_student_kernel, ny, crops),
        [
            array((width, part)),
            array((width, part)),
            array((width, 2 * ny * crops), BF16),
            array((width, 2 * ny * (half - crops)), BF16),
        ],
        [idx, own, other, protos, *totals],
        "shhh" + "v" * ny,
        scratch=[
            pltpu.VMEM((width, part), BF16),
            pltpu.VMEM((width, part), BF16),
            pltpu.VMEM((ny * rows // 128, 128), F32),
            pltpu.VMEM((width, half), BF16),
            pltpu.VMEM((half, part), BF16),
            pltpu.VMEM((2, half, width), F32),
            pltpu.SemaphoreType.DMA((2,)),
            pltpu.SemaphoreType.DMA,
        ],
        flops=4 * 2 * ny * half * width * part,
        traffic=8 * ny * half * width,
    )


def weight_kernel(ny, crops, idx, prob, wnorm, turned_d, turned_i, expo_d, expo_i, colparts, rowparts, out, left_d, left_i, scales, rowscale):
    copies, _, _ = out.shape
    width, part = prob.shape
    own = width // copies
    group = rowparts.shape[0] // ny
    sub = rowparts.shape[1]
    scales[...] = GRAD_SCALE / jnp.sum(colparts[...], axis=0)
    for y in range(ny):
        rowscale[y * sub : (y + 1) * sub, :] = 1.0 / jnp.sum(
            rowparts[y * group : (y + 1) * group], axis=0
        )
    cd = crops // 128
    ci = sub // 2 - cd
    lines_d, lines_i = [], []
    for y in range(ny):
        for core in range(2):
            for t in range(cd):
                at = y * sub + core * cd + t
                lines_d.append(rowscale[at : at + 1, :])
            for t in range(ci):
                at = y * sub + 2 * cd + core * ci + t
                lines_i.append(rowscale[at : at + 1, :])
    left_d[...] = (turned_d[...].astype(F32) * jnp.concatenate(lines_d, axis=1)).astype(BF16)
    left_i[...] = (turned_i[...].astype(F32) * jnp.concatenate(lines_i, axis=1)).astype(BF16)
    per_head = scales.shape[0] // 2
    first = idx[3] * (part // 128)
    for at in range(0, part, BN):
        span = slice(at, at + BN)
        wsum = prob[:, span]
        for head, (left, expo) in enumerate(((left_d, expo_d), (left_i, expo_i))):
            target = jnp.dot(left[...], expo[:, span], preferred_element_type=F32)
            base = head * per_head + first + at // 128
            line = [scales[pl.ds(base + t, 1), :] for t in range(BN // 128)]
            wsum = wsum - target * jnp.concatenate(line, axis=1)
        coldot = jnp.sum(wnorm[:, span] * wsum, axis=0, keepdims=True)
        for t in range(BN // 128):
            lanes = slice(128 * t, 128 * (t + 1))
            row = at // 128 + t
            for d in range(copies):
                out[d, row * own : (row + 1) * own, :] = wsum[d * own : (d + 1) * own, lanes]
            tail = part // 128 * own + row
            out[:, tail : tail + 1, :] = jnp.broadcast_to(
                coldot[:, lanes][None], (copies, 1, 128)
            )


def weight_pass(idx, prob, wnorm, turned, expo, colparts, rowparts, crops, ny, copies):
    width, part = prob.shape
    lines = part // 128 * (width // copies + 1)
    rows = turned[0].shape[1] + turned[1].shape[1]
    return call(
        functools.partial(weight_kernel, ny, crops),
        array((copies, lines, 128)),
        [idx, prob, wnorm, *turned, *expo, colparts, rowparts],
        "svvvvvvvv",
        scratch=[
            pltpu.VMEM(turned[0].shape, BF16),
            pltpu.VMEM(turned[1].shape, BF16),
            pltpu.VMEM(colparts.shape[1:], F32),
            pltpu.VMEM((ny * rowparts.shape[1], 128), F32),
        ],
        flops=2 * rows * width * part,
        traffic=2 * rows * part,
    )


def norm_kernel(protos, out):
    out[...] = unit_cols(protos[...])[1]


def norm_pass(protos):
    width, columns = protos.shape
    step = columns // 8
    return pl.pallas_call(
        norm_kernel,
        grid=(8,),
        in_specs=[pl.BlockSpec((width, step), lambda j: (0, j))],
        out_specs=pl.BlockSpec((1, step), lambda j: (0, j)),
        out_shape=array((1, columns)),
        compiler_params=pltpu.CompilerParams(vmem_limit_bytes=VMEM_LIMIT),
        cost_estimate=pl.CostEstimate(
            flops=3 * width * columns, bytes_accessed=2 * width * columns, transcendentals=0
        ),
    )(protos)


def proto_kernel(nx, ny, idx, parts, protos, winv, out, rows, sem):
    own, columns = out.shape
    copies = parts.shape[0]
    part = columns // (2 * ny)
    tail = part // 128 * own
    at = pl.multiple_of(idx[2] * (2 * own), 2 * own)
    fetch = pltpu.make_async_copy(protos.at[pl.ds(at, 2 * own), :], rows, sem)
    fetch.start()
    fetch.wait()
    for y in range(ny):
        for core in range(2):
            for t in range(part // 128):
                first = core * (columns // 2) + y * part + 128 * t
                lanes = slice(first, first + 128)
                wsum = jnp.zeros((own, 128), F32)
                coldot = jnp.zeros((1, 128), F32)
                for x in range(nx):
                    source = (x * ny + y) * 2 + core
                    wsum = wsum + parts[source, t * own : (t + 1) * own, :]
                    coldot = coldot + parts[source, tail + t : tail + t + 1, :]
                inv = winv[:, lanes]
                both = rows[:, lanes].astype(F32)
                wnorm = jnp.where(idx[0] == 0, both[:own, :], both[own:, :]) * inv
                out[:, lanes] = (wsum - wnorm * coldot) * inv


def proto_pass(idx, parts, protos, winv, nx, ny):
    width, columns = protos.shape
    own = width // parts.shape[0]
    return call(
        functools.partial(proto_kernel, nx, ny),
        array((own, columns)),
        [idx, parts, protos, winv],
        "svhv",
        scratch=[pltpu.VMEM((2 * own, columns), BF16), pltpu.SemaphoreType.DMA],
    )


def spread_row(line):
    return jnp.transpose(jnp.broadcast_to(line, (128, 128)))


def scaled_kernel(crops, idx, mix, totals, mine, theirs, buf):
    rows, width = mix.shape
    prob = GRAD_SCALE / totals[...]
    for t in range(rows // 128):
        span = slice(128 * t, 128 * (t + 1))
        p = jnp.concatenate([spread_row(prob[t : t + 1, :])] * (width // 128), axis=1)
        buf[span, :] = mix[span, :] * p
    part_rows(crops, idx, buf, mine, theirs)


def plain_kernel(crops, idx, mix, mine, theirs):
    part_rows(crops, idx, mix, mine, theirs)


def part_rows(crops, idx, buf, mine, theirs):
    rest = mine.shape[0] - crops
    for side, ref in ((idx[0], mine), (1 - idx[0], theirs)):
        ref[:crops, :] = buf[pl.ds(pl.multiple_of(side * crops, crops), crops), :]
        ref[crops:, :] = buf[pl.ds(pl.multiple_of(2 * crops + side * rest, 128), rest), :]


def part_pass(idx, mix, totals, crops):
    rows, width = mix.shape
    shapes = [array((rows // 2, width)), array((rows // 2, width))]
    if totals is None:
        return call(functools.partial(plain_kernel, crops), shapes, [idx, mix], "sv")
    return call(
        functools.partial(scaled_kernel, crops),
        shapes,
        [idx, mix, totals],
        "svv",
        scratch=[pltpu.VMEM((rows, width), F32)],
    )


def pack_kernel(nz, crops, mine, came, out):
    half = mine.shape[0]
    chunk = half // nz
    share = crops // nz
    rest = chunk - share
    for z in range(nz):
        for src, dst, size in ((z * share, z * chunk, share), (crops + z * rest, z * chunk + share, rest)):
            out[dst : dst + size, :] = mine[src : src + size, :] + came[src : src + size, :]


def pack_pass(mine, came, nz, crops):
    return call(functools.partial(pack_kernel, nz, crops), array(mine.shape), [mine, came], "vv")


def feature_kernel(nz, ny, crops, pair, patches, idx, mask, rowparts, *refs):
    count = 4 if pair else 2
    pieces = refs[:count]
    all_crops, all_rows, crop_out, patch_out, masked_rows, dense, scale, crop_rows = refs[count:]
    z = idx[1]
    masked = mask.shape[1]
    crop_share = crop_out.shape[0]
    share = patch_out.shape[0]
    crop_at = pl.multiple_of(z * crop_share, 16)
    patch_at = pl.multiple_of(z * share, 128)
    rest = pieces[0].shape[0] - crop_share
    sub = rowparts.shape[1]
    group = rowparts.shape[0] // ny
    cd = crops // 128
    ci = sub // 2 - cd
    sums = jnp.sum(rowparts[pl.ds(idx[3] * group, group), :, :], axis=0)
    row = GRAD_SCALE / sums
    low = idx[0] == 0
    for t in range(cd + ci):
        a, b = (t, cd + t) if t < cd else (cd + t, cd + ci + t)
        line = jnp.where(low, row[a : a + 1, :], row[b : b + 1, :])
        scale[128 * t : 128 * (t + 1), :] = spread_row(line)
    wide = pieces[0].shape[1] // 128

    def fgrad(prob, target, at, size):
        r = scale[pl.ds(pl.multiple_of(at, 16), size), :]
        return prob - target * jnp.concatenate([r] * wide, axis=1)

    crop_rows[...] = fgrad(
        pieces[0][:crop_share, :], pieces[1][:crop_share, :], z * crop_share, crop_share
    )
    spots = ((z, 0),) if not pair else ((z, 0), (z + 1 - 2 * lax.rem(z, 2), 2))
    for place, which in spots:
        value = fgrad(
            pieces[which][crop_share:, :], pieces[which + 1][crop_share:, :], crops + place * rest, rest
        )
        at = pl.multiple_of(lax.rem(place, 2) * rest, 8) if pair else 0
        masked_rows[pl.ds(at, rest), :] = value
    dense[...] = jnp.zeros_like(dense)
    first_row = z * share
    first_image = first_row // patches
    offset = first_row - first_image * patches
    for image in range(masked_rows.shape[0] // masked):

        def put(m, _):
            at = mask[first_image + image, m] + image * patches - offset

            @pl.when(jnp.logical_and(at >= 0, at < share))
            def _():
                dense[pl.ds(at, 1), :] = masked_rows[pl.ds(image * masked + m, 1), :]

            return 0

        lax.fori_loop(0, masked, put, 0, unroll=4)

    def back(x, d):
        xf = x.astype(F32)
        inv = lax.rsqrt(jnp.sum(xf * xf, axis=-1, keepdims=True) + EPS)
        u = xf * inv
        return (d - u * jnp.sum(u * d, axis=-1, keepdims=True)) * inv

    crop_out[...] = back(all_crops[pl.ds(crop_at, crop_share), :], crop_rows[...])
    patch_out[...] = back(all_rows[pl.ds(patch_at, share), :], dense[...])


def feature_pass(idx, mask, rowparts, pieces, all_crops, all_rows, nz, ny, patches):
    crops, width = all_crops.shape
    crop_share = crops // nz
    share = all_rows.shape[0] // nz
    pair = len(pieces) == 4
    count = len(pieces) // 2 * (pieces[0].shape[0] - crop_share)
    half = rowparts.shape[1] // 2 * 128
    return call(
        functools.partial(feature_kernel, nz, ny, crops, pair, patches),
        [array((crop_share, width)), array((share, width))],
        [idx, mask, rowparts, *pieces, all_crops, all_rows],
        "ssv" + "v" * len(pieces) + "vv",
        scratch=[
            pltpu.VMEM((count, width), F32),
            pltpu.VMEM((share, width), F32),
            pltpu.VMEM((half, 128), F32),
            pltpu.VMEM((crop_share, width), F32),
        ],
    )


def shifted(n, s):
    return [(i, (i + s) % n) for i in range(n)]


def local(
    sizes,
    student_crops,
    teacher_crops,
    student_patches,
    teacher_patches,
    patch_mask,
    student_protos,
    teacher_protos,
):
    nx, ny, nz = sizes
    images, masked = patch_mask.shape
    patches = student_patches.shape[0] // images
    crops = student_crops.shape[0]
    ix, iy, ic, iz = (lax.axis_index(a) for a in ("x", "y", "c", "z"))
    idx = jnp.stack([ic, iz, ix * ny + iy, iy]).astype(jnp.int32)
    swap = [(0, 1), (1, 0)]

    own = prep(teacher_crops, teacher_patches, student_crops, student_patches, patch_mask)
    other = lax.ppermute(own, "c", swap)
    all_own = lax.all_gather(own, "y")
    all_other = lax.ppermute(all_own, "c", swap)

    expo, sums = teacher_pass(idx, own, other, teacher_protos, crops, nx * ny)
    sub = 2 * (crops + images * masked) // 128
    for step in range(ITERS):
        colparts = lax.all_to_all(sums, ("x", "y"), 0, 0)
        if step == 0:
            total, mix = student_pass(idx, own, other, student_protos, crops)
        if step < ITERS - 1:
            sums = row_pass(expo, colparts, total if step == 0 else None, crops, 2 * nz)
            rowparts = lax.all_to_all(sums, ("c", "z"), 0, 0)
            if step == 0:
                totals = jnp.sum(rowparts[:, sub:, :], axis=0)
            sums = column_pass(expo, rowparts, crops, nx * ny)
        else:
            sums, target = last_row_pass(
                idx, expo, colparts, student_protos, crops, 2 * nz * ny
            )
            rowparts = lax.all_to_all(sums, ("y", "c", "z"), 0, 0)

    all_totals = [totals] + [lax.ppermute(totals, "y", shifted(ny, s)) for s in range(1, ny)]
    wide_expo = wide_teacher_pass(idx, all_own, all_other, teacher_protos, crops)
    prob, wnorm, *turned = wide_student_pass(
        idx, all_own, all_other, student_protos, all_totals, crops
    )
    winv = norm_pass(student_protos)
    outgoing = weight_pass(
        idx, prob, wnorm, turned, wide_expo, colparts, rowparts, crops, ny, nx * ny * 2
    )
    parts = lax.all_to_all(outgoing, ("x", "y", "c"), 0, 0)
    proto_grad = proto_pass(idx, parts, student_protos, winv, nx, ny)

    reduced = []
    for value, scale in ((mix, totals), (target, None)):
        mine, theirs = part_pass(idx, value, scale, crops)
        packed = pack_pass(mine, lax.ppermute(theirs, "c", swap), nz, crops)
        reduced.append(lax.psum_scatter(packed, "z", scatter_dimension=0, tiled=True))
    pieces = list(reduced)
    if student_patches.shape[0] // nz < patches:
        pair = [(i, i ^ 1) for i in range(nz)]
        pieces += [lax.ppermute(r, "z", pair) for r in reduced]
    crop_grad, patch_grad = feature_pass(
        idx, patch_mask, rowparts, pieces, student_crops, student_patches, nz, ny, patches
    )
    return (proto_grad, crop_grad, patch_grad)


def solution(mesh):
    dp, nz = mesh.devices.shape
    nx = 4 if dp == 32 else 2
    ny = dp // (2 * nx)
    grid = Mesh(mesh.devices.reshape(nx, ny, 2, nz), ("x", "y", "c", "z"))
    rows = ("x", "y", "c")
    in_specs = (
        P(rows, None),
        P(rows, None),
        P(rows, None),
        P(rows, None),
        P(rows, None),
        P(None, "z"),
        P(None, "z"),
    )
    out_specs = (P(rows, "z"), P(rows + ("z",), None), P(rows + ("z",), None))
    return jax.shard_map(
        functools.partial(local, (nx, ny, nz)),
        mesh=grid,
        in_specs=in_specs,
        out_specs=out_specs,
        check_vma=False,
    )
```

```python
import functools

import jax
import jax.numpy as jnp
from jax import lax
from jax.experimental import pallas as pl
from jax.experimental.pallas import tpu as pltpu
from jax.sharding import Mesh, PartitionSpec as P

ITERS = 3
EPS = 1e-06
TEACHER_TEMP = 0.07
STUDENT_TEMP = 0.1
LOSS_SCALE = 256.0
GRAD_SCALE = LOSS_SCALE / STUDENT_TEMP
LOG2E = 1.4426950408889634

BN = 512
F32 = jnp.float32
BF16 = jnp.bfloat16
VMEM_LIMIT = 58 * 1024 * 1024
SMEM = pl.BlockSpec(memory_space=pltpu.SMEM)
VMEM = pl.BlockSpec(memory_space=pltpu.VMEM)
HBM = pl.BlockSpec(memory_space=pltpu.HBM)


def call(kernel, out_shape, args, specs, outs="", scratch=(), flops=0, traffic=0):
    spaces = {"s": SMEM, "v": VMEM, "h": HBM}
    if not isinstance(out_shape, list):
        out_specs = VMEM
    else:
        out_specs = [spaces[letter] for letter in outs or "v" * len(out_shape)]
    return pl.pallas_call(
        kernel,
        out_shape=out_shape,
        out_specs=out_specs,
        in_specs=[spaces[letter] for letter in specs],
        scratch_shapes=list(scratch),
        compiler_params=pltpu.CompilerParams(vmem_limit_bytes=VMEM_LIMIT),
        cost_estimate=pl.CostEstimate(flops=flops, bytes_accessed=traffic, transcendentals=0),
    )(*args)


def array(shape, dtype=F32):
    return jax.ShapeDtypeStruct(shape, dtype)


def stream(source, buf, sem, steps, body):
    def copy(j, slot):
        return pltpu.make_async_copy(source(j), buf.at[slot], sem.at[slot])

    copy(0, 0).start()

    def step(j, _):
        slot = lax.rem(j, 2)

        @pl.when(j + 1 < steps)
        def _():
            copy(j + 1, 1 - slot).start()

        copy(j, slot).wait()
        body(j, buf.at[slot])
        return 0

    lax.fori_loop(0, steps, step, 0)


def unit(x):
    xf = x.astype(F32)
    return xf * lax.rsqrt(jnp.sum(xf * xf, axis=-1, keepdims=True) + EPS)


def unit_cols(w):
    wf = w.astype(F32)
    inv = lax.rsqrt(jnp.sum(wf * wf, axis=0, keepdims=True) + EPS)
    return wf * inv, inv


def prep_kernel(tcrops, tpatch, scrops, spatch, mask, out, tc, tp, sc, sp, sem):
    images, masked = mask.shape
    patches = tp.shape[0] // images
    count = tc.shape[0]
    half = out.shape[0] // 2
    copies = [
        pltpu.make_async_copy(src, dst, sem.at[i])
        for i, (src, dst) in enumerate(((tcrops, tc), (tpatch, tp), (scrops, sc), (spatch, sp)))
    ]
    for copy in copies:
        copy.start()
    for side, (crops, patch_rows) in enumerate(((tc, tp), (sc, sp))):
        copies[2 * side].wait()
        copies[2 * side + 1].wait()
        base = side * half
        out[base : base + count, :] = unit(crops[...])
        for i in range(images):
            place = lax.broadcasted_iota(jnp.int32, (patches, masked), 0)
            chosen = (place == mask[i : i + 1, :]).astype(F32).astype(BF16)
            rows = lax.dot_general(
                chosen,
                patch_rows[i * patches : (i + 1) * patches, :],
                (((0,), (0,)), ((), ())),
                preferred_element_type=F32,
            )
            at = base + count + i * masked
            out[at : at + masked, :] = unit(rows)


def prep(tcrops, tpatch, scrops, spatch, mask):
    half = tcrops.shape[0] + mask.size
    return call(
        prep_kernel,
        array((2 * half, tcrops.shape[1])),
        [tcrops, tpatch, scrops, spatch, mask],
        "hhhhv",
        scratch=[pltpu.VMEM(a.shape, BF16) for a in (tcrops, tpatch, scrops, spatch)]
        + [pltpu.SemaphoreType.DMA((4,))],
    )


def place_rows(core, crops, base, half, own, other, dest):
    rest = half - crops
    for side, ref in ((core, own), (1 - core, other)):
        at = pl.multiple_of(side * crops, crops)
        dest[pl.ds(at, crops), :] = ref[base : base + crops, :].astype(dest.dtype)
        at = pl.multiple_of(2 * crops + side * rest, 128)
        dest[pl.ds(at, rest), :] = ref[base + crops : base + half, :].astype(dest.dtype)


def row_blocks(start, stop):
    return [(a, min(a + 256, stop)) for a in range(start, stop, 256)]


def proto_source(core, protos):
    columns = protos.shape[1] // 2
    return lambda j: protos.at[:, pl.ds(pl.multiple_of(core * columns + j * BN, BN), BN)]


def proto_scratch(width):
    return [pltpu.VMEM((2, width, BN), BF16), pltpu.SemaphoreType.DMA((2,))]


def put_columns(step, heads, out):
    copies = out.shape[0]
    per_head = out.shape[1] // 2
    for head in range(2):
        for t in range(BN // 128):
            piece = heads[head][:, 128 * t : 128 * (t + 1)]
            out[:, pl.ds(head * per_head + step * (BN // 128) + t, 1), :] = jnp.broadcast_to(
                piece[None], (copies, 1, 128)
            )


def get_columns(step, head, lines):
    base = head * (lines.shape[0] // 2) + step * (BN // 128)
    return jnp.concatenate([lines[pl.ds(base + t, 1), :] for t in range(BN // 128)], axis=1)


def line_up(values):
    return jnp.concatenate([values[t : t + 1, :] for t in range(values.shape[0])], axis=1)


def teacher_kernel(crops, idx, own, other, protos, expo, sums, feats, out, osem, buf, sem):
    rows, columns = expo.shape
    place_rows(idx[0], crops, 0, rows // 2, own, other, feats)
    steps = columns // BN

    def leave(j, slot):
        at = pl.multiple_of(j * BN, BN)
        return pltpu.make_async_copy(out.at[slot], expo.at[:, pl.ds(at, BN)], osem.at[slot])

    def step(j, block):
        w = unit_cols(block[...])[0].astype(BF16)
        slot = lax.rem(j, 2)

        @pl.when(j >= 2)
        def _():
            leave(j - 2, slot).wait()

        heads = []
        for first, last in ((0, 2 * crops), (2 * crops, rows)):
            part = jnp.zeros((1, BN), F32)
            for start, stop in row_blocks(first, last):
                score = jnp.dot(feats[start:stop, :], w, preferred_element_type=F32)
                e = jnp.exp2(score * (LOG2E / TEACHER_TEMP)).astype(BF16)
                out[slot, start:stop, :] = e
                part = part + jnp.sum(e.astype(F32), axis=0, keepdims=True)
            heads.append(part)
        leave(j, slot).start()
        put_columns(j, heads, sums)

    stream(proto_source(idx[0], protos), buf, sem, steps, step)
    for j in (steps - 2, steps - 1):
        leave(j, j % 2).wait()


def teacher_pass(idx, own, other, protos, crops, copies):
    rows, width = own.shape
    columns = protos.shape[1] // 2
    return call(
        functools.partial(teacher_kernel, crops),
        [array((rows, columns), BF16), array((copies, 2 * columns // 128, 128))],
        [idx, own, other, protos],
        "svvh",
        "hv",
        scratch=[
            pltpu.VMEM((rows, width), BF16),
            pltpu.VMEM((2, rows, BN), BF16),
            pltpu.SemaphoreType.DMA((2,)),
        ]
        + proto_scratch(width),
        flops=2 * rows * width * columns,
        traffic=2 * rows * columns,
    )


def student_kernel(crops, idx, own, other, protos, total, mix, feats, acc, buf, sem):
    rows = feats.shape[0]
    place_rows(idx[0], crops, rows // 2, rows // 2, own, other, feats)
    acc[...] = jnp.zeros_like(acc)
    mix[...] = jnp.zeros_like(mix)

    def step(j, block):
        w = unit_cols(block[...])[0].astype(BF16)
        for start, stop in row_blocks(0, rows):
            score = jnp.dot(feats[start:stop, :], w, preferred_element_type=F32)
            p = jnp.exp2(score * (LOG2E / STUDENT_TEMP))
            part = p[:, :128]
            for t in range(1, BN // 128):
                part = part + p[:, 128 * t : 128 * (t + 1)]
            acc[start:stop, :] += part
            mix[start:stop, :] += lax.dot_general(
                p.astype(BF16), w, (((1,), (1,)), ((), ())), preferred_element_type=F32
            )

    stream(proto_source(idx[0], protos), buf, sem, protos.shape[1] // 2 // BN, step)
    for t in range(rows // 128):
        block = jnp.transpose(acc[128 * t : 128 * (t + 1), :])
        total[t : t + 1, :] = jnp.sum(block, axis=0, keepdims=True)


def student_pass(idx, own, other, protos, crops):
    rows, width = own.shape
    columns = protos.shape[1] // 2
    return call(
        functools.partial(student_kernel, crops),
        [array((rows // 128, 128)), array((rows, width))],
        [idx, own, other, protos],
        "svvh",
        scratch=[pltpu.VMEM((rows, width), BF16), pltpu.VMEM((rows, 128), F32)]
        + proto_scratch(width),
        flops=4 * rows * width * columns,
        traffic=2 * width * columns,
    )


def row_copies(source, dest, sems):
    return [
        pltpu.make_async_copy(
            source.at[pl.ds(128 * i, 128), :], dest.at[pl.ds(128 * i, 128), :], sems.at[i]
        )
        for i in range(source.shape[0] // 128)
    ]


def column_copies(source, dest, sems):
    return [
        pltpu.make_async_copy(
            source.at[:, pl.ds(BN * j, BN)], dest.at[:, pl.ds(BN * j, BN)], sems.at[j]
        )
        for j in range(source.shape[1] // BN)
    ]


def expo_scratch(expo, blocks):
    return [pltpu.VMEM(expo.shape, BF16), pltpu.SemaphoreType.DMA((blocks,))]


def sum_rows(crops, expo, copies_in, colscale, out):
    copies = out.shape[0]
    rows, columns = expo.shape
    per_head = columns // 128

    for i in range(rows // 128):
        copies_in[i].wait()
        head = 0 if i < 2 * crops // 128 else 1
        at = 128 * i

        def chunk(k, acc):
            e = expo[pl.ds(at, 128), pl.ds(pl.multiple_of(k * 128, 128), 128)].astype(F32)
            return acc + e * colscale[pl.ds(head * per_head + k, 1), :]

        acc = lax.fori_loop(0, per_head, chunk, jnp.zeros((128, 128), F32), unroll=8)
        sums = jnp.sum(jnp.transpose(acc), axis=0, keepdims=True)
        out[:, i : i + 1, :] = jnp.broadcast_to(sums[None], (copies, 1, 128))


def row_kernel(crops, extra, expo, colparts, *refs):
    out, colscale, buf, sems = refs[-4:]
    copies_in = row_copies(expo, buf, sems)
    for copy in copies_in:
        copy.start()
    if extra:
        total = refs[0]
        count = total.shape[0]
        out[:, count:, :] = jnp.broadcast_to(total[...][None], (out.shape[0], count, 128))
    colscale[...] = 1.0 / jnp.sum(colparts[...], axis=0)
    sum_rows(crops, buf, copies_in, colscale, out)


def row_pass(expo, colparts, total, crops, copies):
    rows, columns = expo.shape
    extra = total is not None
    return call(
        functools.partial(row_kernel, crops, extra),
        array((copies, rows // 128 * (2 if extra else 1), 128)),
        [expo, colparts] + ([total] if extra else []),
        "hvv" if extra else "hv",
        scratch=[pltpu.VMEM((2 * columns // 128, 128), F32)] + expo_scratch(expo, rows // 128),
        flops=2 * rows * columns,
        traffic=2 * rows * columns,
    )


def target_kernel(crops, idx, expo, colparts, protos, mine, theirs, target, colscale, ebuf, esem, buf, sem):
    rows, columns = expo.shape
    steps = columns // BN
    copies_in = column_copies(expo, ebuf, esem)
    for copy in copies_in:
        copy.start()
    colscale[...] = 1.0 / jnp.sum(colparts[...], axis=0)
    target[...] = jnp.zeros_like(target)

    def step(j, block):
        wnorm = unit_cols(block[...])[0]
        at = pl.multiple_of(j * BN, BN)
        pltpu.make_async_copy(
            expo.at[:, pl.ds(at, BN)], ebuf.at[:, pl.ds(at, BN)], esem.at[j]
        ).wait()
        for head, (first, last) in enumerate(((0, 2 * crops), (2 * crops, rows))):
            w = (wnorm * get_columns(j, head, colscale)).astype(BF16)
            target[first:last, :] += lax.dot_general(
                ebuf[first:last, pl.ds(at, BN)],
                w,
                (((1,), (1,)), ((), ())),
                preferred_element_type=F32,
            )

    stream(proto_source(idx[0], protos), buf, sem, steps, step)
    part_rows(crops, idx, target, mine, theirs)


def target_pass(idx, expo, colparts, protos, crops):
    rows, columns = expo.shape
    width = protos.shape[0]
    return call(
        functools.partial(target_kernel, crops),
        [array((rows // 2, width)), array((rows // 2, width))],
        [idx, expo, colparts, protos],
        "shvh",
        scratch=[pltpu.VMEM((rows, width), F32), pltpu.VMEM((2 * columns // 128, 128), F32)]
        + expo_scratch(expo, columns // BN)
        + proto_scratch(width),
        flops=2 * rows * columns * width,
        traffic=2 * rows * columns,
    )


def split3(v):
    high = v.astype(BF16)
    rest = v - high.astype(F32)
    middle = rest.astype(BF16)
    low = (rest - middle.astype(F32)).astype(BF16)
    pad = jnp.zeros((13, v.shape[1]), F32)
    parts = [high.astype(F32), middle.astype(F32), low.astype(F32), pad]
    return jnp.concatenate(parts, axis=0).astype(BF16)


def column_kernel(crops, expo, rowparts, out, buf, sems):
    rows, columns = expo.shape
    copies_in = column_copies(expo, buf, sems)
    for copy in copies_in:
        copy.start()
    scale = line_up(1.0 / jnp.sum(rowparts[:, : rows // 128, :], axis=0))
    spans = [(0, 2 * crops), (2 * crops, rows)]
    lefts = [split3(scale[:, first:last]) for first, last in spans]
    for j in range(columns // BN):
        copies_in[j].wait()
        heads = []
        for left, (first, last) in zip(lefts, spans):
            sums = jnp.dot(
                left, buf[first:last, j * BN : (j + 1) * BN], preferred_element_type=F32
            )
            heads.append(sums[0:1, :] + sums[1:2, :] + sums[2:3, :])
        put_columns(j, heads, out)


def column_pass(expo, rowparts, crops, copies):
    rows, columns = expo.shape
    return call(
        functools.partial(column_kernel, crops),
        array((copies, 2 * columns // 128, 128)),
        [expo, rowparts],
        "hv",
        scratch=expo_scratch(expo, columns // BN),
        flops=2 * rows * columns,
        traffic=2 * rows * columns,
    )


def part_source(idx, ny, protos):
    columns = protos.shape[1] // 2
    part = columns // ny
    at = pl.multiple_of(idx[0] * columns + idx[3] * part, 128)
    return protos.at[:, pl.ds(at, part)]


def stream_rows(ny, base, half, own, other, buf, sem, body):
    def copy(step, slot):
        ref = own if step < ny else other
        return pltpu.make_async_copy(
            ref.at[step % ny, pl.ds(base, half), :], buf.at[slot], sem.at[slot]
        )

    copy(0, 0).start()
    for step in range(2 * ny):
        if step + 1 < 2 * ny:
            copy(step + 1, (step + 1) % 2).start()
        copy(step, step % 2).wait()
        body(step // ny, step % ny, buf.at[step % 2])


def wide_teacher_kernel(ny, crops, idx, own, other, protos, expo_d, expo_i, w, wbuf, out, osem, buf, sem, wsem):
    half = buf.shape[1]
    rest = half - crops
    fetch = pltpu.make_async_copy(part_source(idx, ny, protos), wbuf, wsem)
    fetch.start()
    fetch.wait()
    w[...] = unit_cols(wbuf[...])[0].astype(BF16)
    leaving = []

    def body(side, y, ref):
        place = 2 * y + jnp.where(idx[0] == side, 0, 1)
        slot = len(leaving) % 2
        if len(leaving) >= 2:
            for copy in leaving[-2]:
                copy.wait()
        feats = ref[...].astype(BF16)
        for start in range(0, half, 128):
            score = jnp.dot(feats[start : start + 128, :], w[...], preferred_element_type=F32)
            e = jnp.exp2(score * (LOG2E / TEACHER_TEMP)).astype(BF16)
            out[slot, start : start + 128, :] = e
        at_d = pl.multiple_of(place * crops, 128)
        at_i = pl.multiple_of(place * rest, 128)
        copies = (
            pltpu.make_async_copy(
                out.at[slot, pl.ds(0, crops), :], expo_d.at[pl.ds(at_d, crops), :], osem.at[slot, 0]
            ),
            pltpu.make_async_copy(
                out.at[slot, pl.ds(crops, rest), :], expo_i.at[pl.ds(at_i, rest), :], osem.at[slot, 1]
            ),
        )
        for copy in copies:
            copy.start()
        leaving.append(copies)

    stream_rows(ny, 0, half, own, other, buf, sem, body)
    for copies in leaving[-2:]:
        for copy in copies:
            copy.wait()


def wide_teacher_pass(idx, own, other, protos, crops):
    ny, rows, width = own.shape
    half = rows // 2
    part = protos.shape[1] // 2 // ny
    return call(
        functools.partial(wide_teacher_kernel, ny, crops),
        [array((2 * ny * crops, part), BF16), array((2 * ny * (half - crops), part), BF16)],
        [idx, own, other, protos],
        "shhh",
        "hh",
        scratch=[
            pltpu.VMEM((width, part), BF16),
            pltpu.VMEM((width, part), BF16),
            pltpu.VMEM((2, half, part), BF16),
            pltpu.SemaphoreType.DMA((2, 2)),
            pltpu.VMEM((2, half, width), F32),
            pltpu.SemaphoreType.DMA((2,)),
            pltpu.SemaphoreType.DMA,
        ],
        flops=2 * 2 * ny * half * width * part,
        traffic=8 * ny * half * width,
    )


def wide_student_kernel(ny, crops, idx, own, other, protos, *refs):
    totals = refs[:ny]
    out, wnorm_out, turned_d, turned_i, w, wbuf, scale, left, expo, buf, sem, wsem = refs[ny:]
    half = buf.shape[1]
    rest = half - crops
    sub = totals[0].shape[0]
    fetch = pltpu.make_async_copy(part_source(idx, ny, protos), wbuf, wsem)
    fetch.start()
    for s in range(ny):
        y = lax.rem(idx[3] + ny - s, ny)
        scale[pl.ds(pl.multiple_of(y * sub, sub), sub), :] = GRAD_SCALE / totals[s][...]
    fetch.wait()
    wnorm_out[...] = unit_cols(wbuf[...])[0]
    w[...] = wnorm_out[...].astype(BF16)
    out[...] = jnp.zeros_like(out)

    def body(side, y, ref):
        core = jnp.where(idx[0] == side, 0, 1)
        place = 2 * y + core
        feats = ref[...].astype(BF16)
        turned = jnp.transpose(feats.astype(F32))
        turned_d[:, pl.ds(pl.multiple_of(place * crops, 128), crops)] = turned[:, :crops].astype(BF16)
        turned_i[:, pl.ds(pl.multiple_of(place * rest, 128), rest)] = turned[:, crops:].astype(BF16)
        lines = [scale[pl.ds(y * sub + core * (crops // 128) + t, 1), :] for t in range(crops // 128)]
        first = y * sub + 2 * crops // 128 + core * (rest // 128)
        lines += [scale[pl.ds(first + t, 1), :] for t in range(rest // 128)]
        left[...] = (turned * jnp.concatenate(lines, axis=1)).astype(BF16)
        for start in range(0, half, 128):
            score = jnp.dot(feats[start : start + 128, :], w[...], preferred_element_type=F32)
            expo[start : start + 128, :] = jnp.exp2(score * (LOG2E / STUDENT_TEMP)).astype(BF16)
        out[...] += jnp.dot(left[...], expo[...], preferred_element_type=F32)

    stream_rows(ny, half, half, own, other, buf, sem, body)


def wide_student_pass(idx, own, other, protos, totals, crops):
    ny, rows, width = own.shape
    half = rows // 2
    part = protos.shape[1] // 2 // ny
    return call(
        functools.partial(wide_student_kernel, ny, crops),
        [
            array((width, part)),
            array((width, part)),
            array((width, 2 * ny * crops), BF16),
            array((width, 2 * ny * (half - crops)), BF16),
        ],
        [idx, own, other, protos, *totals],
        "shhh" + "v" * ny,
        scratch=[
            pltpu.VMEM((width, part), BF16),
            pltpu.VMEM((width, part), BF16),
            pltpu.VMEM((ny * rows // 128, 128), F32),
            pltpu.VMEM((width, half), BF16),
            pltpu.VMEM((half, part), BF16),
            pltpu.VMEM((2, half, width), F32),
            pltpu.SemaphoreType.DMA((2,)),
            pltpu.SemaphoreType.DMA,
        ],
        flops=4 * 2 * ny * half * width * part,
        traffic=8 * ny * half * width,
    )


def weight_kernel(ny, crops, idx, prob, wnorm, turned_d, turned_i, expo_d, expo_i, colparts, rowparts, out, left_d, left_i, scales, rowscale, buf_d, buf_i, sems_d, sems_i):
    copies, _, _ = out.shape
    width, part = prob.shape
    own = width // copies
    copies_d = column_copies(expo_d, buf_d, sems_d)
    copies_i = column_copies(expo_i, buf_i, sems_i)
    for pair in zip(copies_d, copies_i):
        for copy in pair:
            copy.start()
    group = rowparts.shape[0] // ny
    sub = rowparts.shape[1]
    scales[...] = GRAD_SCALE / jnp.sum(colparts[...], axis=0)
    for y in range(ny):
        rowscale[y * sub : (y + 1) * sub, :] = 1.0 / jnp.sum(
            rowparts[y * group : (y + 1) * group], axis=0
        )
    cd = crops // 128
    ci = sub // 2 - cd
    lines_d, lines_i = [], []
    for y in range(ny):
        for core in range(2):
            for t in range(cd):
                at = y * sub + core * cd + t
                lines_d.append(rowscale[at : at + 1, :])
            for t in range(ci):
                at = y * sub + 2 * cd + core * ci + t
                lines_i.append(rowscale[at : at + 1, :])
    left_d[...] = (turned_d[...].astype(F32) * jnp.concatenate(lines_d, axis=1)).astype(BF16)
    left_i[...] = (turned_i[...].astype(F32) * jnp.concatenate(lines_i, axis=1)).astype(BF16)
    per_head = scales.shape[0] // 2
    first = idx[3] * (part // 128)
    for at in range(0, part, BN):
        span = slice(at, at + BN)
        wsum = prob[:, span]
        copies_d[at // BN].wait()
        copies_i[at // BN].wait()
        for head, (left, expo) in enumerate(((left_d, buf_d), (left_i, buf_i))):
            target = jnp.dot(left[...], expo[:, span], preferred_element_type=F32)
            base = head * per_head + first + at // 128
            line = [scales[pl.ds(base + t, 1), :] for t in range(BN // 128)]
            wsum = wsum - target * jnp.concatenate(line, axis=1)
        coldot = jnp.sum(wnorm[:, span] * wsum, axis=0, keepdims=True)
        for t in range(BN // 128):
            lanes = slice(128 * t, 128 * (t + 1))
            row = at // 128 + t
            for d in range(copies):
                out[d, row * own : (row + 1) * own, :] = wsum[d * own : (d + 1) * own, lanes]
            tail = part // 128 * own + row
            out[:, tail : tail + 1, :] = jnp.broadcast_to(
                coldot[:, lanes][None], (copies, 1, 128)
            )


def weight_pass(idx, prob, wnorm, turned, expo, colparts, rowparts, crops, ny, copies):
    width, part = prob.shape
    lines = part // 128 * (width // copies + 1)
    rows = turned[0].shape[1] + turned[1].shape[1]
    return call(
        functools.partial(weight_kernel, ny, crops),
        array((copies, lines, 128)),
        [idx, prob, wnorm, *turned, *expo, colparts, rowparts],
        "svvvvhhvv",
        scratch=[
            pltpu.VMEM(turned[0].shape, BF16),
            pltpu.VMEM(turned[1].shape, BF16),
            pltpu.VMEM(colparts.shape[1:], F32),
            pltpu.VMEM((ny * rowparts.shape[1], 128), F32),
            pltpu.VMEM(expo[0].shape, BF16),
            pltpu.VMEM(expo[1].shape, BF16),
            pltpu.SemaphoreType.DMA((part // BN,)),
            pltpu.SemaphoreType.DMA((part // BN,)),
        ],
        flops=2 * rows * width * part,
        traffic=2 * rows * part,
    )


def norm_kernel(protos, out):
    out[...] = unit_cols(protos[...])[1]


def norm_pass(protos):
    width, columns = protos.shape
    step = columns // 8
    return pl.pallas_call(
        norm_kernel,
        grid=(8,),
        in_specs=[pl.BlockSpec((width, step), lambda j: (0, j))],
        out_specs=pl.BlockSpec((1, step), lambda j: (0, j)),
        out_shape=array((1, columns)),
        compiler_params=pltpu.CompilerParams(vmem_limit_bytes=VMEM_LIMIT),
        cost_estimate=pl.CostEstimate(
            flops=3 * width * columns, bytes_accessed=2 * width * columns, transcendentals=0
        ),
    )(protos)


def proto_kernel(nx, ny, idx, parts, protos, winv, out, rows, sem):
    own, columns = out.shape
    copies = parts.shape[0]
    part = columns // (2 * ny)
    tail = part // 128 * own
    at = pl.multiple_of(idx[2] * (2 * own), 2 * own)
    fetch = pltpu.make_async_copy(protos.at[pl.ds(at, 2 * own), :], rows, sem)
    fetch.start()
    fetch.wait()
    for y in range(ny):
        for core in range(2):
            for t in range(part // 128):
                first = core * (columns // 2) + y * part + 128 * t
                lanes = slice(first, first + 128)
                wsum = jnp.zeros((own, 128), F32)
                coldot = jnp.zeros((1, 128), F32)
                for x in range(nx):
                    source = (x * ny + y) * 2 + core
                    wsum = wsum + parts[source, t * own : (t + 1) * own, :]
                    coldot = coldot + parts[source, tail + t : tail + t + 1, :]
                inv = winv[:, lanes]
                both = rows[:, lanes].astype(F32)
                wnorm = jnp.where(idx[0] == 0, both[:own, :], both[own:, :]) * inv
                out[:, lanes] = (wsum - wnorm * coldot) * inv


def proto_pass(idx, parts, protos, winv, nx, ny):
    width, columns = protos.shape
    own = width // parts.shape[0]
    return call(
        functools.partial(proto_kernel, nx, ny),
        array((own, columns)),
        [idx, parts, protos, winv],
        "svhv",
        scratch=[pltpu.VMEM((2 * own, columns), BF16), pltpu.SemaphoreType.DMA],
    )


def spread_row(line):
    return jnp.transpose(jnp.broadcast_to(line, (128, 128)))


def scaled_kernel(crops, idx, mix, totals, mine, theirs, buf):
    rows, width = mix.shape
    prob = GRAD_SCALE / totals[...]
    for t in range(rows // 128):
        span = slice(128 * t, 128 * (t + 1))
        p = jnp.concatenate([spread_row(prob[t : t + 1, :])] * (width // 128), axis=1)
        buf[span, :] = mix[span, :] * p
    part_rows(crops, idx, buf, mine, theirs)


def part_rows(crops, idx, buf, mine, theirs):
    rest = mine.shape[0] - crops
    for side, ref in ((idx[0], mine), (1 - idx[0], theirs)):
        ref[:crops, :] = buf[pl.ds(pl.multiple_of(side * crops, crops), crops), :]
        ref[crops:, :] = buf[pl.ds(pl.multiple_of(2 * crops + side * rest, 128), rest), :]


def part_pass(idx, mix, totals, crops):
    rows, width = mix.shape
    return call(
        functools.partial(scaled_kernel, crops),
        [array((rows // 2, width)), array((rows // 2, width))],
        [idx, mix, totals],
        "svv",
        scratch=[pltpu.VMEM((rows, width), F32)],
    )


def pack_rows(nz, crops, mine, came, out):
    half = mine.shape[0]
    chunk = half // nz
    share = crops // nz
    rest = chunk - share
    for z in range(nz):
        for src, dst, size in ((z * share, z * chunk, share), (crops + z * rest, z * chunk + share, rest)):
            out[dst : dst + size, :] = mine[src : src + size, :] + came[src : src + size, :]


def halve(idx, bit, total, keep, send):
    size = total.shape[0] // 2
    side = lax.rem(idx[1] // bit, 2)
    keep[...] = total[pl.ds(pl.multiple_of(side * size, 64), size), :]
    send[...] = total[pl.ds(pl.multiple_of((1 - side) * size, 64), size), :]


def pack_half_kernel(nz, crops, idx, mine, came, keep, send, total):
    pack_rows(nz, crops, mine, came, total)
    halve(idx, nz // 2, total, keep, send)


def pack_half_pass(idx, mine, came, nz, crops):
    rows, width = mine.shape
    return call(
        functools.partial(pack_half_kernel, nz, crops),
        [array((rows // 2, width)), array((rows // 2, width))],
        [idx, mine, came],
        "svv",
        scratch=[pltpu.VMEM((rows, width), F32)],
    )


def fold_kernel(bit, idx, mine, came, keep, send, total):
    total[...] = mine[...] + came[...]
    halve(idx, bit, total, keep, send)


def fold_pass(idx, mine, came, bit):
    rows, width = mine.shape
    return call(
        functools.partial(fold_kernel, bit),
        [array((rows // 2, width)), array((rows // 2, width))],
        [idx, mine, came],
        "svv",
        scratch=[pltpu.VMEM((rows, width), F32)],
    )


def add_kernel(mine, came, out):
    out[...] = mine[...] + came[...]


def add_pass(mine, came):
    return call(add_kernel, array(mine.shape), [mine, came], "vv")


def mix_kernel(nz, ny, crops, bit, idx, rowparts, target, target_came, prob, prob_came, *refs):
    scale = refs[-1]
    total = refs[-2]
    sub = rowparts.shape[1]
    group = rowparts.shape[0] // ny
    cd = crops // 128
    ci = sub // 2 - cd
    row = GRAD_SCALE / jnp.sum(rowparts[pl.ds(idx[3] * group, group), :, :], axis=0)
    low = idx[0] == 0
    for t in range(cd + ci):
        a, b = (t, cd + t) if t < cd else (cd + t, cd + ci + t)
        line = jnp.where(low, row[a : a + 1, :], row[b : b + 1, :])
        scale[128 * t : 128 * (t + 1), :] = spread_row(line)
    rows, width = target.shape
    here = nz // 2
    chunk = rows // here
    share = crops // nz
    rest = chunk - share
    first = idx[1] // here * here
    for k in range(here):
        z = first + k
        for at, src, size in ((0, z * share, share), (share, crops + z * rest, rest)):
            r = scale[pl.ds(pl.multiple_of(src, 16), size), :]
            span = slice(k * chunk + at, k * chunk + at + size)
            value = target[span, :] + target_came[span, :]
            total[span, :] = (
                prob[span, :]
                + prob_came[span, :]
                - value * jnp.concatenate([r] * (width // 128), axis=1)
            )
    if bit:
        halve(idx, bit, total, refs[0], refs[1])


def mix_pass(idx, rowparts, target, target_came, prob, prob_came, nz, ny, crops, bit):
    rows, width = target.shape
    half = rowparts.shape[1] // 2 * 128
    shapes = [array((rows // 2, width))] * 2 if bit else array((rows, width))
    return call(
        functools.partial(mix_kernel, nz, ny, crops, bit),
        shapes,
        [idx, rowparts, target, target_came, prob, prob_came],
        "svvvvv",
        scratch=([pltpu.VMEM((rows, width), F32)] if bit else []) + [pltpu.VMEM((half, 128), F32)],
    )


def feature_kernel(pair, patches, idx, mask, *refs):
    pieces = refs[: 2 if pair else 1]
    all_crops, all_rows, crop_out, patch_out, masked_rows, dense, total = refs[len(pieces) :]
    z = idx[1]
    masked = mask.shape[1]
    crop_share = crop_out.shape[0]
    share = patch_out.shape[0]
    total[...] = pieces[0][...] + pieces[1][...] if pair else pieces[0][...]
    chunk = total.shape[0] // len(pieces)
    rest = chunk - crop_share
    for side in range(len(pieces)):
        masked_rows[side * rest : (side + 1) * rest, :] = total[
            side * chunk + crop_share : (side + 1) * chunk, :
        ]
    crop_at = pl.multiple_of(z * crop_share, 16)
    patch_at = pl.multiple_of(z * share, 128)
    start = pl.multiple_of(lax.rem(z, len(pieces)) * chunk, 16)
    dense[...] = jnp.zeros_like(dense)
    first_row = z * share
    first_image = first_row // patches
    offset = first_row - first_image * patches
    for image in range(masked_rows.shape[0] // masked):

        def put(m, _):
            at = mask[first_image + image, m] + image * patches - offset

            @pl.when(jnp.logical_and(at >= 0, at < share))
            def _():
                dense[pl.ds(at, 1), :] = masked_rows[pl.ds(image * masked + m, 1), :]

            return 0

        lax.fori_loop(0, masked, put, 0, unroll=4)

    def back(x, d):
        xf = x.astype(F32)
        inv = lax.rsqrt(jnp.sum(xf * xf, axis=-1, keepdims=True) + EPS)
        u = xf * inv
        return (d - u * jnp.sum(u * d, axis=-1, keepdims=True)) * inv

    crop_out[...] = back(all_crops[pl.ds(crop_at, crop_share), :], total[pl.ds(start, crop_share), :])
    patch_out[...] = back(all_rows[pl.ds(patch_at, share), :], dense[...])


def feature_pass(idx, mask, pieces, all_crops, all_rows, nz, patches):
    crops, width = all_crops.shape
    crop_share = crops // nz
    share = all_rows.shape[0] // nz
    rows = pieces[0].shape[0]
    return call(
        functools.partial(feature_kernel, len(pieces) == 2, patches),
        [array((crop_share, width)), array((share, width))],
        [idx, mask, *pieces, all_crops, all_rows],
        "ss" + "v" * len(pieces) + "vv",
        scratch=[
            pltpu.VMEM((rows - len(pieces) * crop_share, width), F32),
            pltpu.VMEM((share, width), F32),
            pltpu.VMEM((rows, width), F32),
        ],
    )


def tie(*values):
    return lax.optimization_barrier(values)


def shifted(n, s):
    return [(i, (i + s) % n) for i in range(n)]


def local(
    sizes,
    student_crops,
    teacher_crops,
    student_patches,
    teacher_patches,
    patch_mask,
    student_protos,
    teacher_protos,
):
    nx, ny, nz = sizes
    images, masked = patch_mask.shape
    patches = student_patches.shape[0] // images
    crops = student_crops.shape[0]
    ix, iy, ic, iz = (lax.axis_index(a) for a in ("x", "y", "c", "z"))
    idx = jnp.stack([ic, iz, ix * ny + iy, iy]).astype(jnp.int32)
    swap = [(0, 1), (1, 0)]

    own = prep(teacher_crops, teacher_patches, student_crops, student_patches, patch_mask)
    other = lax.ppermute(own, "c", swap)
    all_own = lax.all_gather(own, "y")
    expo, sums = teacher_pass(idx, own, other, teacher_protos, crops, nx * ny)
    sub = 2 * (crops + images * masked) // 128

    pair = student_patches.shape[0] // nz < patches

    def across(value, bit):
        return lax.ppermute(value, "z", [(i, i ^ bit) for i in range(nz)])

    colparts = lax.all_to_all(sums, ("x", "y"), 0, 0)
    total, mix = student_pass(idx, own, other, student_protos, crops)
    winv = norm_pass(student_protos)
    colparts, winv = tie(colparts, winv)
    sums = row_pass(expo, colparts, total, crops, 2 * nz)
    rowparts = lax.all_to_all(sums, ("c", "z"), 0, 0)
    totals = jnp.sum(rowparts[:, sub:, :], axis=0)
    sums = column_pass(expo, rowparts, crops, nx * ny)

    colparts = lax.all_to_all(sums, ("x", "y"), 0, 0)
    totals, _ = tie(totals, sums)
    all_totals = [totals] + [lax.ppermute(totals, "y", shifted(ny, s)) for s in range(1, ny)]
    mine, theirs = part_pass(idx, mix, totals, crops)
    p_keep, p_send = pack_half_pass(idx, mine, lax.ppermute(theirs, "c", swap), nz, crops)
    colparts, p_send, *all_totals = tie(colparts, p_send, *all_totals)
    p_came = across(p_send, nz // 2)
    sums = row_pass(expo, colparts, None, crops, 2 * nz)
    all_own, sums = tie(all_own, sums)
    all_other = lax.ppermute(all_own, "c", swap)
    rowparts = lax.all_to_all(sums, ("c", "z"), 0, 0)
    sums = column_pass(expo, rowparts, crops, nx * ny)

    colparts = lax.all_to_all(sums, ("x", "y"), 0, 0)
    all_own, all_other, _ = tie(all_own, all_other, sums)
    wide_expo = wide_teacher_pass(idx, all_own, all_other, teacher_protos, crops)
    colparts, p_came, *wide_expo = tie(colparts, p_came, *wide_expo)
    target_mine, target_theirs = target_pass(idx, expo, colparts, student_protos, crops)
    colparts, target_theirs = tie(colparts, target_theirs)
    sums = row_pass(expo, colparts, None, crops, 2 * nz * ny)
    target_came = lax.ppermute(target_theirs, "c", swap)
    keep, send = pack_half_pass(idx, target_mine, target_came, nz, crops)
    sums, send = tie(sums, send)
    rowparts = lax.all_to_all(sums, ("y", "c", "z"), 0, 0)
    came = across(send, nz // 2)
    all_own, all_other, _ = tie(all_own, all_other, sums)
    prob, wnorm, *turned = wide_student_pass(
        idx, all_own, all_other, student_protos, all_totals, crops
    )
    prob, came = tie(prob, came)
    outgoing = weight_pass(
        idx, prob, wnorm, turned, wide_expo, colparts, rowparts, crops, ny, nx * ny * 2
    )
    parts = lax.all_to_all(outgoing, ("x", "y", "c"), 0, 0)
    proto_grad = proto_pass(idx, parts, student_protos, winv, nx, ny)
    bits = [nz >> k for k in range(2, nz.bit_length()) if nz >> k > (1 if pair else 0)]
    total = mix_pass(
        idx, rowparts, keep, came, p_keep, p_came, nz, ny, crops, bits[0] if bits else 0
    )
    for i, bit in enumerate(bits):
        keep, send = total
        came = across(send, bit)
        if i + 1 < len(bits):
            total = fold_pass(idx, keep, came, bits[i + 1])
        else:
            total = add_pass(keep, came)
    pieces = [total]
    if pair:
        pieces.append(across(total, 1))
    crop_grad, patch_grad = feature_pass(
        idx, patch_mask, pieces, student_crops, student_patches, nz, patches
    )
    return (proto_grad, crop_grad, patch_grad)


def solution(mesh):
    dp, nz = mesh.devices.shape
    nx = 4 if dp == 32 else 2
    ny = dp // (2 * nx)
    grid = Mesh(mesh.devices.reshape(nx, ny, 2, nz), ("x", "y", "c", "z"))
    rows = ("x", "y", "c")
    in_specs = (
        P(rows, None),
        P(rows, None),
        P(rows, None),
        P(rows, None),
        P(rows, None),
        P(None, "z"),
        P(None, "z"),
    )
    out_specs = (P(rows, "z"), P(rows + ("z",), None), P(rows + ("z",), None))
    return jax.shard_map(
        functools.partial(local, (nx, ny, nz)),
        mesh=grid,
        in_specs=in_specs,
        out_specs=out_specs,
        check_vma=False,
    )
```

```python
import functools

import jax
import jax.numpy as jnp
from jax import lax
from jax.experimental import pallas as pl
from jax.experimental.pallas import tpu as pltpu
from jax.sharding import Mesh, PartitionSpec as P

ITERS = 3
EPS = 1e-06
TEACHER_TEMP = 0.07
STUDENT_TEMP = 0.1
LOSS_SCALE = 256.0
GRAD_SCALE = LOSS_SCALE / STUDENT_TEMP
LOG2E = 1.4426950408889634

BN = 512
F32 = jnp.float32
BF16 = jnp.bfloat16
VMEM_LIMIT = 52 * 1024 * 1024
SMEM = pl.BlockSpec(memory_space=pltpu.SMEM)
VMEM = pl.BlockSpec(memory_space=pltpu.VMEM)
HBM = pl.BlockSpec(memory_space=pltpu.HBM)


def call(kernel, out_shape, args, specs, outs="", scratch=(), flops=0, traffic=0):
    spaces = {"s": SMEM, "v": VMEM, "h": HBM}
    if not isinstance(out_shape, list):
        out_specs = VMEM
    else:
        out_specs = [spaces[letter] for letter in outs or "v" * len(out_shape)]
    return pl.pallas_call(
        kernel,
        out_shape=out_shape,
        out_specs=out_specs,
        in_specs=[spaces[letter] for letter in specs],
        scratch_shapes=list(scratch),
        compiler_params=pltpu.CompilerParams(vmem_limit_bytes=VMEM_LIMIT),
        cost_estimate=pl.CostEstimate(flops=flops, bytes_accessed=traffic, transcendentals=0),
    )(*args)


def array(shape, dtype=F32):
    return jax.ShapeDtypeStruct(shape, dtype)


def stream(source, buf, sem, steps, body):
    def copy(j, slot):
        return pltpu.make_async_copy(source(j), buf.at[slot], sem.at[slot])

    copy(0, 0).start()

    def step(j, _):
        slot = lax.rem(j, 2)

        @pl.when(j + 1 < steps)
        def _():
            copy(j + 1, 1 - slot).start()

        copy(j, slot).wait()
        body(j, buf.at[slot])
        return 0

    lax.fori_loop(0, steps, step, 0)


def unit(x):
    xf = x.astype(F32)
    return xf * lax.rsqrt(jnp.sum(xf * xf, axis=-1, keepdims=True) + EPS)


def unit_cols(w):
    wf = w.astype(F32)
    inv = lax.rsqrt(jnp.sum(wf * wf, axis=0, keepdims=True) + EPS)
    return wf * inv, inv


def prep_kernel(tcrops, tpatch, scrops, spatch, mask, out, tc, tp, sc, sp, sem):
    images, masked = mask.shape
    patches = tp.shape[0] // images
    count = tc.shape[0]
    half = out.shape[0] // 2
    copies = [
        pltpu.make_async_copy(src, dst, sem.at[i])
        for i, (src, dst) in enumerate(((tcrops, tc), (tpatch, tp), (scrops, sc), (spatch, sp)))
    ]
    for copy in copies:
        copy.start()
    for side, (crops, patch_rows) in enumerate(((tc, tp), (sc, sp))):
        copies[2 * side].wait()
        copies[2 * side + 1].wait()
        base = side * half
        out[base : base + count, :] = unit(crops[...])
        for i in range(images):
            place = lax.broadcasted_iota(jnp.int32, (patches, masked), 0)
            chosen = (place == mask[i : i + 1, :]).astype(F32).astype(BF16)
            rows = lax.dot_general(
                chosen,
                patch_rows[i * patches : (i + 1) * patches, :],
                (((0,), (0,)), ((), ())),
                preferred_element_type=F32,
            )
            at = base + count + i * masked
            out[at : at + masked, :] = unit(rows)


def prep(tcrops, tpatch, scrops, spatch, mask):
    half = tcrops.shape[0] + mask.size
    return call(
        prep_kernel,
        array((2 * half, tcrops.shape[1])),
        [tcrops, tpatch, scrops, spatch, mask],
        "hhhhv",
        scratch=[pltpu.VMEM(a.shape, BF16) for a in (tcrops, tpatch, scrops, spatch)]
        + [pltpu.SemaphoreType.DMA((4,))],
    )


def place_rows(core, crops, base, half, own, other, dest):
    rest = half - crops
    for side, ref in ((core, own), (1 - core, other)):
        at = pl.multiple_of(side * crops, crops)
        dest[pl.ds(at, crops), :] = ref[base : base + crops, :].astype(dest.dtype)
        at = pl.multiple_of(2 * crops + side * rest, 128)
        dest[pl.ds(at, rest), :] = ref[base + crops : base + half, :].astype(dest.dtype)


def row_blocks(start, stop):
    return [(a, min(a + 256, stop)) for a in range(start, stop, 256)]


def proto_source(core, protos, size=BN):
    columns = protos.shape[1] // 2
    return lambda j: protos.at[:, pl.ds(pl.multiple_of(core * columns + j * size, size), size)]


def proto_scratch(width, size=BN):
    return [pltpu.VMEM((2, width, size), BF16), pltpu.SemaphoreType.DMA((2,))]


def put_columns(step, heads, out):
    copies = out.shape[0]
    per_head = out.shape[1] // 2
    for head in range(2):
        for t in range(BN // 128):
            piece = heads[head][:, 128 * t : 128 * (t + 1)]
            out[:, pl.ds(head * per_head + step * (BN // 128) + t, 1), :] = jnp.broadcast_to(
                piece[None], (copies, 1, 128)
            )


def get_columns(step, head, lines):
    base = head * (lines.shape[0] // 2) + step * (BN // 128)
    return jnp.concatenate([lines[pl.ds(base + t, 1), :] for t in range(BN // 128)], axis=1)


def line_up(values):
    return jnp.concatenate([values[t : t + 1, :] for t in range(values.shape[0])], axis=1)


def teacher_kernel(crops, idx, own, other, protos, expo, sums, feats, out, osem, buf, sem):
    rows, columns = expo.shape
    place_rows(idx[0], crops, 0, rows // 2, own, other, feats)
    steps = columns // BN

    def leave(j, slot):
        at = pl.multiple_of(j * BN, BN)
        return pltpu.make_async_copy(out.at[slot], expo.at[:, pl.ds(at, BN)], osem.at[slot])

    def step(j, block):
        w = unit_cols(block[...])[0].astype(BF16)
        slot = lax.rem(j, 2)

        @pl.when(j >= 2)
        def _():
            leave(j - 2, slot).wait()

        heads = []
        for first, last in ((0, 2 * crops), (2 * crops, rows)):
            part = jnp.zeros((1, BN), F32)
            for start, stop in row_blocks(first, last):
                score = jnp.dot(feats[start:stop, :], w, preferred_element_type=F32)
                e = jnp.exp2(score * (LOG2E / TEACHER_TEMP))
                out[slot, start:stop, :] = e.astype(BF16)
                part = part + jnp.sum(e, axis=0, keepdims=True)
            heads.append(part)
        leave(j, slot).start()
        put_columns(j, heads, sums)

    stream(proto_source(idx[0], protos), buf, sem, steps, step)
    for j in (steps - 2, steps - 1):
        leave(j, j % 2).wait()


def teacher_pass(idx, own, other, protos, crops, copies):
    rows, width = own.shape
    columns = protos.shape[1] // 2
    return call(
        functools.partial(teacher_kernel, crops),
        [array((rows, columns), BF16), array((copies, 2 * columns // 128, 128))],
        [idx, own, other, protos],
        "svvh",
        "hv",
        scratch=[
            pltpu.VMEM((rows, width), BF16),
            pltpu.VMEM((2, rows, BN), BF16),
            pltpu.SemaphoreType.DMA((2,)),
        ]
        + proto_scratch(width),
        flops=2 * rows * width * columns,
        traffic=2 * rows * columns,
    )


def student_kernel(crops, idx, own, other, protos, total, mix, feats, acc, buf, sem):
    rows = feats.shape[0]
    size = buf.shape[2]
    place_rows(idx[0], crops, rows // 2, rows // 2, own, other, feats)
    acc[...] = jnp.zeros_like(acc)
    mix[...] = jnp.zeros_like(mix)

    def step(j, block):
        w = unit_cols(block[...])[0].astype(BF16)
        for start, stop in row_blocks(0, rows):
            score = jnp.dot(feats[start:stop, :], w, preferred_element_type=F32)
            p = jnp.exp2(score * (LOG2E / STUDENT_TEMP))
            part = p[:, :128]
            for t in range(1, size // 128):
                part = part + p[:, 128 * t : 128 * (t + 1)]
            acc[start:stop, :] += part
            mix[start:stop, :] += lax.dot_general(
                p.astype(BF16), w, (((1,), (1,)), ((), ())), preferred_element_type=F32
            )

    stream(proto_source(idx[0], protos, size), buf, sem, protos.shape[1] // 2 // size, step)
    for t in range(rows // 128):
        block = jnp.transpose(acc[128 * t : 128 * (t + 1), :])
        total[t : t + 1, :] = jnp.sum(block, axis=0, keepdims=True)


def student_pass(idx, own, other, protos, crops):
    rows, width = own.shape
    columns = protos.shape[1] // 2
    return call(
        functools.partial(student_kernel, crops),
        [array((rows // 128, 128)), array((rows, width))],
        [idx, own, other, protos],
        "svvh",
        scratch=[pltpu.VMEM((rows, width), BF16), pltpu.VMEM((rows, 128), F32)]
        + proto_scratch(width, 2 * BN),
        flops=4 * rows * width * columns,
        traffic=2 * width * columns,
    )


def row_copies(source, dest, sems):
    return [
        pltpu.make_async_copy(
            source.at[pl.ds(128 * i, 128), :], dest.at[pl.ds(128 * i, 128), :], sems.at[i]
        )
        for i in range(source.shape[0] // 128)
    ]


def column_copies(source, dest, sems):
    return [
        pltpu.make_async_copy(
            source.at[:, pl.ds(BN * j, BN)], dest.at[:, pl.ds(BN * j, BN)], sems.at[j]
        )
        for j in range(source.shape[1] // BN)
    ]


def expo_scratch(expo, blocks):
    return [pltpu.VMEM(expo.shape, BF16), pltpu.SemaphoreType.DMA((blocks,))]


def sum_rows(crops, expo, copies_in, colscale, out):
    copies = out.shape[0]
    rows, columns = expo.shape
    per_head = columns // 128

    for i in range(rows // 128):
        copies_in[i].wait()
        head = 0 if i < 2 * crops // 128 else 1
        at = 128 * i

        def chunk(k, acc):
            e = expo[pl.ds(at, 128), pl.ds(pl.multiple_of(k * 128, 128), 128)].astype(F32)
            return acc + e * colscale[pl.ds(head * per_head + k, 1), :]

        acc = lax.fori_loop(0, per_head, chunk, jnp.zeros((128, 128), F32), unroll=8)
        sums = jnp.sum(jnp.transpose(acc), axis=0, keepdims=True)
        out[:, i : i + 1, :] = jnp.broadcast_to(sums[None], (copies, 1, 128))


def row_kernel(crops, extra, expo, colparts, *refs):
    out, colscale, buf, sems = refs[-4:]
    copies_in = row_copies(expo, buf, sems)
    for copy in copies_in:
        copy.start()
    if extra:
        total = refs[0]
        count = total.shape[0]
        out[:, count:, :] = jnp.broadcast_to(total[...][None], (out.shape[0], count, 128))
    colscale[...] = 1.0 / jnp.sum(colparts[...], axis=0)
    sum_rows(crops, buf, copies_in, colscale, out)


def row_pass(expo, colparts, total, crops, copies):
    rows, columns = expo.shape
    extra = total is not None
    return call(
        functools.partial(row_kernel, crops, extra),
        array((copies, rows // 128 * (2 if extra else 1), 128)),
        [expo, colparts] + ([total] if extra else []),
        "hvv" if extra else "hv",
        scratch=[pltpu.VMEM((2 * columns // 128, 128), F32)] + expo_scratch(expo, rows // 128),
        flops=2 * rows * columns,
        traffic=2 * rows * columns,
    )


def target_kernel(crops, idx, expo, colparts, protos, mine, theirs, target, colscale, ebuf, esem, buf, sem):
    rows, columns = expo.shape
    steps = columns // BN
    copies_in = column_copies(expo, ebuf, esem)
    for copy in copies_in:
        copy.start()
    colscale[...] = 1.0 / jnp.sum(colparts[...], axis=0)
    target[...] = jnp.zeros_like(target)

    def step(j, block):
        wnorm = unit_cols(block[...])[0]
        at = pl.multiple_of(j * BN, BN)
        pltpu.make_async_copy(
            expo.at[:, pl.ds(at, BN)], ebuf.at[:, pl.ds(at, BN)], esem.at[j]
        ).wait()
        for head, (first, last) in enumerate(((0, 2 * crops), (2 * crops, rows))):
            w = (wnorm * get_columns(j, head, colscale)).astype(BF16)
            target[first:last, :] += lax.dot_general(
                ebuf[first:last, pl.ds(at, BN)],
                w,
                (((1,), (1,)), ((), ())),
                preferred_element_type=F32,
            )

    stream(proto_source(idx[0], protos), buf, sem, steps, step)
    part_rows(crops, idx, target, mine, theirs)


def target_pass(idx, expo, colparts, protos, crops):
    rows, columns = expo.shape
    width = protos.shape[0]
    return call(
        functools.partial(target_kernel, crops),
        [array((rows // 2, width)), array((rows // 2, width))],
        [idx, expo, colparts, protos],
        "shvh",
        scratch=[pltpu.VMEM((rows, width), F32), pltpu.VMEM((2 * columns // 128, 128), F32)]
        + expo_scratch(expo, columns // BN)
        + proto_scratch(width),
        flops=2 * rows * columns * width,
        traffic=2 * rows * columns,
    )


def split3(v):
    high = v.astype(BF16)
    rest = v - high.astype(F32)
    middle = rest.astype(BF16)
    low = (rest - middle.astype(F32)).astype(BF16)
    pad = jnp.zeros((13, v.shape[1]), F32)
    parts = [high.astype(F32), middle.astype(F32), low.astype(F32), pad]
    return jnp.concatenate(parts, axis=0).astype(BF16)


def column_kernel(crops, expo, rowparts, out, buf, sems):
    rows, columns = expo.shape
    copies_in = column_copies(expo, buf, sems)
    for copy in copies_in:
        copy.start()
    scale = line_up(1.0 / jnp.sum(rowparts[:, : rows // 128, :], axis=0))
    spans = [(0, 2 * crops), (2 * crops, rows)]
    lefts = [split3(scale[:, first:last]) for first, last in spans]
    for j in range(columns // BN):
        copies_in[j].wait()
        heads = []
        for left, (first, last) in zip(lefts, spans):
            sums = jnp.dot(
                left, buf[first:last, j * BN : (j + 1) * BN], preferred_element_type=F32
            )
            heads.append(sums[0:1, :] + sums[1:2, :] + sums[2:3, :])
        put_columns(j, heads, out)


def column_pass(expo, rowparts, crops, copies):
    rows, columns = expo.shape
    return call(
        functools.partial(column_kernel, crops),
        array((copies, 2 * columns // 128, 128)),
        [expo, rowparts],
        "hv",
        scratch=expo_scratch(expo, columns // BN),
        flops=2 * rows * columns,
        traffic=2 * rows * columns,
    )


def part_source(idx, ny, protos):
    columns = protos.shape[1] // 2
    part = columns // ny
    at = pl.multiple_of(idx[0] * columns + idx[3] * part, 128)
    return protos.at[:, pl.ds(at, part)]


def stream_rows(ny, base, half, own, other, buf, sem, body):
    def copy(step, slot):
        ref = own if step < ny else other
        return pltpu.make_async_copy(
            ref.at[step % ny, pl.ds(base, half), :], buf.at[slot], sem.at[slot]
        )

    copy(0, 0).start()
    for step in range(2 * ny):
        if step + 1 < 2 * ny:
            copy(step + 1, (step + 1) % 2).start()
        copy(step, step % 2).wait()
        body(step // ny, step % ny, buf.at[step % 2])


def wide_teacher_kernel(ny, crops, idx, own, other, protos, expo_d, expo_i, w, wbuf, out, osem, buf, sem, wsem):
    half = buf.shape[1]
    rest = half - crops
    fetch = pltpu.make_async_copy(part_source(idx, ny, protos), wbuf, wsem)
    fetch.start()
    fetch.wait()
    w[...] = unit_cols(wbuf[...])[0].astype(BF16)
    leaving = []

    def body(side, y, ref):
        place = 2 * y + jnp.where(idx[0] == side, 0, 1)
        slot = len(leaving) % 2
        if len(leaving) >= 2:
            for copy in leaving[-2]:
                copy.wait()
        feats = ref[...].astype(BF16)
        for start in range(0, half, 128):
            score = jnp.dot(feats[start : start + 128, :], w[...], preferred_element_type=F32)
            e = jnp.exp2(score * (LOG2E / TEACHER_TEMP)).astype(BF16)
            out[slot, start : start + 128, :] = e
        at_d = pl.multiple_of(place * crops, 128)
        at_i = pl.multiple_of(place * rest, 128)
        copies = (
            pltpu.make_async_copy(
                out.at[slot, pl.ds(0, crops), :], expo_d.at[pl.ds(at_d, crops), :], osem.at[slot, 0]
            ),
            pltpu.make_async_copy(
                out.at[slot, pl.ds(crops, rest), :], expo_i.at[pl.ds(at_i, rest), :], osem.at[slot, 1]
            ),
        )
        for copy in copies:
            copy.start()
        leaving.append(copies)

    stream_rows(ny, 0, half, own, other, buf, sem, body)
    for copies in leaving[-2:]:
        for copy in copies:
            copy.wait()


def wide_teacher_pass(idx, own, other, protos, crops):
    ny, rows, width = own.shape
    half = rows // 2
    part = protos.shape[1] // 2 // ny
    return call(
        functools.partial(wide_teacher_kernel, ny, crops),
        [array((2 * ny * crops, part), BF16), array((2 * ny * (half - crops), part), BF16)],
        [idx, own, other, protos],
        "shhh",
        "hh",
        scratch=[
            pltpu.VMEM((width, part), BF16),
            pltpu.VMEM((width, part), BF16),
            pltpu.VMEM((2, half, part), BF16),
            pltpu.SemaphoreType.DMA((2, 2)),
            pltpu.VMEM((2, half, width), F32),
            pltpu.SemaphoreType.DMA((2,)),
            pltpu.SemaphoreType.DMA,
        ],
        flops=2 * 2 * ny * half * width * part,
        traffic=8 * ny * half * width,
    )


def wide_student_kernel(ny, crops, idx, own, other, protos, *refs):
    totals = refs[:ny]
    out, wnorm_out, turned_d, turned_i, w, wbuf, scale, left, expo, buf, sem, wsem = refs[ny:]
    half = buf.shape[1]
    rest = half - crops
    sub = totals[0].shape[0]
    fetch = pltpu.make_async_copy(part_source(idx, ny, protos), wbuf, wsem)
    fetch.start()
    for s in range(ny):
        y = lax.rem(idx[3] + ny - s, ny)
        scale[pl.ds(pl.multiple_of(y * sub, sub), sub), :] = GRAD_SCALE / totals[s][...]
    fetch.wait()
    wnorm_out[...] = unit_cols(wbuf[...])[0]
    w[...] = wnorm_out[...].astype(BF16)
    out[...] = jnp.zeros_like(out)

    def body(side, y, ref):
        core = jnp.where(idx[0] == side, 0, 1)
        place = 2 * y + core
        feats = ref[...].astype(BF16)
        turned = jnp.transpose(feats.astype(F32))
        turned_d[:, pl.ds(pl.multiple_of(place * crops, 128), crops)] = turned[:, :crops].astype(BF16)
        turned_i[:, pl.ds(pl.multiple_of(place * rest, 128), rest)] = turned[:, crops:].astype(BF16)
        lines = [scale[pl.ds(y * sub + core * (crops // 128) + t, 1), :] for t in range(crops // 128)]
        first = y * sub + 2 * crops // 128 + core * (rest // 128)
        lines += [scale[pl.ds(first + t, 1), :] for t in range(rest // 128)]
        left[...] = (turned * jnp.concatenate(lines, axis=1)).astype(BF16)
        for start in range(0, half, 128):
            score = jnp.dot(feats[start : start + 128, :], w[...], preferred_element_type=F32)
            expo[start : start + 128, :] = jnp.exp2(score * (LOG2E / STUDENT_TEMP)).astype(BF16)
        out[...] += jnp.dot(left[...], expo[...], preferred_element_type=F32)

    stream_rows(ny, half, half, own, other, buf, sem, body)


def wide_student_pass(idx, own, other, protos, totals, crops):
    ny, rows, width = own.shape
    half = rows // 2
    part = protos.shape[1] // 2 // ny
    return call(
        functools.partial(wide_student_kernel, ny, crops),
        [
            array((width, part)),
            array((width, part)),
            array((width, 2 * ny * crops), BF16),
            array((width, 2 * ny * (half - crops)), BF16),
        ],
        [idx, own, other, protos, *totals],
        "shhh" + "v" * ny,
        scratch=[
            pltpu.VMEM((width, part), BF16),
            pltpu.VMEM((width, part), BF16),
            pltpu.VMEM((ny * rows // 128, 128), F32),
            pltpu.VMEM((width, half), BF16),
            pltpu.VMEM((half, part), BF16),
            pltpu.VMEM((2, half, width), F32),
            pltpu.SemaphoreType.DMA((2,)),
            pltpu.SemaphoreType.DMA,
        ],
        flops=4 * 2 * ny * half * width * part,
        traffic=8 * ny * half * width,
    )


def weight_kernel(ny, crops, idx, prob, wnorm, turned_d, turned_i, expo_d, expo_i, colparts, rowparts, out, left_d, left_i, scales, rowscale, buf_d, buf_i, sems_d, sems_i, targets):
    copies, _, _ = out.shape
    width, part = prob.shape
    own = width // copies
    streams = []
    for expo, buf, sems in ((expo_d, buf_d, sems_d), (expo_i, buf_i, sems_i)):
        size = buf.shape[0] // sems.shape[0]
        streams.append(
            [
                pltpu.make_async_copy(
                    expo.at[pl.ds(i * size, size), :], buf.at[pl.ds(i * size, size), :], sems.at[i]
                )
                for i in range(sems.shape[0])
            ]
        )
    for copy in streams[0] + streams[1]:
        copy.start()
    group = rowparts.shape[0] // ny
    sub = rowparts.shape[1]
    scales[...] = GRAD_SCALE / jnp.sum(colparts[...], axis=0)
    for y in range(ny):
        rowscale[y * sub : (y + 1) * sub, :] = 1.0 / jnp.sum(
            rowparts[y * group : (y + 1) * group], axis=0
        )
    cd = crops // 128
    ci = sub // 2 - cd
    lines_d, lines_i = [], []
    for y in range(ny):
        for core in range(2):
            for t in range(cd):
                at = y * sub + core * cd + t
                lines_d.append(rowscale[at : at + 1, :])
            for t in range(ci):
                at = y * sub + 2 * cd + core * ci + t
                lines_i.append(rowscale[at : at + 1, :])
    left_d[...] = (turned_d[...].astype(F32) * jnp.concatenate(lines_d, axis=1)).astype(BF16)
    left_i[...] = (turned_i[...].astype(F32) * jnp.concatenate(lines_i, axis=1)).astype(BF16)
    per_head = scales.shape[0] // 2
    first = idx[3] * (part // 128)
    for head, (left, buf) in enumerate(((left_d, buf_d), (left_i, buf_i))):
        size = buf.shape[0] // len(streams[head])
        for i, copy in enumerate(streams[head]):
            copy.wait()
            span = slice(i * size, (i + 1) * size)
            value = jnp.dot(left[:, span], buf[span, :], preferred_element_type=F32)
            if i == 0:
                targets[head] = value
            else:
                targets[head] += value
    for at in range(0, part, BN):
        span = slice(at, at + BN)
        wsum = prob[:, span]
        for head in range(2):
            base = head * per_head + first + at // 128
            line = [scales[pl.ds(base + t, 1), :] for t in range(BN // 128)]
            wsum = wsum - targets[head, :, span] * jnp.concatenate(line, axis=1)
        coldot = jnp.sum(wnorm[:, span] * wsum, axis=0, keepdims=True)
        for t in range(BN // 128):
            lanes = slice(128 * t, 128 * (t + 1))
            row = at // 128 + t
            for d in range(copies):
                out[d, row * own : (row + 1) * own, :] = wsum[d * own : (d + 1) * own, lanes]
            tail = part // 128 * own + row
            out[:, tail : tail + 1, :] = jnp.broadcast_to(
                coldot[:, lanes][None], (copies, 1, 128)
            )


def weight_pass(idx, prob, wnorm, turned, expo, colparts, rowparts, crops, ny, copies):
    width, part = prob.shape
    lines = part // 128 * (width // copies + 1)
    rows = turned[0].shape[1] + turned[1].shape[1]
    return call(
        functools.partial(weight_kernel, ny, crops),
        array((copies, lines, 128)),
        [idx, prob, wnorm, *turned, *expo, colparts, rowparts],
        "svvvvhhvv",
        scratch=[
            pltpu.VMEM(turned[0].shape, BF16),
            pltpu.VMEM(turned[1].shape, BF16),
            pltpu.VMEM(colparts.shape[1:], F32),
            pltpu.VMEM((ny * rowparts.shape[1], 128), F32),
            pltpu.VMEM(expo[0].shape, BF16),
            pltpu.VMEM(expo[1].shape, BF16),
            pltpu.SemaphoreType.DMA((expo[0].shape[0] // 512,)),
            pltpu.SemaphoreType.DMA((expo[1].shape[0] // 512,)),
            pltpu.VMEM((2, width, part), F32),
        ],
        flops=2 * rows * width * part,
        traffic=2 * rows * part,
    )


def norm_kernel(protos, out):
    out[...] = unit_cols(protos[...])[1]


def norm_pass(protos):
    width, columns = protos.shape
    step = columns // 8
    return pl.pallas_call(
        norm_kernel,
        grid=(8,),
        in_specs=[pl.BlockSpec((width, step), lambda j: (0, j))],
        out_specs=pl.BlockSpec((1, step), lambda j: (0, j)),
        out_shape=array((1, columns)),
        compiler_params=pltpu.CompilerParams(vmem_limit_bytes=VMEM_LIMIT),
        cost_estimate=pl.CostEstimate(
            flops=3 * width * columns, bytes_accessed=2 * width * columns, transcendentals=0
        ),
    )(protos)


def proto_kernel(nx, ny, idx, parts, protos, winv, out, rows, sem):
    own, columns = out.shape
    copies = parts.shape[0]
    part = columns // (2 * ny)
    tail = part // 128 * own
    at = pl.multiple_of(idx[2] * (2 * own), 2 * own)
    fetch = pltpu.make_async_copy(protos.at[pl.ds(at, 2 * own), :], rows, sem)
    fetch.start()
    fetch.wait()
    for y in range(ny):
        for core in range(2):
            for t in range(part // 128):
                first = core * (columns // 2) + y * part + 128 * t
                lanes = slice(first, first + 128)
                wsum = jnp.zeros((own, 128), F32)
                coldot = jnp.zeros((1, 128), F32)
                for x in range(nx):
                    source = (x * ny + y) * 2 + core
                    wsum = wsum + parts[source, t * own : (t + 1) * own, :]
                    coldot = coldot + parts[source, tail + t : tail + t + 1, :]
                inv = winv[:, lanes]
                both = rows[:, lanes].astype(F32)
                wnorm = jnp.where(idx[0] == 0, both[:own, :], both[own:, :]) * inv
                out[:, lanes] = (wsum - wnorm * coldot) * inv


def proto_pass(idx, parts, protos, winv, nx, ny):
    width, columns = protos.shape
    own = width // parts.shape[0]
    return call(
        functools.partial(proto_kernel, nx, ny),
        array((own, columns)),
        [idx, parts, protos, winv],
        "svhv",
        scratch=[pltpu.VMEM((2 * own, columns), BF16), pltpu.SemaphoreType.DMA],
    )


def spread_row(line):
    return jnp.transpose(jnp.broadcast_to(line, (128, 128)))


def scaled_kernel(crops, idx, mix, totals, mine, theirs, buf):
    rows, width = mix.shape
    prob = GRAD_SCALE / totals[...]
    for t in range(rows // 128):
        span = slice(128 * t, 128 * (t + 1))
        p = jnp.concatenate([spread_row(prob[t : t + 1, :])] * (width // 128), axis=1)
        buf[span, :] = mix[span, :] * p
    part_rows(crops, idx, buf, mine, theirs)


def part_rows(crops, idx, buf, mine, theirs):
    rest = mine.shape[0] - crops
    for side, ref in ((idx[0], mine), (1 - idx[0], theirs)):
        ref[:crops, :] = buf[pl.ds(pl.multiple_of(side * crops, crops), crops), :]
        ref[crops:, :] = buf[pl.ds(pl.multiple_of(2 * crops + side * rest, 128), rest), :]


def part_pass(idx, mix, totals, crops):
    rows, width = mix.shape
    return call(
        functools.partial(scaled_kernel, crops),
        [array((rows // 2, width)), array((rows // 2, width))],
        [idx, mix, totals],
        "svv",
        scratch=[pltpu.VMEM((rows, width), F32)],
    )


def pack_rows(nz, crops, mine, came, out):
    half = mine.shape[0]
    chunk = half // nz
    share = crops // nz
    rest = chunk - share
    for z in range(nz):
        for src, dst, size in ((z * share, z * chunk, share), (crops + z * rest, z * chunk + share, rest)):
            out[dst : dst + size, :] = mine[src : src + size, :] + came[src : src + size, :]


def halve(idx, bit, total, keep, send):
    size = total.shape[0] // 2
    side = lax.rem(idx[1] // bit, 2)
    keep[...] = total[pl.ds(pl.multiple_of(side * size, 64), size), :]
    send[...] = total[pl.ds(pl.multiple_of((1 - side) * size, 64), size), :]


def pack_half_kernel(nz, crops, idx, mine, came, keep, send, total):
    pack_rows(nz, crops, mine, came, total)
    halve(idx, nz // 2, total, keep, send)


def pack_half_pass(idx, mine, came, nz, crops):
    rows, width = mine.shape
    return call(
        functools.partial(pack_half_kernel, nz, crops),
        [array((rows // 2, width)), array((rows // 2, width))],
        [idx, mine, came],
        "svv",
        scratch=[pltpu.VMEM((rows, width), F32)],
    )


def fold_kernel(bit, idx, mine, came, keep, send, total):
    total[...] = mine[...] + came[...]
    halve(idx, bit, total, keep, send)


def fold_pass(idx, mine, came, bit):
    rows, width = mine.shape
    return call(
        functools.partial(fold_kernel, bit),
        [array((rows // 2, width)), array((rows // 2, width))],
        [idx, mine, came],
        "svv",
        scratch=[pltpu.VMEM((rows, width), F32)],
    )


def mix_kernel(nz, ny, crops, bit, idx, rowparts, target, target_came, prob, prob_came, *refs):
    scale = refs[-1]
    total = refs[-2]
    sub = rowparts.shape[1]
    group = rowparts.shape[0] // ny
    cd = crops // 128
    ci = sub // 2 - cd
    row = GRAD_SCALE / jnp.sum(rowparts[pl.ds(idx[3] * group, group), :, :], axis=0)
    low = idx[0] == 0
    for t in range(cd + ci):
        a, b = (t, cd + t) if t < cd else (cd + t, cd + ci + t)
        line = jnp.where(low, row[a : a + 1, :], row[b : b + 1, :])
        scale[128 * t : 128 * (t + 1), :] = spread_row(line)
    rows, width = target.shape
    here = nz // 2
    chunk = rows // here
    share = crops // nz
    rest = chunk - share
    first = idx[1] // here * here
    for k in range(here):
        z = first + k
        for at, src, size in ((0, z * share, share), (share, crops + z * rest, rest)):
            r = scale[pl.ds(pl.multiple_of(src, 16), size), :]
            span = slice(k * chunk + at, k * chunk + at + size)
            value = target[span, :] + target_came[span, :]
            total[span, :] = (
                prob[span, :]
                + prob_came[span, :]
                - value * jnp.concatenate([r] * (width // 128), axis=1)
            )
    if bit:
        halve(idx, bit, total, refs[0], refs[1])


def mix_pass(idx, rowparts, target, target_came, prob, prob_came, nz, ny, crops, bit):
    rows, width = target.shape
    half = rowparts.shape[1] // 2 * 128
    shapes = [array((rows // 2, width))] * 2 if bit else array((rows, width))
    return call(
        functools.partial(mix_kernel, nz, ny, crops, bit),
        shapes,
        [idx, rowparts, target, target_came, prob, prob_came],
        "svvvvv",
        scratch=([pltpu.VMEM((rows, width), F32)] if bit else []) + [pltpu.VMEM((half, 128), F32)],
    )


def feature_kernel(count, chunks, patches, idx, mask, *refs):
    pieces = refs[:count]
    all_crops, all_rows, crop_out, patch_out, masked_rows, dense, total = refs[count:]
    z = idx[1]
    masked = mask.shape[1]
    crop_share = crop_out.shape[0]
    share = patch_out.shape[0]
    value = pieces[0][...]
    for piece in pieces[1:]:
        value = value + piece[...]
    total[...] = value
    chunk = total.shape[0] // chunks
    rest = chunk - crop_share
    for side in range(chunks):
        masked_rows[side * rest : (side + 1) * rest, :] = total[
            side * chunk + crop_share : (side + 1) * chunk, :
        ]
    crop_at = pl.multiple_of(z * crop_share, 16)
    patch_at = pl.multiple_of(z * share, 128)
    start = pl.multiple_of(lax.rem(z, chunks) * chunk, 16)
    dense[...] = jnp.zeros_like(dense)
    first_row = z * share
    first_image = first_row // patches
    offset = first_row - first_image * patches
    for image in range(masked_rows.shape[0] // masked):

        def put(m, _):
            at = mask[first_image + image, m] + image * patches - offset

            @pl.when(jnp.logical_and(at >= 0, at < share))
            def _():
                dense[pl.ds(at, 1), :] = masked_rows[pl.ds(image * masked + m, 1), :]

            return 0

        lax.fori_loop(0, masked, put, 0, unroll=4)

    def back(x, d):
        xf = x.astype(F32)
        inv = lax.rsqrt(jnp.sum(xf * xf, axis=-1, keepdims=True) + EPS)
        u = xf * inv
        return (d - u * jnp.sum(u * d, axis=-1, keepdims=True)) * inv

    crop_out[...] = back(all_crops[pl.ds(crop_at, crop_share), :], total[pl.ds(start, crop_share), :])
    patch_out[...] = back(all_rows[pl.ds(patch_at, share), :], dense[...])


def feature_pass(idx, mask, pieces, all_crops, all_rows, nz, patches, pair):
    crops, width = all_crops.shape
    crop_share = crops // nz
    share = all_rows.shape[0] // nz
    rows = pieces[0].shape[0]
    return call(
        functools.partial(feature_kernel, len(pieces), 2 if pair else 1, patches),
        [array((crop_share, width)), array((share, width))],
        [idx, mask, *pieces, all_crops, all_rows],
        "ss" + "v" * len(pieces) + "vv",
        scratch=[
            pltpu.VMEM((rows - (2 if pair else 1) * crop_share, width), F32),
            pltpu.VMEM((share, width), F32),
            pltpu.VMEM((rows, width), F32),
        ],
    )


def tie(*values):
    return lax.optimization_barrier(values)


def shifted(n, s):
    return [(i, (i + s) % n) for i in range(n)]


def local(
    sizes,
    student_crops,
    teacher_crops,
    student_patches,
    teacher_patches,
    patch_mask,
    student_protos,
    teacher_protos,
):
    nx, ny, nz = sizes
    images, masked = patch_mask.shape
    patches = student_patches.shape[0] // images
    crops = student_crops.shape[0]
    ix, iy, ic, iz = (lax.axis_index(a) for a in ("x", "y", "c", "z"))
    idx = jnp.stack([ic, iz, ix * ny + iy, iy]).astype(jnp.int32)
    swap = [(0, 1), (1, 0)]

    own = prep(teacher_crops, teacher_patches, student_crops, student_patches, patch_mask)
    other = lax.ppermute(own, "c", swap)
    all_own = lax.all_gather(own, "y")
    expo, sums = teacher_pass(idx, own, other, teacher_protos, crops, nx * ny)
    sub = 2 * (crops + images * masked) // 128

    pair = student_patches.shape[0] // nz < patches

    def across(value, bit):
        return lax.ppermute(value, "z", [(i, i ^ bit) for i in range(nz)])

    colparts = lax.all_to_all(sums, ("x", "y"), 0, 0)
    total, mix = student_pass(idx, own, other, student_protos, crops)
    sums = row_pass(expo, colparts, total, crops, 2 * nz)
    rowparts = lax.all_to_all(sums, ("c", "z"), 0, 0)
    later_protos, _ = tie(student_protos, sums)
    winv = norm_pass(later_protos)
    rowparts, winv = tie(rowparts, winv)
    totals = jnp.sum(rowparts[:, sub:, :], axis=0)
    sums = column_pass(expo, rowparts, crops, nx * ny)

    colparts = lax.all_to_all(sums, ("x", "y"), 0, 0)
    totals, _ = tie(totals, sums)
    all_totals = [totals] + [lax.ppermute(totals, "y", shifted(ny, s)) for s in range(1, ny)]
    mine, theirs = part_pass(idx, mix, totals, crops)
    p_keep, p_send = pack_half_pass(idx, mine, lax.ppermute(theirs, "c", swap), nz, crops)
    colparts, p_send, *all_totals = tie(colparts, p_send, *all_totals)
    p_came = across(p_send, nz // 2)
    sums = row_pass(expo, colparts, None, crops, 2 * nz)
    all_own, sums = tie(all_own, sums)
    all_other = lax.ppermute(all_own, "c", swap)
    rowparts = lax.all_to_all(sums, ("c", "z"), 0, 0)
    sums = column_pass(expo, rowparts, crops, nx * ny)

    colparts = lax.all_to_all(sums, ("x", "y"), 0, 0)
    all_own, all_other, _ = tie(all_own, all_other, sums)
    wide_expo = wide_teacher_pass(idx, all_own, all_other, teacher_protos, crops)
    colparts, p_came, *wide_expo = tie(colparts, p_came, *wide_expo)
    target_mine, target_theirs = target_pass(idx, expo, colparts, student_protos, crops)
    colparts, target_theirs = tie(colparts, target_theirs)
    sums = row_pass(expo, colparts, None, crops, 2 * nz * ny)
    target_came = lax.ppermute(target_theirs, "c", swap)
    keep, send = pack_half_pass(idx, target_mine, target_came, nz, crops)
    sums, send = tie(sums, send)
    rowparts = lax.all_to_all(sums, ("y", "c", "z"), 0, 0)
    came = across(send, nz // 2)
    all_own, all_other, _ = tie(all_own, all_other, sums)
    prob, wnorm, *turned = wide_student_pass(
        idx, all_own, all_other, student_protos, all_totals, crops
    )
    prob, came = tie(prob, came)
    outgoing = weight_pass(
        idx, prob, wnorm, turned, wide_expo, colparts, rowparts, crops, ny, nx * ny * 2
    )
    parts = lax.all_to_all(outgoing, ("x", "y", "c"), 0, 0)
    proto_grad = proto_pass(idx, parts, student_protos, winv, nx, ny)
    bits = [nz >> k for k in range(2, nz.bit_length()) if nz >> k > (1 if pair else 0)]
    total = mix_pass(
        idx, rowparts, keep, came, p_keep, p_came, nz, ny, crops, bits[0] if bits else 0
    )
    pieces = [total]
    for i, bit in enumerate(bits):
        keep, send = total
        last = i + 1 == len(bits)
        pieces = [keep, across(send, bit)]
        if last and pair:
            pieces += [across(keep, 1), across(send, bit ^ 1)]
        elif not last:
            total = fold_pass(idx, *pieces, bits[i + 1])
    if pair and not bits:
        pieces.append(across(total, 1))
    crop_grad, patch_grad = feature_pass(
        idx, patch_mask, pieces, student_crops, student_patches, nz, patches, pair
    )
    return (proto_grad, crop_grad, patch_grad)


def solution(mesh):
    dp, nz = mesh.devices.shape
    nx = 4 if dp == 32 else 2
    ny = dp // (2 * nx)
    grid = Mesh(mesh.devices.reshape(nx, ny, 2, nz), ("x", "y", "c", "z"))
    rows = ("x", "y", "c")
    in_specs = (
        P(rows, None),
        P(rows, None),
        P(rows, None),
        P(rows, None),
        P(rows, None),
        P(None, "z"),
        P(None, "z"),
    )
    out_specs = (P(rows, "z"), P(rows + ("z",), None), P(rows + ("z",), None))
    return jax.shard_map(
        functools.partial(local, (nx, ny, nz)),
        mesh=grid,
        in_specs=in_specs,
        out_specs=out_specs,
        check_vma=False,
    )
```

```python
import functools

import jax
import jax.numpy as jnp
from jax import lax
from jax.experimental import pallas as pl
from jax.experimental.pallas import tpu as pltpu
from jax.sharding import Mesh, PartitionSpec as P

ITERS = 3
EPS = 1e-06
TEACHER_TEMP = 0.07
STUDENT_TEMP = 0.1
LOSS_SCALE = 256.0
GRAD_SCALE = LOSS_SCALE / STUDENT_TEMP
LOG2E = 1.4426950408889634

BN = 512
F32 = jnp.float32
BF16 = jnp.bfloat16
VMEM_LIMIT = 52 * 1024 * 1024
SMEM = pl.BlockSpec(memory_space=pltpu.SMEM)
VMEM = pl.BlockSpec(memory_space=pltpu.VMEM)
HBM = pl.BlockSpec(memory_space=pltpu.HBM)


def call(kernel, out_shape, args, specs, outs="", scratch=(), flops=0, traffic=0):
    spaces = {"s": SMEM, "v": VMEM, "h": HBM}
    if not isinstance(out_shape, list):
        out_specs = VMEM
    else:
        out_specs = [spaces[letter] for letter in outs or "v" * len(out_shape)]
    return pl.pallas_call(
        kernel,
        out_shape=out_shape,
        out_specs=out_specs,
        in_specs=[spaces[letter] for letter in specs],
        scratch_shapes=list(scratch),
        compiler_params=pltpu.CompilerParams(vmem_limit_bytes=VMEM_LIMIT),
        cost_estimate=pl.CostEstimate(flops=flops, bytes_accessed=traffic, transcendentals=0),
    )(*args)


def array(shape, dtype=F32):
    return jax.ShapeDtypeStruct(shape, dtype)


def stream(source, buf, sem, steps, body):
    def copy(j):
        return pltpu.make_async_copy(source(j), buf.at[j], sem.at[j])

    for j in range(steps):
        copy(j).start()

    def step(j, _):
        copy(j).wait()
        body(j, buf.at[j])
        return 0

    lax.fori_loop(0, steps, step, 0)


def unit(x):
    xf = x.astype(F32)
    return xf * lax.rsqrt(jnp.sum(xf * xf, axis=-1, keepdims=True) + EPS)


def unit_cols(w):
    wf = w.astype(F32)
    inv = lax.rsqrt(jnp.sum(wf * wf, axis=0, keepdims=True) + EPS)
    return wf * inv, inv


def prep_kernel(tcrops, tpatch, scrops, spatch, mask, out, tc, tp, sc, sp, sem):
    images, masked = mask.shape
    patches = tp.shape[0] // images
    count = tc.shape[0]
    half = out.shape[0] // 2
    copies = [
        pltpu.make_async_copy(src, dst, sem.at[i])
        for i, (src, dst) in enumerate(((tcrops, tc), (tpatch, tp), (scrops, sc), (spatch, sp)))
    ]
    for copy in copies:
        copy.start()
    for side, (crops, patch_rows) in enumerate(((tc, tp), (sc, sp))):
        copies[2 * side].wait()
        copies[2 * side + 1].wait()
        base = side * half
        out[base : base + count, :] = unit(crops[...])
        for i in range(images):
            place = lax.broadcasted_iota(jnp.int32, (patches, masked), 0)
            chosen = (place == mask[i : i + 1, :]).astype(F32).astype(BF16)
            rows = lax.dot_general(
                chosen,
                patch_rows[i * patches : (i + 1) * patches, :],
                (((0,), (0,)), ((), ())),
                preferred_element_type=F32,
            )
            at = base + count + i * masked
            out[at : at + masked, :] = unit(rows)


def prep(tcrops, tpatch, scrops, spatch, mask):
    half = tcrops.shape[0] + mask.size
    return call(
        prep_kernel,
        array((2 * half, tcrops.shape[1])),
        [tcrops, tpatch, scrops, spatch, mask],
        "hhhhv",
        scratch=[pltpu.VMEM(a.shape, BF16) for a in (tcrops, tpatch, scrops, spatch)]
        + [pltpu.SemaphoreType.DMA((4,))],
    )


def place_rows(core, crops, base, half, own, other, dest):
    rest = half - crops
    for side, ref in ((core, own), (1 - core, other)):
        at = pl.multiple_of(side * crops, crops)
        dest[pl.ds(at, crops), :] = ref[base : base + crops, :].astype(dest.dtype)
        at = pl.multiple_of(2 * crops + side * rest, 128)
        dest[pl.ds(at, rest), :] = ref[base + crops : base + half, :].astype(dest.dtype)


def row_blocks(start, stop):
    return [(a, min(a + 256, stop)) for a in range(start, stop, 256)]


def proto_source(core, protos, size=BN):
    columns = protos.shape[1] // 2
    return lambda j: protos.at[:, pl.ds(pl.multiple_of(core * columns + j * size, size), size)]


def proto_scratch(width, columns, size=BN):
    steps = columns // size
    return [pltpu.VMEM((steps, width, size), BF16), pltpu.SemaphoreType.DMA((steps,))]


def put_columns(step, heads, out):
    copies = out.shape[0]
    per_head = out.shape[1] // 2
    for head in range(2):
        for t in range(BN // 128):
            piece = heads[head][:, 128 * t : 128 * (t + 1)]
            out[:, pl.ds(head * per_head + step * (BN // 128) + t, 1), :] = jnp.broadcast_to(
                piece[None], (copies, 1, 128)
            )


def get_columns(step, head, lines):
    base = head * (lines.shape[0] // 2) + step * (BN // 128)
    return jnp.concatenate([lines[pl.ds(base + t, 1), :] for t in range(BN // 128)], axis=1)


def line_up(values):
    return jnp.concatenate([values[t : t + 1, :] for t in range(values.shape[0])], axis=1)


def teacher_kernel(crops, idx, own, other, protos, expo, sums, feats, out, osem, buf, sem):
    rows, columns = expo.shape
    place_rows(idx[0], crops, 0, rows // 2, own, other, feats)
    steps = columns // BN

    def leave(j, slot):
        at = pl.multiple_of(j * BN, BN)
        return pltpu.make_async_copy(out.at[slot], expo.at[:, pl.ds(at, BN)], osem.at[slot])

    def step(j, block):
        w = unit_cols(block[...])[0].astype(BF16)
        slot = lax.rem(j, 4)

        @pl.when(j >= 4)
        def _():
            leave(j - 4, slot).wait()

        heads = []
        for first, last in ((0, 2 * crops), (2 * crops, rows)):
            part = jnp.zeros((1, BN), F32)
            for start, stop in row_blocks(first, last):
                score = jnp.dot(feats[start:stop, :], w, preferred_element_type=F32)
                e = jnp.exp2(score * (LOG2E / TEACHER_TEMP))
                out[slot, start:stop, :] = e.astype(BF16)
                part = part + jnp.sum(e, axis=0, keepdims=True)
            heads.append(part)
        leave(j, slot).start()
        put_columns(j, heads, sums)

    stream(proto_source(idx[0], protos), buf, sem, steps, step)
    for j in range(max(steps - 4, 0), steps):
        leave(j, j % 4).wait()


def teacher_pass(idx, own, other, protos, crops, copies):
    rows, width = own.shape
    columns = protos.shape[1] // 2
    return call(
        functools.partial(teacher_kernel, crops),
        [array((rows, columns), BF16), array((copies, 2 * columns // 128, 128))],
        [idx, own, other, protos],
        "svvh",
        "hv",
        scratch=[
            pltpu.VMEM((rows, width), BF16),
            pltpu.VMEM((4, rows, BN), BF16),
            pltpu.SemaphoreType.DMA((4,)),
        ]
        + proto_scratch(width, columns),
        flops=2 * rows * width * columns,
        traffic=2 * rows * columns,
    )


def student_kernel(crops, idx, own, other, protos, total, mix, feats, acc, buf, sem):
    rows = feats.shape[0]
    size = buf.shape[2]
    place_rows(idx[0], crops, rows // 2, rows // 2, own, other, feats)
    acc[...] = jnp.zeros_like(acc)
    mix[...] = jnp.zeros_like(mix)

    def step(j, block):
        w = unit_cols(block[...])[0].astype(BF16)
        for start, stop in row_blocks(0, rows):
            score = jnp.dot(feats[start:stop, :], w, preferred_element_type=F32)
            p = jnp.exp2(score * (LOG2E / STUDENT_TEMP))
            part = p[:, :128]
            for t in range(1, size // 128):
                part = part + p[:, 128 * t : 128 * (t + 1)]
            acc[start:stop, :] += part
            mix[start:stop, :] += lax.dot_general(
                p.astype(BF16), w, (((1,), (1,)), ((), ())), preferred_element_type=F32
            )

    stream(proto_source(idx[0], protos, size), buf, sem, protos.shape[1] // 2 // size, step)
    for t in range(rows // 128):
        block = jnp.transpose(acc[128 * t : 128 * (t + 1), :])
        total[t : t + 1, :] = jnp.sum(block, axis=0, keepdims=True)


def student_pass(idx, own, other, protos, crops):
    rows, width = own.shape
    columns = protos.shape[1] // 2
    return call(
        functools.partial(student_kernel, crops),
        [array((rows // 128, 128)), array((rows, width))],
        [idx, own, other, protos],
        "svvh",
        scratch=[pltpu.VMEM((rows, width), BF16), pltpu.VMEM((rows, 128), F32)]
        + proto_scratch(width, columns, 2 * BN),
        flops=4 * rows * width * columns,
        traffic=2 * width * columns,
    )


def row_copies(source, dest, sems):
    return [
        pltpu.make_async_copy(
            source.at[pl.ds(128 * i, 128), :], dest.at[pl.ds(128 * i, 128), :], sems.at[i]
        )
        for i in range(source.shape[0] // 128)
    ]


def column_copies(source, dest, sems):
    return [
        pltpu.make_async_copy(
            source.at[:, pl.ds(BN * j, BN)], dest.at[:, pl.ds(BN * j, BN)], sems.at[j]
        )
        for j in range(source.shape[1] // BN)
    ]


def expo_scratch(expo, blocks):
    return [pltpu.VMEM(expo.shape, BF16), pltpu.SemaphoreType.DMA((blocks,))]


def sum_rows(crops, expo, copies_in, colscale, out):
    copies = out.shape[0]
    rows, columns = expo.shape
    per_head = columns // 128

    for i in range(rows // 128):
        copies_in[i].wait()
        head = 0 if i < 2 * crops // 128 else 1
        at = 128 * i

        def chunk(k, acc):
            e = expo[pl.ds(at, 128), pl.ds(pl.multiple_of(k * 128, 128), 128)].astype(F32)
            return acc + e * colscale[pl.ds(head * per_head + k, 1), :]

        acc = lax.fori_loop(0, per_head, chunk, jnp.zeros((128, 128), F32), unroll=8)
        sums = jnp.sum(jnp.transpose(acc), axis=0, keepdims=True)
        out[:, i : i + 1, :] = jnp.broadcast_to(sums[None], (copies, 1, 128))


def row_kernel(crops, extra, expo, colparts, *refs):
    out, colscale, buf, sems = refs[-4:]
    copies_in = row_copies(expo, buf, sems)
    for copy in copies_in:
        copy.start()
    if extra:
        total = refs[0]
        count = total.shape[0]
        out[:, count:, :] = jnp.broadcast_to(total[...][None], (out.shape[0], count, 128))
    colscale[...] = 1.0 / jnp.sum(colparts[...], axis=0)
    sum_rows(crops, buf, copies_in, colscale, out)


def row_pass(expo, colparts, total, crops, copies):
    rows, columns = expo.shape
    extra = total is not None
    return call(
        functools.partial(row_kernel, crops, extra),
        array((copies, rows // 128 * (2 if extra else 1), 128)),
        [expo, colparts] + ([total] if extra else []),
        "hvv" if extra else "hv",
        scratch=[pltpu.VMEM((2 * columns // 128, 128), F32)] + expo_scratch(expo, rows // 128),
        flops=2 * rows * columns,
        traffic=2 * rows * columns,
    )


def target_kernel(crops, idx, expo, colparts, protos, mine, theirs, target, colscale, ebuf, esem, buf, sem):
    rows, columns = expo.shape
    steps = columns // BN
    copies_in = column_copies(expo, ebuf, esem)
    for copy in copies_in:
        copy.start()
    colscale[...] = 1.0 / jnp.sum(colparts[...], axis=0)
    target[...] = jnp.zeros_like(target)

    def step(j, block):
        wnorm = unit_cols(block[...])[0]
        at = pl.multiple_of(j * BN, BN)
        pltpu.make_async_copy(
            expo.at[:, pl.ds(at, BN)], ebuf.at[:, pl.ds(at, BN)], esem.at[j]
        ).wait()
        for head, (first, last) in enumerate(((0, 2 * crops), (2 * crops, rows))):
            w = (wnorm * get_columns(j, head, colscale)).astype(BF16)
            target[first:last, :] += lax.dot_general(
                ebuf[first:last, pl.ds(at, BN)],
                w,
                (((1,), (1,)), ((), ())),
                preferred_element_type=F32,
            )

    stream(proto_source(idx[0], protos), buf, sem, steps, step)
    part_rows(crops, idx, target, mine, theirs)


def target_pass(idx, expo, colparts, protos, crops):
    rows, columns = expo.shape
    width = protos.shape[0]
    return call(
        functools.partial(target_kernel, crops),
        [array((rows // 2, width)), array((rows // 2, width))],
        [idx, expo, colparts, protos],
        "shvh",
        scratch=[pltpu.VMEM((rows, width), F32), pltpu.VMEM((2 * columns // 128, 128), F32)]
        + expo_scratch(expo, columns // BN)
        + proto_scratch(width, columns),
        flops=2 * rows * columns * width,
        traffic=2 * rows * columns,
    )


def split3(v):
    high = v.astype(BF16)
    rest = v - high.astype(F32)
    middle = rest.astype(BF16)
    low = (rest - middle.astype(F32)).astype(BF16)
    pad = jnp.zeros((13, v.shape[1]), F32)
    parts = [high.astype(F32), middle.astype(F32), low.astype(F32), pad]
    return jnp.concatenate(parts, axis=0).astype(BF16)


def column_kernel(crops, expo, rowparts, out, buf, sems):
    rows, columns = expo.shape
    copies_in = column_copies(expo, buf, sems)
    for copy in copies_in:
        copy.start()
    scale = line_up(1.0 / jnp.sum(rowparts[:, : rows // 128, :], axis=0))
    spans = [(0, 2 * crops), (2 * crops, rows)]
    lefts = [split3(scale[:, first:last]) for first, last in spans]
    for j in range(columns // BN):
        copies_in[j].wait()
        heads = []
        for left, (first, last) in zip(lefts, spans):
            sums = jnp.dot(
                left, buf[first:last, j * BN : (j + 1) * BN], preferred_element_type=F32
            )
            heads.append(sums[0:1, :] + sums[1:2, :] + sums[2:3, :])
        put_columns(j, heads, out)


def column_pass(expo, rowparts, crops, copies):
    rows, columns = expo.shape
    return call(
        functools.partial(column_kernel, crops),
        array((copies, 2 * columns // 128, 128)),
        [expo, rowparts],
        "hv",
        scratch=expo_scratch(expo, columns // BN),
        flops=2 * rows * columns,
        traffic=2 * rows * columns,
    )


def part_source(idx, ny, protos):
    columns = protos.shape[1] // 2
    part = columns // ny
    at = pl.multiple_of(idx[0] * columns + idx[3] * part, 128)
    return protos.at[:, pl.ds(at, part)]


def stream_rows(ny, here, base, half, refs, buf, sem, ready, body):
    copies = [
        pltpu.make_async_copy(ref.at[pl.ds(base, half), :], buf.at[i], sem.at[i])
        for i, ref in enumerate(refs)
    ]
    for copy in copies:
        copy.start()
    ready()
    for i, copy in enumerate(copies):
        copy.wait()
        body(i // ny, lax.rem(here + ny - i % ny, ny), buf.at[i])


def wide_teacher_kernel(ny, crops, idx, protos, *refs):
    expo_d, expo_i, w, wbuf, out, osem, buf, sem, wsem = refs[2 * ny :]
    half = buf.shape[1]
    rest = half - crops
    fetch = pltpu.make_async_copy(part_source(idx, ny, protos), wbuf, wsem)
    fetch.start()
    leaving = []

    def ready():
        fetch.wait()
        w[...] = unit_cols(wbuf[...])[0].astype(BF16)

    def body(side, y, ref):
        place = 2 * y + jnp.where(idx[0] == side, 0, 1)
        slot = len(leaving) % 4
        if len(leaving) >= 4:
            for copy in leaving[-4]:
                copy.wait()
        feats = ref[...].astype(BF16)
        for start in range(0, half, 128):
            score = jnp.dot(feats[start : start + 128, :], w[...], preferred_element_type=F32)
            e = jnp.exp2(score * (LOG2E / TEACHER_TEMP)).astype(BF16)
            out[slot, start : start + 128, :] = e
        at_d = pl.multiple_of(place * crops, 128)
        at_i = pl.multiple_of(place * rest, 128)
        copies = (
            pltpu.make_async_copy(
                out.at[slot, pl.ds(0, crops), :], expo_d.at[pl.ds(at_d, crops), :], osem.at[slot, 0]
            ),
            pltpu.make_async_copy(
                out.at[slot, pl.ds(crops, rest), :], expo_i.at[pl.ds(at_i, rest), :], osem.at[slot, 1]
            ),
        )
        for copy in copies:
            copy.start()
        leaving.append(copies)

    stream_rows(ny, idx[3], 0, half, refs[: 2 * ny], buf, sem, ready, body)
    for copies in leaving[-4:]:
        for copy in copies:
            copy.wait()


def wide_teacher_pass(idx, gathered, protos, crops):
    ny = len(gathered) // 2
    rows, width = gathered[0].shape
    half = rows // 2
    part = protos.shape[1] // 2 // ny
    return call(
        functools.partial(wide_teacher_kernel, ny, crops),
        [array((2 * ny * crops, part), BF16), array((2 * ny * (half - crops), part), BF16)],
        [idx, protos, *gathered],
        "sh" + "h" * len(gathered),
        "hh",
        scratch=[
            pltpu.VMEM((width, part), BF16),
            pltpu.VMEM((width, part), BF16),
            pltpu.VMEM((4, half, part), BF16),
            pltpu.SemaphoreType.DMA((4, 2)),
            pltpu.VMEM((2 * ny, half, width), F32),
            pltpu.SemaphoreType.DMA((2 * ny,)),
            pltpu.SemaphoreType.DMA,
        ],
        flops=2 * 2 * ny * half * width * part,
        traffic=8 * ny * half * width,
    )


def wide_student_kernel(ny, crops, idx, protos, *refs):
    gathered = refs[: 2 * ny]
    refs = refs[2 * ny :]
    totals = refs[:ny]
    out, wnorm_out, turned_d, turned_i, w, wbuf, scale, left, expo, buf, sem, wsem = refs[ny:]
    half = buf.shape[1]
    rest = half - crops
    sub = totals[0].shape[0]
    fetch = pltpu.make_async_copy(part_source(idx, ny, protos), wbuf, wsem)
    fetch.start()
    for s in range(ny):
        y = lax.rem(idx[3] + ny - s, ny)
        scale[pl.ds(pl.multiple_of(y * sub, sub), sub), :] = GRAD_SCALE / totals[s][...]
    out[...] = jnp.zeros_like(out)

    def ready():
        fetch.wait()
        wnorm_out[...] = unit_cols(wbuf[...])[0]
        w[...] = wnorm_out[...].astype(BF16)

    def body(side, y, ref):
        core = jnp.where(idx[0] == side, 0, 1)
        place = 2 * y + core
        feats = ref[...].astype(BF16)
        turned = jnp.transpose(feats.astype(F32))
        turned_d[:, pl.ds(pl.multiple_of(place * crops, 128), crops)] = turned[:, :crops].astype(BF16)
        turned_i[:, pl.ds(pl.multiple_of(place * rest, 128), rest)] = turned[:, crops:].astype(BF16)
        lines = [scale[pl.ds(y * sub + core * (crops // 128) + t, 1), :] for t in range(crops // 128)]
        first = y * sub + 2 * crops // 128 + core * (rest // 128)
        lines += [scale[pl.ds(first + t, 1), :] for t in range(rest // 128)]
        left[...] = (turned * jnp.concatenate(lines, axis=1)).astype(BF16)
        for start in range(0, half, 128):
            score = jnp.dot(feats[start : start + 128, :], w[...], preferred_element_type=F32)
            expo[start : start + 128, :] = jnp.exp2(score * (LOG2E / STUDENT_TEMP)).astype(BF16)
        out[...] += jnp.dot(left[...], expo[...], preferred_element_type=F32)

    stream_rows(ny, idx[3], half, half, gathered, buf, sem, ready, body)


def wide_student_pass(idx, gathered, protos, totals, crops):
    ny = len(gathered) // 2
    rows, width = gathered[0].shape
    half = rows // 2
    part = protos.shape[1] // 2 // ny
    return call(
        functools.partial(wide_student_kernel, ny, crops),
        [
            array((width, part)),
            array((width, part)),
            array((width, 2 * ny * crops), BF16),
            array((width, 2 * ny * (half - crops)), BF16),
        ],
        [idx, protos, *gathered, *totals],
        "sh" + "h" * len(gathered) + "v" * ny,
        scratch=[
            pltpu.VMEM((width, part), BF16),
            pltpu.VMEM((width, part), BF16),
            pltpu.VMEM((ny * rows // 128, 128), F32),
            pltpu.VMEM((width, half), BF16),
            pltpu.VMEM((half, part), BF16),
            pltpu.VMEM((2 * ny, half, width), F32),
            pltpu.SemaphoreType.DMA((2 * ny,)),
            pltpu.SemaphoreType.DMA,
        ],
        flops=4 * 2 * ny * half * width * part,
        traffic=8 * ny * half * width,
    )


def weight_kernel(ny, crops, idx, prob_in, wnorm_in, turned_d_in, turned_i_in, expo_d, expo_i, colparts, rowparts, out, left_d, left_i, scales, rowscale, buf_d, buf_i, sems_d, sems_i, targets, prob, wnorm, turned_d, turned_i, sem):
    loads = [
        pltpu.make_async_copy(src, dst, sem.at[i])
        for i, (src, dst) in enumerate(
            ((turned_d_in, turned_d), (turned_i_in, turned_i), (prob_in, prob), (wnorm_in, wnorm))
        )
    ]
    for copy in loads[:2]:
        copy.start()
    copies, _, _ = out.shape
    width, part = prob.shape
    own = width // copies
    streams = []
    for expo, buf, sems in ((expo_d, buf_d, sems_d), (expo_i, buf_i, sems_i)):
        size = buf.shape[0] // sems.shape[0]
        streams.append(
            [
                pltpu.make_async_copy(
                    expo.at[pl.ds(i * size, size), :], buf.at[pl.ds(i * size, size), :], sems.at[i]
                )
                for i in range(sems.shape[0])
            ]
        )
    for copy in streams[0] + streams[1] + loads[2:]:
        copy.start()
    group = rowparts.shape[0] // ny
    sub = rowparts.shape[1]
    scales[...] = GRAD_SCALE / jnp.sum(colparts[...], axis=0)
    for y in range(ny):
        rowscale[y * sub : (y + 1) * sub, :] = 1.0 / jnp.sum(
            rowparts[y * group : (y + 1) * group], axis=0
        )
    cd = crops // 128
    ci = sub // 2 - cd
    lines_d, lines_i = [], []
    for y in range(ny):
        for core in range(2):
            for t in range(cd):
                at = y * sub + core * cd + t
                lines_d.append(rowscale[at : at + 1, :])
            for t in range(ci):
                at = y * sub + 2 * cd + core * ci + t
                lines_i.append(rowscale[at : at + 1, :])
    loads[0].wait()
    loads[1].wait()
    left_d[...] = (turned_d[...].astype(F32) * jnp.concatenate(lines_d, axis=1)).astype(BF16)
    left_i[...] = (turned_i[...].astype(F32) * jnp.concatenate(lines_i, axis=1)).astype(BF16)
    per_head = scales.shape[0] // 2
    first = idx[3] * (part // 128)
    for head, (left, buf) in enumerate(((left_d, buf_d), (left_i, buf_i))):
        size = buf.shape[0] // len(streams[head])
        for i, copy in enumerate(streams[head]):
            copy.wait()
            span = slice(i * size, (i + 1) * size)
            value = jnp.dot(left[:, span], buf[span, :], preferred_element_type=F32)
            if i == 0:
                targets[head] = value
            else:
                targets[head] += value
    loads[2].wait()
    loads[3].wait()
    for at in range(0, part, BN):
        span = slice(at, at + BN)
        wsum = prob[:, span]
        for head in range(2):
            base = head * per_head + first + at // 128
            line = [scales[pl.ds(base + t, 1), :] for t in range(BN // 128)]
            wsum = wsum - targets[head, :, span] * jnp.concatenate(line, axis=1)
        coldot = jnp.sum(wnorm[:, span] * wsum, axis=0, keepdims=True)
        for t in range(BN // 128):
            lanes = slice(128 * t, 128 * (t + 1))
            row = at // 128 + t
            for d in range(copies):
                out[d, row * own : (row + 1) * own, :] = wsum[d * own : (d + 1) * own, lanes]
            tail = part // 128 * own + row
            out[:, tail : tail + 1, :] = jnp.broadcast_to(
                coldot[:, lanes][None], (copies, 1, 128)
            )


def weight_pass(idx, prob, wnorm, turned, expo, colparts, rowparts, crops, ny, copies):
    width, part = prob.shape
    lines = part // 128 * (width // copies + 1)
    rows = turned[0].shape[1] + turned[1].shape[1]
    return call(
        functools.partial(weight_kernel, ny, crops),
        array((copies, lines, 128)),
        [idx, prob, wnorm, *turned, *expo, colparts, rowparts],
        "shhhhhhvv",
        scratch=[
            pltpu.VMEM(turned[0].shape, BF16),
            pltpu.VMEM(turned[1].shape, BF16),
            pltpu.VMEM(colparts.shape[1:], F32),
            pltpu.VMEM((ny * rowparts.shape[1], 128), F32),
            pltpu.VMEM(expo[0].shape, BF16),
            pltpu.VMEM(expo[1].shape, BF16),
            pltpu.SemaphoreType.DMA((expo[0].shape[0] // 512,)),
            pltpu.SemaphoreType.DMA((expo[1].shape[0] // 512,)),
            pltpu.VMEM((2, width, part), F32),
            pltpu.VMEM((width, part), F32),
            pltpu.VMEM((width, part), F32),
            pltpu.VMEM(turned[0].shape, BF16),
            pltpu.VMEM(turned[1].shape, BF16),
            pltpu.SemaphoreType.DMA((4,)),
        ],
        flops=2 * rows * width * part,
        traffic=2 * rows * part,
    )


def norm_kernel(protos, out, buf, sem):
    blocks, size, _ = buf.shape
    copies = [
        pltpu.make_async_copy(protos.at[pl.ds(i * size, size), :], buf.at[i], sem.at[i])
        for i in range(blocks)
    ]
    for copy in copies:
        copy.start()
    for i, copy in enumerate(copies):
        copy.wait()
        w = buf[i].astype(F32)
        part = jnp.sum(w * w, axis=0, keepdims=True)
        out[...] = part if i == 0 else out[...] + part
    out[...] = lax.rsqrt(out[...] + EPS)


def norm_pass(protos):
    width, columns = protos.shape
    return call(
        norm_kernel,
        array((1, columns)),
        [protos],
        "h",
        scratch=[pltpu.VMEM((8, width // 8, columns), BF16), pltpu.SemaphoreType.DMA((8,))],
        flops=3 * width * columns,
        traffic=2 * width * columns,
    )


def proto_kernel(nx, ny, idx, parts, protos, winv, out, rows, sem):
    own, columns = out.shape
    copies = parts.shape[0]
    part = columns // (2 * ny)
    tail = part // 128 * own
    at = pl.multiple_of(idx[2] * (2 * own), 2 * own)
    fetch = pltpu.make_async_copy(protos.at[pl.ds(at, 2 * own), :], rows, sem)
    fetch.start()
    fetch.wait()
    for y in range(ny):
        for core in range(2):
            for t in range(part // 128):
                first = core * (columns // 2) + y * part + 128 * t
                lanes = slice(first, first + 128)
                wsum = jnp.zeros((own, 128), F32)
                coldot = jnp.zeros((1, 128), F32)
                for x in range(nx):
                    source = (x * ny + y) * 2 + core
                    wsum = wsum + parts[source, t * own : (t + 1) * own, :]
                    coldot = coldot + parts[source, tail + t : tail + t + 1, :]
                inv = winv[:, lanes]
                both = rows[:, lanes].astype(F32)
                wnorm = jnp.where(idx[0] == 0, both[:own, :], both[own:, :]) * inv
                out[:, lanes] = (wsum - wnorm * coldot) * inv


def proto_pass(idx, parts, protos, winv, nx, ny):
    width, columns = protos.shape
    own = width // parts.shape[0]
    return call(
        functools.partial(proto_kernel, nx, ny),
        array((own, columns)),
        [idx, parts, protos, winv],
        "svhv",
        scratch=[pltpu.VMEM((2 * own, columns), BF16), pltpu.SemaphoreType.DMA],
    )


def spread_row(line):
    return jnp.transpose(jnp.broadcast_to(line, (128, 128)))


def scaled_kernel(crops, idx, mix, totals, mine, theirs, buf):
    rows, width = mix.shape
    prob = GRAD_SCALE / totals[...]
    for t in range(rows // 128):
        span = slice(128 * t, 128 * (t + 1))
        p = jnp.concatenate([spread_row(prob[t : t + 1, :])] * (width // 128), axis=1)
        buf[span, :] = mix[span, :] * p
    part_rows(crops, idx, buf, mine, theirs)


def part_rows(crops, idx, buf, mine, theirs):
    rest = mine.shape[0] - crops
    for side, ref in ((idx[0], mine), (1 - idx[0], theirs)):
        ref[:crops, :] = buf[pl.ds(pl.multiple_of(side * crops, crops), crops), :]
        ref[crops:, :] = buf[pl.ds(pl.multiple_of(2 * crops + side * rest, 128), rest), :]


def part_pass(idx, mix, totals, crops):
    rows, width = mix.shape
    return call(
        functools.partial(scaled_kernel, crops),
        [array((rows // 2, width)), array((rows // 2, width))],
        [idx, mix, totals],
        "svv",
        scratch=[pltpu.VMEM((rows, width), F32)],
    )


def pack_rows(nz, crops, mine, came, out):
    half = mine.shape[0]
    chunk = half // nz
    share = crops // nz
    rest = chunk - share
    for z in range(nz):
        for src, dst, size in ((z * share, z * chunk, share), (crops + z * rest, z * chunk + share, rest)):
            out[dst : dst + size, :] = mine[src : src + size, :] + came[src : src + size, :]


def halve(idx, bit, total, keep, send):
    size = total.shape[0] // 2
    side = lax.rem(idx[1] // bit, 2)
    keep[...] = total[pl.ds(pl.multiple_of(side * size, 64), size), :]
    send[...] = total[pl.ds(pl.multiple_of((1 - side) * size, 64), size), :]


def pack_half_kernel(nz, crops, idx, mine, came, keep, send, total):
    pack_rows(nz, crops, mine, came, total)
    halve(idx, nz // 2, total, keep, send)


def pack_half_pass(idx, mine, came, nz, crops):
    rows, width = mine.shape
    return call(
        functools.partial(pack_half_kernel, nz, crops),
        [array((rows // 2, width)), array((rows // 2, width))],
        [idx, mine, came],
        "svv",
        scratch=[pltpu.VMEM((rows, width), F32)],
    )


def fold_kernel(bit, idx, mine, came, keep, send, total):
    total[...] = mine[...] + came[...]
    halve(idx, bit, total, keep, send)


def fold_pass(idx, mine, came, bit):
    rows, width = mine.shape
    return call(
        functools.partial(fold_kernel, bit),
        [array((rows // 2, width)), array((rows // 2, width))],
        [idx, mine, came],
        "svv",
        scratch=[pltpu.VMEM((rows, width), F32)],
    )


def mix_kernel(nz, ny, crops, bit, idx, rowparts, target, target_came, prob, prob_came, *refs):
    scale = refs[-1]
    total = refs[-2]
    sub = rowparts.shape[1]
    group = rowparts.shape[0] // ny
    cd = crops // 128
    ci = sub // 2 - cd
    row = GRAD_SCALE / jnp.sum(rowparts[pl.ds(idx[3] * group, group), :, :], axis=0)
    low = idx[0] == 0
    for t in range(cd + ci):
        a, b = (t, cd + t) if t < cd else (cd + t, cd + ci + t)
        line = jnp.where(low, row[a : a + 1, :], row[b : b + 1, :])
        scale[128 * t : 128 * (t + 1), :] = spread_row(line)
    rows, width = target.shape
    here = nz // 2
    chunk = rows // here
    share = crops // nz
    rest = chunk - share
    first = idx[1] // here * here
    for k in range(here):
        z = first + k
        for at, src, size in ((0, z * share, share), (share, crops + z * rest, rest)):
            r = scale[pl.ds(pl.multiple_of(src, 16), size), :]
            span = slice(k * chunk + at, k * chunk + at + size)
            value = target[span, :] + target_came[span, :]
            total[span, :] = (
                prob[span, :]
                + prob_came[span, :]
                - value * jnp.concatenate([r] * (width // 128), axis=1)
            )
    if bit:
        halve(idx, bit, total, refs[0], refs[1])


def mix_pass(idx, rowparts, target, target_came, prob, prob_came, nz, ny, crops, bit):
    rows, width = target.shape
    half = rowparts.shape[1] // 2 * 128
    shapes = [array((rows // 2, width))] * 2 if bit else array((rows, width))
    return call(
        functools.partial(mix_kernel, nz, ny, crops, bit),
        shapes,
        [idx, rowparts, target, target_came, prob, prob_came],
        "svvvvv",
        scratch=([pltpu.VMEM((rows, width), F32)] if bit else []) + [pltpu.VMEM((half, 128), F32)],
    )


def feature_kernel(count, chunks, patches, idx, mask, *refs):
    pieces = refs[:count]
    all_crops, all_rows, crop_out, patch_out, masked_rows, dense, total = refs[count:]
    z = idx[1]
    masked = mask.shape[1]
    crop_share = crop_out.shape[0]
    share = patch_out.shape[0]
    value = pieces[0][...]
    for piece in pieces[1:]:
        value = value + piece[...]
    total[...] = value
    chunk = total.shape[0] // chunks
    rest = chunk - crop_share
    for side in range(chunks):
        masked_rows[side * rest : (side + 1) * rest, :] = total[
            side * chunk + crop_share : (side + 1) * chunk, :
        ]
    crop_at = pl.multiple_of(z * crop_share, 16)
    patch_at = pl.multiple_of(z * share, 128)
    start = pl.multiple_of(lax.rem(z, chunks) * chunk, 16)
    dense[...] = jnp.zeros_like(dense)
    first_row = z * share
    first_image = first_row // patches
    offset = first_row - first_image * patches
    for image in range(masked_rows.shape[0] // masked):

        def put(m, _):
            at = mask[first_image + image, m] + image * patches - offset

            @pl.when(jnp.logical_and(at >= 0, at < share))
            def _():
                dense[pl.ds(at, 1), :] = masked_rows[pl.ds(image * masked + m, 1), :]

            return 0

        lax.fori_loop(0, masked, put, 0, unroll=4)

    def back(x, d):
        xf = x.astype(F32)
        inv = lax.rsqrt(jnp.sum(xf * xf, axis=-1, keepdims=True) + EPS)
        u = xf * inv
        return (d - u * jnp.sum(u * d, axis=-1, keepdims=True)) * inv

    crop_out[...] = back(all_crops[pl.ds(crop_at, crop_share), :], total[pl.ds(start, crop_share), :])
    patch_out[...] = back(all_rows[pl.ds(patch_at, share), :], dense[...])


def feature_pass(idx, mask, pieces, all_crops, all_rows, nz, patches, pair):
    crops, width = all_crops.shape
    crop_share = crops // nz
    share = all_rows.shape[0] // nz
    rows = pieces[0].shape[0]
    return call(
        functools.partial(feature_kernel, len(pieces), 2 if pair else 1, patches),
        [array((crop_share, width)), array((share, width))],
        [idx, mask, *pieces, all_crops, all_rows],
        "ss" + "v" * len(pieces) + "vv",
        scratch=[
            pltpu.VMEM((rows - (2 if pair else 1) * crop_share, width), F32),
            pltpu.VMEM((share, width), F32),
            pltpu.VMEM((rows, width), F32),
        ],
    )


def tie(*values):
    return lax.optimization_barrier(values)


def shifted(n, s):
    return [(i, (i + s) % n) for i in range(n)]


def local(
    sizes,
    student_crops,
    teacher_crops,
    student_patches,
    teacher_patches,
    patch_mask,
    student_protos,
    teacher_protos,
):
    nx, ny, nz = sizes
    images, masked = patch_mask.shape
    patches = student_patches.shape[0] // images
    crops = student_crops.shape[0]
    ix, iy, ic, iz = (lax.axis_index(a) for a in ("x", "y", "c", "z"))
    idx = jnp.stack([ic, iz, ix * ny + iy, iy]).astype(jnp.int32)
    swap = [(0, 1), (1, 0)]

    own = prep(teacher_crops, teacher_patches, student_crops, student_patches, patch_mask)
    other = lax.ppermute(own, "c", swap)
    up, down = shifted(ny, 1), shifted(ny, ny - 1)
    from_up = lax.ppermute(own, "y", up)
    from_down = lax.ppermute(own, "y", down) if ny > 2 else None
    expo, sums = teacher_pass(idx, own, other, teacher_protos, crops, nx * ny)
    sub = 2 * (crops + images * masked) // 128

    pair = student_patches.shape[0] // nz < patches

    def across(value, bit):
        return lax.ppermute(value, "z", [(i, i ^ bit) for i in range(nz)])

    colparts = lax.all_to_all(sums, ("x", "y"), 0, 0)
    total, mix = student_pass(idx, own, other, student_protos, crops)
    sums = row_pass(expo, colparts, total, crops, 2 * nz)
    rowparts = lax.all_to_all(sums, ("c", "z"), 0, 0)
    later_protos, _ = tie(student_protos, sums)
    winv = norm_pass(later_protos)
    rowparts, winv, from_up, from_down = tie(rowparts, winv, from_up, from_down)
    ring = [own, from_up]
    while len(ring) < ny - 1:
        ring.append(lax.ppermute(ring[-1], "y", up))
    if ny > 2:
        ring.append(from_down)
    totals = jnp.sum(rowparts[:, sub:, :], axis=0)
    sums = column_pass(expo, rowparts, crops, nx * ny)

    colparts = lax.all_to_all(sums, ("x", "y"), 0, 0)
    totals, _ = tie(totals, sums)
    all_totals = [totals] + [lax.ppermute(totals, "y", shifted(ny, s)) for s in range(1, ny)]
    mine, theirs = part_pass(idx, mix, totals, crops)
    p_keep, p_send = pack_half_pass(idx, mine, lax.ppermute(theirs, "c", swap), nz, crops)
    colparts, p_send, *all_totals = tie(colparts, p_send, *all_totals)
    p_came = across(p_send, nz // 2)
    sums = row_pass(expo, colparts, None, crops, 2 * nz)
    sums, *ring = tie(sums, *ring)
    gathered = ring + [other] + [lax.ppermute(rows, "c", swap) for rows in ring[1:]]
    rowparts = lax.all_to_all(sums, ("c", "z"), 0, 0)
    sums = column_pass(expo, rowparts, crops, nx * ny)

    colparts = lax.all_to_all(sums, ("x", "y"), 0, 0)
    *gathered, _ = tie(*gathered, sums)
    wide_expo = wide_teacher_pass(idx, gathered, teacher_protos, crops)
    colparts, p_came, *wide_expo = tie(colparts, p_came, *wide_expo)
    target_mine, target_theirs = target_pass(idx, expo, colparts, student_protos, crops)
    colparts, target_theirs = tie(colparts, target_theirs)
    sums = row_pass(expo, colparts, None, crops, 2 * nz * ny)
    target_came = lax.ppermute(target_theirs, "c", swap)
    keep, send = pack_half_pass(idx, target_mine, target_came, nz, crops)
    sums, send = tie(sums, send)
    rowparts = lax.all_to_all(sums, ("y", "c", "z"), 0, 0)
    came = across(send, nz // 2)
    *gathered, _ = tie(*gathered, sums)
    prob, wnorm, *turned = wide_student_pass(idx, gathered, student_protos, all_totals, crops)
    prob, came = tie(prob, came)
    outgoing = weight_pass(
        idx, prob, wnorm, turned, wide_expo, colparts, rowparts, crops, ny, nx * ny * 2
    )
    parts = lax.all_to_all(outgoing, ("x", "y", "c"), 0, 0)
    proto_grad = proto_pass(idx, parts, student_protos, winv, nx, ny)
    bits = [nz >> k for k in range(2, nz.bit_length()) if nz >> k > (1 if pair else 0)]
    total = mix_pass(
        idx, rowparts, keep, came, p_keep, p_came, nz, ny, crops, bits[0] if bits else 0
    )
    pieces = [total]
    for i, bit in enumerate(bits):
        keep, send = total
        last = i + 1 == len(bits)
        pieces = [keep, across(send, bit)]
        if last and pair:
            pieces += [across(keep, 1), across(send, bit ^ 1)]
        elif not last:
            total = fold_pass(idx, *pieces, bits[i + 1])
    if pair and not bits:
        pieces.append(across(total, 1))
    crop_grad, patch_grad = feature_pass(
        idx, patch_mask, pieces, student_crops, student_patches, nz, patches, pair
    )
    return (proto_grad, crop_grad, patch_grad)


def solution(mesh):
    dp, nz = mesh.devices.shape
    nx = 4 if dp == 32 else 2
    ny = dp // (2 * nx)
    grid = Mesh(mesh.devices.reshape(nx, ny, 2, nz), ("x", "y", "c", "z"))
    rows = ("x", "y", "c")
    in_specs = (
        P(rows, None),
        P(rows, None),
        P(rows, None),
        P(rows, None),
        P(rows, None),
        P(None, "z"),
        P(None, "z"),
    )
    out_specs = (P(rows, "z"), P(rows + ("z",), None), P(rows + ("z",), None))
    return jax.shard_map(
        functools.partial(local, (nx, ny, nz)),
        mesh=grid,
        in_specs=in_specs,
        out_specs=out_specs,
        check_vma=False,
    )
```

```python
import functools

import jax
import jax.numpy as jnp
from jax import lax
from jax.experimental import pallas as pl
from jax.experimental.pallas import tpu as pltpu
from jax.sharding import Mesh, PartitionSpec as P

ITERS = 3
EPS = 1e-06
TEACHER_TEMP = 0.07
STUDENT_TEMP = 0.1
LOSS_SCALE = 256.0
GRAD_SCALE = LOSS_SCALE / STUDENT_TEMP
LOG2E = 1.4426950408889634

BN = 512
F32 = jnp.float32
BF16 = jnp.bfloat16
VMEM_LIMIT = 52 * 1024 * 1024
SMEM = pl.BlockSpec(memory_space=pltpu.SMEM)
VMEM = pl.BlockSpec(memory_space=pltpu.VMEM)
HBM = pl.BlockSpec(memory_space=pltpu.HBM)


def call(kernel, out_shape, args, specs, outs="", scratch=(), flops=0, traffic=0):
    spaces = {"s": SMEM, "v": VMEM, "h": HBM}
    if not isinstance(out_shape, list):
        out_specs = VMEM
    else:
        out_specs = [spaces[letter] for letter in outs or "v" * len(out_shape)]
    return pl.pallas_call(
        kernel,
        out_shape=out_shape,
        out_specs=out_specs,
        in_specs=[spaces[letter] for letter in specs],
        scratch_shapes=list(scratch),
        compiler_params=pltpu.CompilerParams(vmem_limit_bytes=VMEM_LIMIT),
        cost_estimate=pl.CostEstimate(flops=flops, bytes_accessed=traffic, transcendentals=0),
    )(*args)


def array(shape, dtype=F32):
    return jax.ShapeDtypeStruct(shape, dtype)


def stream(source, buf, sem, steps, body):
    def copy(j):
        return pltpu.make_async_copy(source(j), buf.at[j], sem.at[j])

    for j in range(steps):
        copy(j).start()

    def step(j, _):
        copy(j).wait()
        body(j, buf.at[j])
        return 0

    lax.fori_loop(0, steps, step, 0)


def unit(x):
    xf = x.astype(F32)
    return xf * lax.rsqrt(jnp.sum(xf * xf, axis=-1, keepdims=True) + EPS)


def unit_cols(w):
    wf = w.astype(F32)
    inv = lax.rsqrt(jnp.sum(wf * wf, axis=0, keepdims=True) + EPS)
    return wf * inv, inv


def prep_kernel(tcrops, tpatch, scrops, spatch, mask, out, tc, tp, sc, sp, sem):
    images, masked = mask.shape
    patches = tp.shape[0] // images
    count = tc.shape[0]
    half = out.shape[0] // 2
    copies = [
        pltpu.make_async_copy(src, dst, sem.at[i])
        for i, (src, dst) in enumerate(((tcrops, tc), (tpatch, tp), (scrops, sc), (spatch, sp)))
    ]
    for copy in copies:
        copy.start()
    for side, (crops, patch_rows) in enumerate(((tc, tp), (sc, sp))):
        copies[2 * side].wait()
        copies[2 * side + 1].wait()
        base = side * half
        out[base : base + count, :] = unit(crops[...])
        for i in range(images):
            place = lax.broadcasted_iota(jnp.int32, (patches, masked), 0)
            chosen = (place == mask[i : i + 1, :]).astype(F32).astype(BF16)
            rows = lax.dot_general(
                chosen,
                patch_rows[i * patches : (i + 1) * patches, :],
                (((0,), (0,)), ((), ())),
                preferred_element_type=F32,
            )
            at = base + count + i * masked
            out[at : at + masked, :] = unit(rows)


def prep(tcrops, tpatch, scrops, spatch, mask):
    half = tcrops.shape[0] + mask.size
    return call(
        prep_kernel,
        array((2 * half, tcrops.shape[1])),
        [tcrops, tpatch, scrops, spatch, mask],
        "hhhhv",
        scratch=[pltpu.VMEM(a.shape, BF16) for a in (tcrops, tpatch, scrops, spatch)]
        + [pltpu.SemaphoreType.DMA((4,))],
    )


def place_rows(core, crops, base, half, own, other, dest):
    rest = half - crops
    for side, ref in ((core, own), (1 - core, other)):
        at = pl.multiple_of(side * crops, crops)
        dest[pl.ds(at, crops), :] = ref[base : base + crops, :].astype(dest.dtype)
        at = pl.multiple_of(2 * crops + side * rest, 128)
        dest[pl.ds(at, rest), :] = ref[base + crops : base + half, :].astype(dest.dtype)


def row_blocks(start, stop):
    return [(a, min(a + 256, stop)) for a in range(start, stop, 256)]


def proto_source(core, protos, size=BN):
    columns = protos.shape[1] // 2
    return lambda j: protos.at[:, pl.ds(pl.multiple_of(core * columns + j * size, size), size)]


def proto_scratch(width, columns, size=BN):
    steps = columns // size
    return [pltpu.VMEM((steps, width, size), BF16), pltpu.SemaphoreType.DMA((steps,))]


def put_columns(step, heads, out):
    copies = out.shape[0]
    per_head = out.shape[1] // 2
    for head in range(2):
        for t in range(BN // 128):
            piece = heads[head][:, 128 * t : 128 * (t + 1)]
            out[:, pl.ds(head * per_head + step * (BN // 128) + t, 1), :] = jnp.broadcast_to(
                piece[None], (copies, 1, 128)
            )


def get_columns(step, head, lines):
    base = head * (lines.shape[0] // 2) + step * (BN // 128)
    return jnp.concatenate([lines[pl.ds(base + t, 1), :] for t in range(BN // 128)], axis=1)


def line_up(values):
    return jnp.concatenate([values[t : t + 1, :] for t in range(values.shape[0])], axis=1)


def teacher_kernel(crops, idx, own, other, protos, expo, sums, feats, out, osem, buf, sem):
    rows, columns = expo.shape
    place_rows(idx[0], crops, 0, rows // 2, own, other, feats)
    steps = columns // BN

    def leave(j, slot):
        at = pl.multiple_of(j * BN, BN)
        return pltpu.make_async_copy(out.at[slot], expo.at[:, pl.ds(at, BN)], osem.at[slot])

    def step(j, block):
        w = unit_cols(block[...])[0].astype(BF16)
        slot = lax.rem(j, 4)

        @pl.when(j >= 4)
        def _():
            leave(j - 4, slot).wait()

        heads = []
        for first, last in ((0, 2 * crops), (2 * crops, rows)):
            part = jnp.zeros((1, BN), F32)
            for start, stop in row_blocks(first, last):
                score = jnp.dot(feats[start:stop, :], w, preferred_element_type=F32)
                e = jnp.exp2(score * (LOG2E / TEACHER_TEMP))
                out[slot, start:stop, :] = e.astype(BF16)
                part = part + jnp.sum(e, axis=0, keepdims=True)
            heads.append(part)
        leave(j, slot).start()
        put_columns(j, heads, sums)

    stream(proto_source(idx[0], protos), buf, sem, steps, step)
    for j in range(max(steps - 4, 0), steps):
        leave(j, j % 4).wait()


def teacher_pass(idx, own, other, protos, crops, copies):
    rows, width = own.shape
    columns = protos.shape[1] // 2
    return call(
        functools.partial(teacher_kernel, crops),
        [array((rows, columns), BF16), array((copies, 2 * columns // 128, 128))],
        [idx, own, other, protos],
        "svvh",
        "hv",
        scratch=[
            pltpu.VMEM((rows, width), BF16),
            pltpu.VMEM((4, rows, BN), BF16),
            pltpu.SemaphoreType.DMA((4,)),
        ]
        + proto_scratch(width, columns),
        flops=2 * rows * width * columns,
        traffic=2 * rows * columns,
    )


def student_kernel(crops, idx, own, other, protos, total, mix, feats, acc, buf, sem):
    rows = feats.shape[0]
    size = buf.shape[2]
    place_rows(idx[0], crops, rows // 2, rows // 2, own, other, feats)
    acc[...] = jnp.zeros_like(acc)
    mix[...] = jnp.zeros_like(mix)

    def step(j, block):
        w = unit_cols(block[...])[0].astype(BF16)
        for start, stop in row_blocks(0, rows):
            score = jnp.dot(feats[start:stop, :], w, preferred_element_type=F32)
            p = jnp.exp2(score * (LOG2E / STUDENT_TEMP))
            part = p[:, :128]
            for t in range(1, size // 128):
                part = part + p[:, 128 * t : 128 * (t + 1)]
            acc[start:stop, :] += part
            mix[start:stop, :] += lax.dot_general(
                p.astype(BF16), w, (((1,), (1,)), ((), ())), preferred_element_type=F32
            )

    stream(proto_source(idx[0], protos, size), buf, sem, protos.shape[1] // 2 // size, step)
    for t in range(rows // 128):
        block = jnp.transpose(acc[128 * t : 128 * (t + 1), :])
        total[t : t + 1, :] = jnp.sum(block, axis=0, keepdims=True)


def student_pass(idx, own, other, protos, crops):
    rows, width = own.shape
    columns = protos.shape[1] // 2
    return call(
        functools.partial(student_kernel, crops),
        [array((rows // 128, 128)), array((rows, width))],
        [idx, own, other, protos],
        "svvh",
        scratch=[pltpu.VMEM((rows, width), BF16), pltpu.VMEM((rows, 128), F32)]
        + proto_scratch(width, columns, 2 * BN),
        flops=4 * rows * width * columns,
        traffic=2 * width * columns,
    )


def row_copies(source, dest, sems):
    return [
        pltpu.make_async_copy(
            source.at[pl.ds(128 * i, 128), :], dest.at[pl.ds(128 * i, 128), :], sems.at[i]
        )
        for i in range(source.shape[0] // 128)
    ]


def column_copies(source, dest, sems):
    return [
        pltpu.make_async_copy(
            source.at[:, pl.ds(BN * j, BN)], dest.at[:, pl.ds(BN * j, BN)], sems.at[j]
        )
        for j in range(source.shape[1] // BN)
    ]


def expo_scratch(expo, blocks):
    return [pltpu.VMEM(expo.shape, BF16), pltpu.SemaphoreType.DMA((blocks,))]


def sum_rows(crops, expo, copies_in, colscale, out):
    copies = out.shape[0]
    rows, columns = expo.shape
    per_head = columns // 128

    for i in range(rows // 128):
        copies_in[i].wait()
        head = 0 if i < 2 * crops // 128 else 1
        at = 128 * i

        def chunk(k, acc):
            e = expo[pl.ds(at, 128), pl.ds(pl.multiple_of(k * 128, 128), 128)].astype(F32)
            return acc + e * colscale[pl.ds(head * per_head + k, 1), :]

        acc = lax.fori_loop(0, per_head, chunk, jnp.zeros((128, 128), F32), unroll=8)
        sums = jnp.sum(jnp.transpose(acc), axis=0, keepdims=True)
        out[:, i : i + 1, :] = jnp.broadcast_to(sums[None], (copies, 1, 128))


def row_kernel(crops, extra, expo, colparts, *refs):
    out, colscale, buf, sems = refs[-4:]
    copies_in = row_copies(expo, buf, sems)
    for copy in copies_in:
        copy.start()
    if extra:
        total = refs[0]
        count = total.shape[0]
        out[:, count:, :] = jnp.broadcast_to(total[...][None], (out.shape[0], count, 128))
    colscale[...] = 1.0 / jnp.sum(colparts[...], axis=0)
    sum_rows(crops, buf, copies_in, colscale, out)


def row_pass(expo, colparts, total, crops, copies):
    rows, columns = expo.shape
    extra = total is not None
    return call(
        functools.partial(row_kernel, crops, extra),
        array((copies, rows // 128 * (2 if extra else 1), 128)),
        [expo, colparts] + ([total] if extra else []),
        "hvv" if extra else "hv",
        scratch=[pltpu.VMEM((2 * columns // 128, 128), F32)] + expo_scratch(expo, rows // 128),
        flops=2 * rows * columns,
        traffic=2 * rows * columns,
    )


def target_kernel(crops, idx, expo, colparts, protos, mine, theirs, target, colscale, ebuf, esem, buf, sem):
    rows, columns = expo.shape
    steps = columns // BN
    copies_in = column_copies(expo, ebuf, esem)
    for copy in copies_in:
        copy.start()
    colscale[...] = 1.0 / jnp.sum(colparts[...], axis=0)
    target[...] = jnp.zeros_like(target)

    def step(j, block):
        wnorm = unit_cols(block[...])[0]
        at = pl.multiple_of(j * BN, BN)
        pltpu.make_async_copy(
            expo.at[:, pl.ds(at, BN)], ebuf.at[:, pl.ds(at, BN)], esem.at[j]
        ).wait()
        for head, (first, last) in enumerate(((0, 2 * crops), (2 * crops, rows))):
            w = (wnorm * get_columns(j, head, colscale)).astype(BF16)
            target[first:last, :] += lax.dot_general(
                ebuf[first:last, pl.ds(at, BN)],
                w,
                (((1,), (1,)), ((), ())),
                preferred_element_type=F32,
            )

    stream(proto_source(idx[0], protos), buf, sem, steps, step)
    part_rows(crops, idx, target, mine, theirs)


def target_pass(idx, expo, colparts, protos, crops):
    rows, columns = expo.shape
    width = protos.shape[0]
    return call(
        functools.partial(target_kernel, crops),
        [array((rows // 2, width)), array((rows // 2, width))],
        [idx, expo, colparts, protos],
        "shvh",
        scratch=[pltpu.VMEM((rows, width), F32), pltpu.VMEM((2 * columns // 128, 128), F32)]
        + expo_scratch(expo, columns // BN)
        + proto_scratch(width, columns),
        flops=2 * rows * columns * width,
        traffic=2 * rows * columns,
    )


def split3(v):
    high = v.astype(BF16)
    rest = v - high.astype(F32)
    middle = rest.astype(BF16)
    low = (rest - middle.astype(F32)).astype(BF16)
    pad = jnp.zeros((13, v.shape[1]), F32)
    parts = [high.astype(F32), middle.astype(F32), low.astype(F32), pad]
    return jnp.concatenate(parts, axis=0).astype(BF16)


def column_kernel(crops, expo, rowparts, out, buf, sems):
    rows, columns = expo.shape
    copies_in = column_copies(expo, buf, sems)
    for copy in copies_in:
        copy.start()
    scale = line_up(1.0 / jnp.sum(rowparts[:, : rows // 128, :], axis=0))
    spans = [(0, 2 * crops), (2 * crops, rows)]
    lefts = [split3(scale[:, first:last]) for first, last in spans]
    for j in range(columns // BN):
        copies_in[j].wait()
        heads = []
        for left, (first, last) in zip(lefts, spans):
            sums = jnp.dot(
                left, buf[first:last, j * BN : (j + 1) * BN], preferred_element_type=F32
            )
            heads.append(sums[0:1, :] + sums[1:2, :] + sums[2:3, :])
        put_columns(j, heads, out)


def column_pass(expo, rowparts, crops, copies):
    rows, columns = expo.shape
    return call(
        functools.partial(column_kernel, crops),
        array((copies, 2 * columns // 128, 128)),
        [expo, rowparts],
        "hv",
        scratch=expo_scratch(expo, columns // BN),
        flops=2 * rows * columns,
        traffic=2 * rows * columns,
    )


def part_source(idx, ny, protos):
    columns = protos.shape[1] // 2
    part = columns // ny
    at = pl.multiple_of(idx[0] * columns + idx[3] * part, 128)
    return protos.at[:, pl.ds(at, part)]


def stream_rows(ny, here, base, half, refs, buf, sem, ready, body):
    copies = [
        pltpu.make_async_copy(ref.at[pl.ds(base, half), :], buf.at[i], sem.at[i])
        for i, ref in enumerate(refs)
    ]
    for copy in copies:
        copy.start()
    ready()
    for i, copy in enumerate(copies):
        copy.wait()
        body(i // ny, lax.rem(here + ny - i % ny, ny), buf.at[i])


def wide_teacher_kernel(ny, crops, idx, protos, *refs):
    expo_d, expo_i, w, wbuf, out, osem, buf, sem, wsem = refs[2 * ny :]
    half = buf.shape[1]
    rest = half - crops
    fetch = pltpu.make_async_copy(part_source(idx, ny, protos), wbuf, wsem)
    fetch.start()
    leaving = []

    def ready():
        fetch.wait()
        w[...] = unit_cols(wbuf[...])[0].astype(BF16)

    def body(side, y, ref):
        place = 2 * y + jnp.where(idx[0] == side, 0, 1)
        slot = len(leaving) % 4
        if len(leaving) >= 4:
            for copy in leaving[-4]:
                copy.wait()
        feats = ref[...].astype(BF16)
        for start, stop in row_blocks(0, half):
            score = jnp.dot(feats[start:stop, :], w[...], preferred_element_type=F32)
            out[slot, start:stop, :] = jnp.exp2(score * (LOG2E / TEACHER_TEMP)).astype(BF16)
        at_d = pl.multiple_of(place * crops, 128)
        at_i = pl.multiple_of(place * rest, 128)
        copies = (
            pltpu.make_async_copy(
                out.at[slot, pl.ds(0, crops), :], expo_d.at[pl.ds(at_d, crops), :], osem.at[slot, 0]
            ),
            pltpu.make_async_copy(
                out.at[slot, pl.ds(crops, rest), :], expo_i.at[pl.ds(at_i, rest), :], osem.at[slot, 1]
            ),
        )
        for copy in copies:
            copy.start()
        leaving.append(copies)

    stream_rows(ny, idx[3], 0, half, refs[: 2 * ny], buf, sem, ready, body)
    for copies in leaving[-4:]:
        for copy in copies:
            copy.wait()


def wide_teacher_pass(idx, gathered, protos, crops):
    ny = len(gathered) // 2
    rows, width = gathered[0].shape
    half = rows // 2
    part = protos.shape[1] // 2 // ny
    return call(
        functools.partial(wide_teacher_kernel, ny, crops),
        [array((2 * ny * crops, part), BF16), array((2 * ny * (half - crops), part), BF16)],
        [idx, protos, *gathered],
        "sh" + "h" * len(gathered),
        "hh",
        scratch=[
            pltpu.VMEM((width, part), BF16),
            pltpu.VMEM((width, part), BF16),
            pltpu.VMEM((4, half, part), BF16),
            pltpu.SemaphoreType.DMA((4, 2)),
            pltpu.VMEM((2 * ny, half, width), F32),
            pltpu.SemaphoreType.DMA((2 * ny,)),
            pltpu.SemaphoreType.DMA,
        ],
        flops=2 * 2 * ny * half * width * part,
        traffic=8 * ny * half * width,
    )


def wide_student_kernel(ny, crops, idx, protos, *refs):
    gathered = refs[: 2 * ny]
    refs = refs[2 * ny :]
    totals = refs[:ny]
    out, wnorm_out, turned_d, turned_i, w, wbuf, scale, left, expo, buf, sem, wsem = refs[ny:]
    half = buf.shape[1]
    rest = half - crops
    sub = totals[0].shape[0]
    fetch = pltpu.make_async_copy(part_source(idx, ny, protos), wbuf, wsem)
    fetch.start()
    for s in range(ny):
        y = lax.rem(idx[3] + ny - s, ny)
        scale[pl.ds(pl.multiple_of(y * sub, sub), sub), :] = GRAD_SCALE / totals[s][...]
    out[...] = jnp.zeros_like(out)

    def ready():
        fetch.wait()
        wnorm_out[...] = unit_cols(wbuf[...])[0]
        w[...] = wnorm_out[...].astype(BF16)

    def body(side, y, ref):
        core = jnp.where(idx[0] == side, 0, 1)
        place = 2 * y + core
        feats = ref[...].astype(BF16)
        turned = jnp.transpose(feats.astype(F32))
        turned_d[:, pl.ds(pl.multiple_of(place * crops, 128), crops)] = turned[:, :crops].astype(BF16)
        turned_i[:, pl.ds(pl.multiple_of(place * rest, 128), rest)] = turned[:, crops:].astype(BF16)
        lines = [scale[pl.ds(y * sub + core * (crops // 128) + t, 1), :] for t in range(crops // 128)]
        first = y * sub + 2 * crops // 128 + core * (rest // 128)
        lines += [scale[pl.ds(first + t, 1), :] for t in range(rest // 128)]
        left[...] = (turned * jnp.concatenate(lines, axis=1)).astype(BF16)
        for start, stop in row_blocks(0, half):
            score = jnp.dot(feats[start:stop, :], w[...], preferred_element_type=F32)
            expo[start:stop, :] = jnp.exp2(score * (LOG2E / STUDENT_TEMP)).astype(BF16)
        out[...] += jnp.dot(left[...], expo[...], preferred_element_type=F32)

    stream_rows(ny, idx[3], half, half, gathered, buf, sem, ready, body)


def wide_student_pass(idx, gathered, protos, totals, crops):
    ny = len(gathered) // 2
    rows, width = gathered[0].shape
    half = rows // 2
    part = protos.shape[1] // 2 // ny
    return call(
        functools.partial(wide_student_kernel, ny, crops),
        [
            array((width, part)),
            array((width, part)),
            array((width, 2 * ny * crops), BF16),
            array((width, 2 * ny * (half - crops)), BF16),
        ],
        [idx, protos, *gathered, *totals],
        "sh" + "h" * len(gathered) + "v" * ny,
        scratch=[
            pltpu.VMEM((width, part), BF16),
            pltpu.VMEM((width, part), BF16),
            pltpu.VMEM((ny * rows // 128, 128), F32),
            pltpu.VMEM((width, half), BF16),
            pltpu.VMEM((half, part), BF16),
            pltpu.VMEM((2 * ny, half, width), F32),
            pltpu.SemaphoreType.DMA((2 * ny,)),
            pltpu.SemaphoreType.DMA,
        ],
        flops=4 * 2 * ny * half * width * part,
        traffic=8 * ny * half * width,
    )


def weight_kernel(ny, crops, idx, prob_in, wnorm_in, turned_d_in, turned_i_in, expo_d, expo_i, colparts, rowparts, out, left_d, left_i, scales, rowscale, buf_d, buf_i, sems_d, sems_i, targets, prob, wnorm, turned_d, turned_i, sem):
    loads = [
        pltpu.make_async_copy(src, dst, sem.at[i])
        for i, (src, dst) in enumerate(
            ((turned_d_in, turned_d), (turned_i_in, turned_i), (prob_in, prob), (wnorm_in, wnorm))
        )
    ]
    for copy in loads[:2]:
        copy.start()
    copies, _, _ = out.shape
    width, part = prob.shape
    own = width // copies
    streams = []
    for expo, buf, sems in ((expo_d, buf_d, sems_d), (expo_i, buf_i, sems_i)):
        size = buf.shape[0] // sems.shape[0]
        streams.append(
            [
                pltpu.make_async_copy(
                    expo.at[pl.ds(i * size, size), :], buf.at[pl.ds(i * size, size), :], sems.at[i]
                )
                for i in range(sems.shape[0])
            ]
        )
    for copy in streams[0] + streams[1] + loads[2:]:
        copy.start()
    group = rowparts.shape[0] // ny
    sub = rowparts.shape[1]
    scales[...] = GRAD_SCALE / jnp.sum(colparts[...], axis=0)
    for y in range(ny):
        rowscale[y * sub : (y + 1) * sub, :] = 1.0 / jnp.sum(
            rowparts[y * group : (y + 1) * group], axis=0
        )
    cd = crops // 128
    ci = sub // 2 - cd
    lines_d, lines_i = [], []
    for y in range(ny):
        for core in range(2):
            for t in range(cd):
                at = y * sub + core * cd + t
                lines_d.append(rowscale[at : at + 1, :])
            for t in range(ci):
                at = y * sub + 2 * cd + core * ci + t
                lines_i.append(rowscale[at : at + 1, :])
    loads[0].wait()
    loads[1].wait()
    left_d[...] = (turned_d[...].astype(F32) * jnp.concatenate(lines_d, axis=1)).astype(BF16)
    left_i[...] = (turned_i[...].astype(F32) * jnp.concatenate(lines_i, axis=1)).astype(BF16)
    per_head = scales.shape[0] // 2
    first = idx[3] * (part // 128)
    for head, (left, buf) in enumerate(((left_d, buf_d), (left_i, buf_i))):
        size = buf.shape[0] // len(streams[head])
        for i, copy in enumerate(streams[head]):
            copy.wait()
            span = slice(i * size, (i + 1) * size)
            value = jnp.dot(left[:, span], buf[span, :], preferred_element_type=F32)
            if i == 0:
                targets[head] = value
            else:
                targets[head] += value
    loads[2].wait()
    loads[3].wait()
    for at in range(0, part, BN):
        span = slice(at, at + BN)
        wsum = prob[:, span]
        for head in range(2):
            base = head * per_head + first + at // 128
            line = [scales[pl.ds(base + t, 1), :] for t in range(BN // 128)]
            wsum = wsum - targets[head, :, span] * jnp.concatenate(line, axis=1)
        coldot = jnp.sum(wnorm[:, span] * wsum, axis=0, keepdims=True)
        for t in range(BN // 128):
            lanes = slice(128 * t, 128 * (t + 1))
            row = at // 128 + t
            for d in range(copies):
                out[d, row * own : (row + 1) * own, :] = wsum[d * own : (d + 1) * own, lanes]
            tail = part // 128 * own + row
            out[:, tail : tail + 1, :] = jnp.broadcast_to(
                coldot[:, lanes][None], (copies, 1, 128)
            )


def weight_pass(idx, prob, wnorm, turned, expo, colparts, rowparts, crops, ny, copies):
    width, part = prob.shape
    lines = part // 128 * (width // copies + 1)
    rows = turned[0].shape[1] + turned[1].shape[1]
    return call(
        functools.partial(weight_kernel, ny, crops),
        array((copies, lines, 128)),
        [idx, prob, wnorm, *turned, *expo, colparts, rowparts],
        "shhhhhhvv",
        scratch=[
            pltpu.VMEM(turned[0].shape, BF16),
            pltpu.VMEM(turned[1].shape, BF16),
            pltpu.VMEM(colparts.shape[1:], F32),
            pltpu.VMEM((ny * rowparts.shape[1], 128), F32),
            pltpu.VMEM(expo[0].shape, BF16),
            pltpu.VMEM(expo[1].shape, BF16),
            pltpu.SemaphoreType.DMA((expo[0].shape[0] // 512,)),
            pltpu.SemaphoreType.DMA((expo[1].shape[0] // 512,)),
            pltpu.VMEM((2, width, part), F32),
            pltpu.VMEM((width, part), F32),
            pltpu.VMEM((width, part), F32),
            pltpu.VMEM(turned[0].shape, BF16),
            pltpu.VMEM(turned[1].shape, BF16),
            pltpu.SemaphoreType.DMA((4,)),
        ],
        flops=2 * rows * width * part,
        traffic=2 * rows * part,
    )


def norm_kernel(protos, out, buf, sem):
    blocks, size, _ = buf.shape
    copies = [
        pltpu.make_async_copy(protos.at[pl.ds(i * size, size), :], buf.at[i], sem.at[i])
        for i in range(blocks)
    ]
    for copy in copies:
        copy.start()
    for i, copy in enumerate(copies):
        copy.wait()
        w = buf[i].astype(F32)
        part = jnp.sum(w * w, axis=0, keepdims=True)
        out[...] = part if i == 0 else out[...] + part
    out[...] = lax.rsqrt(out[...] + EPS)


def norm_pass(protos):
    width, columns = protos.shape
    return call(
        norm_kernel,
        array((1, columns)),
        [protos],
        "h",
        scratch=[pltpu.VMEM((8, width // 8, columns), BF16), pltpu.SemaphoreType.DMA((8,))],
        flops=3 * width * columns,
        traffic=2 * width * columns,
    )


def proto_kernel(nx, ny, idx, parts, protos, winv, out, rows, sem):
    own, columns = out.shape
    copies = parts.shape[0]
    part = columns // (2 * ny)
    tail = part // 128 * own
    at = pl.multiple_of(idx[2] * (2 * own), 2 * own)
    fetch = pltpu.make_async_copy(protos.at[pl.ds(at, 2 * own), :], rows, sem)
    fetch.start()
    fetch.wait()
    for y in range(ny):
        for core in range(2):
            for t in range(part // 128):
                first = core * (columns // 2) + y * part + 128 * t
                lanes = slice(first, first + 128)
                wsum = jnp.zeros((own, 128), F32)
                coldot = jnp.zeros((1, 128), F32)
                for x in range(nx):
                    source = (x * ny + y) * 2 + core
                    wsum = wsum + parts[source, t * own : (t + 1) * own, :]
                    coldot = coldot + parts[source, tail + t : tail + t + 1, :]
                inv = winv[:, lanes]
                both = rows[:, lanes].astype(F32)
                wnorm = jnp.where(idx[0] == 0, both[:own, :], both[own:, :]) * inv
                out[:, lanes] = (wsum - wnorm * coldot) * inv


def proto_pass(idx, parts, protos, winv, nx, ny):
    width, columns = protos.shape
    own = width // parts.shape[0]
    return call(
        functools.partial(proto_kernel, nx, ny),
        array((own, columns)),
        [idx, parts, protos, winv],
        "svhv",
        scratch=[pltpu.VMEM((2 * own, columns), BF16), pltpu.SemaphoreType.DMA],
    )


def spread_row(line):
    return jnp.transpose(jnp.broadcast_to(line, (128, 128)))


def scaled_kernel(crops, idx, mix, totals, mine, theirs, buf):
    rows, width = mix.shape
    prob = GRAD_SCALE / totals[...]
    for t in range(rows // 128):
        span = slice(128 * t, 128 * (t + 1))
        p = jnp.concatenate([spread_row(prob[t : t + 1, :])] * (width // 128), axis=1)
        buf[span, :] = mix[span, :] * p
    part_rows(crops, idx, buf, mine, theirs)


def part_rows(crops, idx, buf, mine, theirs):
    rest = mine.shape[0] - crops
    for side, ref in ((idx[0], mine), (1 - idx[0], theirs)):
        ref[:crops, :] = buf[pl.ds(pl.multiple_of(side * crops, crops), crops), :]
        ref[crops:, :] = buf[pl.ds(pl.multiple_of(2 * crops + side * rest, 128), rest), :]


def part_pass(idx, mix, totals, crops):
    rows, width = mix.shape
    return call(
        functools.partial(scaled_kernel, crops),
        [array((rows // 2, width)), array((rows // 2, width))],
        [idx, mix, totals],
        "svv",
        scratch=[pltpu.VMEM((rows, width), F32)],
    )


def pack_rows(nz, crops, mine, came, out):
    half = mine.shape[0]
    chunk = half // nz
    share = crops // nz
    rest = chunk - share
    for z in range(nz):
        for src, dst, size in ((z * share, z * chunk, share), (crops + z * rest, z * chunk + share, rest)):
            out[dst : dst + size, :] = mine[src : src + size, :] + came[src : src + size, :]


def halve(idx, bit, total, keep, send):
    size = total.shape[0] // 2
    side = lax.rem(idx[1] // bit, 2)
    keep[...] = total[pl.ds(pl.multiple_of(side * size, 64), size), :]
    send[...] = total[pl.ds(pl.multiple_of((1 - side) * size, 64), size), :]


def pack_half_kernel(nz, crops, idx, mine, came, keep, send, total):
    pack_rows(nz, crops, mine, came, total)
    halve(idx, nz // 2, total, keep, send)


def pack_half_pass(idx, mine, came, nz, crops):
    rows, width = mine.shape
    return call(
        functools.partial(pack_half_kernel, nz, crops),
        [array((rows // 2, width)), array((rows // 2, width))],
        [idx, mine, came],
        "svv",
        scratch=[pltpu.VMEM((rows, width), F32)],
    )


def fold_kernel(bit, idx, mine, came, keep, send, total):
    total[...] = mine[...] + came[...]
    halve(idx, bit, total, keep, send)


def fold_pass(idx, mine, came, bit):
    rows, width = mine.shape
    return call(
        functools.partial(fold_kernel, bit),
        [array((rows // 2, width)), array((rows // 2, width))],
        [idx, mine, came],
        "svv",
        scratch=[pltpu.VMEM((rows, width), F32)],
    )


def mix_kernel(nz, ny, crops, bit, idx, rowparts, target, target_came, prob, prob_came, *refs):
    scale = refs[-1]
    total = refs[-2]
    sub = rowparts.shape[1]
    group = rowparts.shape[0] // ny
    cd = crops // 128
    ci = sub // 2 - cd
    row = GRAD_SCALE / jnp.sum(rowparts[pl.ds(idx[3] * group, group), :, :], axis=0)
    low = idx[0] == 0
    for t in range(cd + ci):
        a, b = (t, cd + t) if t < cd else (cd + t, cd + ci + t)
        line = jnp.where(low, row[a : a + 1, :], row[b : b + 1, :])
        scale[128 * t : 128 * (t + 1), :] = spread_row(line)
    rows, width = target.shape
    here = nz // 2
    chunk = rows // here
    share = crops // nz
    rest = chunk - share
    first = idx[1] // here * here
    for k in range(here):
        z = first + k
        for at, src, size in ((0, z * share, share), (share, crops + z * rest, rest)):
            r = scale[pl.ds(pl.multiple_of(src, 16), size), :]
            span = slice(k * chunk + at, k * chunk + at + size)
            value = target[span, :] + target_came[span, :]
            total[span, :] = (
                prob[span, :]
                + prob_came[span, :]
                - value * jnp.concatenate([r] * (width // 128), axis=1)
            )
    if bit:
        halve(idx, bit, total, refs[0], refs[1])


def mix_pass(idx, rowparts, target, target_came, prob, prob_came, nz, ny, crops, bit):
    rows, width = target.shape
    half = rowparts.shape[1] // 2 * 128
    shapes = [array((rows // 2, width))] * 2 if bit else array((rows, width))
    return call(
        functools.partial(mix_kernel, nz, ny, crops, bit),
        shapes,
        [idx, rowparts, target, target_came, prob, prob_came],
        "svvvvv",
        scratch=([pltpu.VMEM((rows, width), F32)] if bit else []) + [pltpu.VMEM((half, 128), F32)],
    )


def feature_kernel(count, chunks, patches, idx, mask, *refs):
    pieces = refs[:count]
    all_crops, all_rows, crop_out, patch_out, masked_rows, dense, total = refs[count:]
    z = idx[1]
    masked = mask.shape[1]
    crop_share = crop_out.shape[0]
    share = patch_out.shape[0]
    value = pieces[0][...]
    for piece in pieces[1:]:
        value = value + piece[...]
    total[...] = value
    chunk = total.shape[0] // chunks
    rest = chunk - crop_share
    for side in range(chunks):
        masked_rows[side * rest : (side + 1) * rest, :] = total[
            side * chunk + crop_share : (side + 1) * chunk, :
        ]
    crop_at = pl.multiple_of(z * crop_share, 16)
    patch_at = pl.multiple_of(z * share, 128)
    start = pl.multiple_of(lax.rem(z, chunks) * chunk, 16)
    dense[...] = jnp.zeros_like(dense)
    first_row = z * share
    first_image = first_row // patches
    offset = first_row - first_image * patches
    for image in range(masked_rows.shape[0] // masked):

        def put(m, _):
            at = mask[first_image + image, m] + image * patches - offset

            @pl.when(jnp.logical_and(at >= 0, at < share))
            def _():
                dense[pl.ds(at, 1), :] = masked_rows[pl.ds(image * masked + m, 1), :]

            return 0

        lax.fori_loop(0, masked, put, 0, unroll=4)

    def back(x, d):
        xf = x.astype(F32)
        inv = lax.rsqrt(jnp.sum(xf * xf, axis=-1, keepdims=True) + EPS)
        u = xf * inv
        return (d - u * jnp.sum(u * d, axis=-1, keepdims=True)) * inv

    crop_out[...] = back(all_crops[pl.ds(crop_at, crop_share), :], total[pl.ds(start, crop_share), :])
    patch_out[...] = back(all_rows[pl.ds(patch_at, share), :], dense[...])


def feature_pass(idx, mask, pieces, all_crops, all_rows, nz, patches, pair):
    crops, width = all_crops.shape
    crop_share = crops // nz
    share = all_rows.shape[0] // nz
    rows = pieces[0].shape[0]
    return call(
        functools.partial(feature_kernel, len(pieces), 2 if pair else 1, patches),
        [array((crop_share, width)), array((share, width))],
        [idx, mask, *pieces, all_crops, all_rows],
        "ss" + "v" * len(pieces) + "vv",
        scratch=[
            pltpu.VMEM((rows - (2 if pair else 1) * crop_share, width), F32),
            pltpu.VMEM((share, width), F32),
            pltpu.VMEM((rows, width), F32),
        ],
    )


def tie(*values):
    return lax.optimization_barrier(values)


def shifted(n, s):
    return [(i, (i + s) % n) for i in range(n)]


def local(
    sizes,
    student_crops,
    teacher_crops,
    student_patches,
    teacher_patches,
    patch_mask,
    student_protos,
    teacher_protos,
):
    nx, ny, nz = sizes
    images, masked = patch_mask.shape
    patches = student_patches.shape[0] // images
    crops = student_crops.shape[0]
    ix, iy, ic, iz = (lax.axis_index(a) for a in ("x", "y", "c", "z"))
    idx = jnp.stack([ic, iz, ix * ny + iy, iy]).astype(jnp.int32)
    swap = [(0, 1), (1, 0)]

    own = prep(teacher_crops, teacher_patches, student_crops, student_patches, patch_mask)
    other = lax.ppermute(own, "c", swap)
    up, down = shifted(ny, 1), shifted(ny, ny - 1)
    from_up = lax.ppermute(own, "y", up)
    from_down = lax.ppermute(own, "y", down) if ny > 2 else None
    expo, sums = teacher_pass(idx, own, other, teacher_protos, crops, nx * ny)
    sub = 2 * (crops + images * masked) // 128

    pair = student_patches.shape[0] // nz < patches

    def across(value, bit):
        return lax.ppermute(value, "z", [(i, i ^ bit) for i in range(nz)])

    colparts = lax.all_to_all(sums, ("x", "y"), 0, 0)
    total, mix = student_pass(idx, own, other, student_protos, crops)
    colparts, total, from_up, from_down = tie(colparts, total, from_up, from_down)
    ring = [own, from_up]
    while len(ring) < ny - 1:
        ring.append(lax.ppermute(ring[-1], "y", up))
    if ny > 2:
        ring.append(from_down)
    sums = row_pass(expo, colparts, total, crops, 2 * nz)
    rowparts = lax.all_to_all(sums, ("c", "z"), 0, 0)
    later_protos, _ = tie(student_protos, sums)
    winv = norm_pass(later_protos)
    rowparts, winv = tie(rowparts, winv)
    totals = jnp.sum(rowparts[:, sub:, :], axis=0)
    sums = column_pass(expo, rowparts, crops, nx * ny)

    colparts = lax.all_to_all(sums, ("x", "y"), 0, 0)
    totals, _ = tie(totals, sums)
    all_totals = [totals] + [lax.ppermute(totals, "y", shifted(ny, s)) for s in range(1, ny)]
    mine, theirs = part_pass(idx, mix, totals, crops)
    p_keep, p_send = pack_half_pass(idx, mine, lax.ppermute(theirs, "c", swap), nz, crops)
    colparts, p_send = tie(colparts, p_send)
    p_came = across(p_send, nz // 2)
    sums = row_pass(expo, colparts, None, crops, 2 * nz)
    sums, *ring = tie(sums, *ring)
    gathered = ring + [other] + [lax.ppermute(rows, "c", swap) for rows in ring[1:]]
    rowparts = lax.all_to_all(sums, ("c", "z"), 0, 0)
    rowparts, p_came = tie(rowparts, p_came)
    sums = column_pass(expo, rowparts, crops, nx * ny)

    colparts = lax.all_to_all(sums, ("x", "y"), 0, 0)
    *gathered, _ = tie(*gathered, sums)
    wide_expo = wide_teacher_pass(idx, gathered, teacher_protos, crops)
    wide_expo, all_totals = list(wide_expo), list(all_totals)
    colparts, *both = tie(colparts, *wide_expo, *all_totals)
    wide_expo, all_totals = both[:2], both[2:]
    target_mine, target_theirs = target_pass(idx, expo, colparts, student_protos, crops)
    colparts, target_theirs = tie(colparts, target_theirs)
    sums = row_pass(expo, colparts, None, crops, 2 * nz * ny)
    target_came = lax.ppermute(target_theirs, "c", swap)
    keep, send = pack_half_pass(idx, target_mine, target_came, nz, crops)
    sums, send = tie(sums, send)
    rowparts = lax.all_to_all(sums, ("y", "c", "z"), 0, 0)
    came = across(send, nz // 2)
    *gathered, _ = tie(*gathered, sums)
    prob, wnorm, *turned = wide_student_pass(idx, gathered, student_protos, all_totals, crops)
    prob, came = tie(prob, came)
    outgoing = weight_pass(
        idx, prob, wnorm, turned, wide_expo, colparts, rowparts, crops, ny, nx * ny * 2
    )
    parts = lax.all_to_all(outgoing, ("x", "y", "c"), 0, 0)
    proto_grad = proto_pass(idx, parts, student_protos, winv, nx, ny)
    bits = [nz >> k for k in range(2, nz.bit_length()) if nz >> k > (1 if pair else 0)]
    total = mix_pass(
        idx, rowparts, keep, came, p_keep, p_came, nz, ny, crops, bits[0] if bits else 0
    )
    pieces = [total]
    for i, bit in enumerate(bits):
        keep, send = total
        last = i + 1 == len(bits)
        pieces = [keep, across(send, bit)]
        if last and pair:
            pieces += [across(keep, 1), across(send, bit ^ 1)]
        elif not last:
            total = fold_pass(idx, *pieces, bits[i + 1])
    if pair and not bits:
        pieces.append(across(total, 1))
    crop_grad, patch_grad = feature_pass(
        idx, patch_mask, pieces, student_crops, student_patches, nz, patches, pair
    )
    return (proto_grad, crop_grad, patch_grad)


def solution(mesh):
    dp, nz = mesh.devices.shape
    nx = 4 if dp == 32 else 2
    ny = dp // (2 * nx)
    grid = Mesh(mesh.devices.reshape(nx, ny, 2, nz), ("x", "y", "c", "z"))
    rows = ("x", "y", "c")
    in_specs = (
        P(rows, None),
        P(rows, None),
        P(rows, None),
        P(rows, None),
        P(rows, None),
        P(None, "z"),
        P(None, "z"),
    )
    out_specs = (P(rows, "z"), P(rows + ("z",), None), P(rows + ("z",), None))
    return jax.shard_map(
        functools.partial(local, (nx, ny, nz)),
        mesh=grid,
        in_specs=in_specs,
        out_specs=out_specs,
        check_vma=False,
    )
```

```python
import functools

import jax
import jax.numpy as jnp
from jax import lax
from jax.experimental import pallas as pl
from jax.experimental.pallas import tpu as pltpu
from jax.sharding import Mesh, PartitionSpec as P

ITERS = 3
EPS = 1e-06
TEACHER_TEMP = 0.07
STUDENT_TEMP = 0.1
LOSS_SCALE = 256.0
GRAD_SCALE = LOSS_SCALE / STUDENT_TEMP
LOG2E = 1.4426950408889634

BN = 512
F32 = jnp.float32
BF16 = jnp.bfloat16
SMEM = pl.BlockSpec(memory_space=pltpu.SMEM)
VMEM = pl.BlockSpec(memory_space=pltpu.VMEM)
HBM = pl.BlockSpec(memory_space=pltpu.HBM)


def call(kernel, out_shape, args, specs, outs="", scratch=(), flops=0, traffic=0, limit=52):
    spaces = {"s": SMEM, "v": VMEM, "h": HBM}
    if not isinstance(out_shape, list):
        out_specs = VMEM
    else:
        out_specs = [spaces[letter] for letter in outs or "v" * len(out_shape)]
    return pl.pallas_call(
        kernel,
        out_shape=out_shape,
        out_specs=out_specs,
        in_specs=[spaces[letter] for letter in specs],
        scratch_shapes=list(scratch),
        compiler_params=pltpu.CompilerParams(vmem_limit_bytes=limit * 1024 * 1024),
        cost_estimate=pl.CostEstimate(flops=flops, bytes_accessed=traffic, transcendentals=0),
    )(*args)


def array(shape, dtype=F32):
    return jax.ShapeDtypeStruct(shape, dtype)


def stream(source, buf, sem, steps, body):
    def copy(j):
        return pltpu.make_async_copy(source(j), buf.at[j], sem.at[j])

    for j in range(steps):
        copy(j).start()

    def step(j, _):
        copy(j).wait()
        body(j, buf.at[j])
        return 0

    lax.fori_loop(0, steps, step, 0)


def unit(x):
    xf = x.astype(F32)
    return xf * lax.rsqrt(jnp.sum(xf * xf, axis=-1, keepdims=True) + EPS)


def unit_cols(w):
    wf = w.astype(F32)
    inv = lax.rsqrt(jnp.sum(wf * wf, axis=0, keepdims=True) + EPS)
    return wf * inv, inv


def prep_kernel(tcrops, tpatch, scrops, spatch, mask, out, tc, tp, sc, sp, sem):
    images, masked = mask.shape
    patches = tp.shape[0] // images
    count = tc.shape[0]
    half = out.shape[0] // 2
    copies = [
        pltpu.make_async_copy(src, dst, sem.at[i])
        for i, (src, dst) in enumerate(((tcrops, tc), (tpatch, tp), (scrops, sc), (spatch, sp)))
    ]
    for copy in copies:
        copy.start()
    for side, (crops, patch_rows) in enumerate(((tc, tp), (sc, sp))):
        copies[2 * side].wait()
        copies[2 * side + 1].wait()
        base = side * half
        out[base : base + count, :] = unit(crops[...])
        for i in range(images):
            place = lax.broadcasted_iota(jnp.int32, (patches, masked), 0)
            chosen = (place == mask[i : i + 1, :]).astype(F32).astype(BF16)
            rows = lax.dot_general(
                chosen,
                patch_rows[i * patches : (i + 1) * patches, :],
                (((0,), (0,)), ((), ())),
                preferred_element_type=F32,
            )
            at = base + count + i * masked
            out[at : at + masked, :] = unit(rows)


def prep(tcrops, tpatch, scrops, spatch, mask):
    half = tcrops.shape[0] + mask.size
    return call(
        prep_kernel,
        array((2 * half, tcrops.shape[1])),
        [tcrops, tpatch, scrops, spatch, mask],
        "hhhhv",
        limit=58,
        scratch=[pltpu.VMEM(a.shape, BF16) for a in (tcrops, tpatch, scrops, spatch)]
        + [pltpu.SemaphoreType.DMA((4,))],
    )


def place_rows(core, crops, base, half, own, other, dest):
    rest = half - crops
    for side, ref in ((core, own), (1 - core, other)):
        at = pl.multiple_of(side * crops, crops)
        dest[pl.ds(at, crops), :] = ref[base : base + crops, :].astype(dest.dtype)
        at = pl.multiple_of(2 * crops + side * rest, 128)
        dest[pl.ds(at, rest), :] = ref[base + crops : base + half, :].astype(dest.dtype)


def row_blocks(start, stop):
    return [(a, min(a + 256, stop)) for a in range(start, stop, 256)]


def proto_source(core, protos, size=BN):
    columns = protos.shape[1] // 2
    return lambda j: protos.at[:, pl.ds(pl.multiple_of(core * columns + j * size, size), size)]


def proto_scratch(width, columns, size=BN):
    steps = columns // size
    return [pltpu.VMEM((steps, width, size), BF16), pltpu.SemaphoreType.DMA((steps,))]


def put_columns(step, heads, out):
    copies = out.shape[0]
    per_head = out.shape[1] // 2
    for head in range(2):
        for t in range(BN // 128):
            piece = heads[head][:, 128 * t : 128 * (t + 1)]
            out[:, pl.ds(head * per_head + step * (BN // 128) + t, 1), :] = jnp.broadcast_to(
                piece[None], (copies, 1, 128)
            )


def get_columns(step, head, lines):
    base = head * (lines.shape[0] // 2) + step * (BN // 128)
    return jnp.concatenate([lines[pl.ds(base + t, 1), :] for t in range(BN // 128)], axis=1)


def line_up(values):
    return jnp.concatenate([values[t : t + 1, :] for t in range(values.shape[0])], axis=1)


def teacher_kernel(crops, idx, own, other, protos, expo, sums, feats, out, osem, buf, sem):
    rows, columns = expo.shape
    place_rows(idx[0], crops, 0, rows // 2, own, other, feats)
    steps = columns // BN

    def leave(j, slot):
        at = pl.multiple_of(j * BN, BN)
        return pltpu.make_async_copy(out.at[slot], expo.at[:, pl.ds(at, BN)], osem.at[slot])

    def step(j, block):
        w = unit_cols(block[...])[0].astype(BF16)
        slot = lax.rem(j, 4)

        @pl.when(j >= 4)
        def _():
            leave(j - 4, slot).wait()

        heads = []
        for first, last in ((0, 2 * crops), (2 * crops, rows)):
            part = jnp.zeros((1, BN), F32)
            for start, stop in row_blocks(first, last):
                score = jnp.dot(feats[start:stop, :], w, preferred_element_type=F32)
                e = jnp.exp2(score * (LOG2E / TEACHER_TEMP))
                out[slot, start:stop, :] = e.astype(BF16)
                part = part + jnp.sum(e, axis=0, keepdims=True)
            heads.append(part)
        leave(j, slot).start()
        put_columns(j, heads, sums)

    stream(proto_source(idx[0], protos), buf, sem, steps, step)
    for j in range(max(steps - 4, 0), steps):
        leave(j, j % 4).wait()


def teacher_pass(idx, own, other, protos, crops, copies):
    rows, width = own.shape
    columns = protos.shape[1] // 2
    return call(
        functools.partial(teacher_kernel, crops),
        [array((rows, columns), BF16), array((copies, 2 * columns // 128, 128))],
        [idx, own, other, protos],
        "svvh",
        "hv",
        scratch=[
            pltpu.VMEM((rows, width), BF16),
            pltpu.VMEM((4, rows, BN), BF16),
            pltpu.SemaphoreType.DMA((4,)),
        ]
        + proto_scratch(width, columns),
        flops=2 * rows * width * columns,
        traffic=2 * rows * columns,
    )


def student_kernel(crops, idx, own, other, protos, total, mix, feats, acc, buf, sem):
    rows = feats.shape[0]
    size = buf.shape[2]
    place_rows(idx[0], crops, rows // 2, rows // 2, own, other, feats)
    acc[...] = jnp.zeros_like(acc)
    mix[...] = jnp.zeros_like(mix)

    def step(j, block):
        w = unit_cols(block[...])[0].astype(BF16)
        for start, stop in row_blocks(0, rows):
            score = jnp.dot(feats[start:stop, :], w, preferred_element_type=F32)
            p = jnp.exp2(score * (LOG2E / STUDENT_TEMP))
            part = p[:, :128]
            for t in range(1, size // 128):
                part = part + p[:, 128 * t : 128 * (t + 1)]
            acc[start:stop, :] += part
            mix[start:stop, :] += lax.dot_general(
                p.astype(BF16), w, (((1,), (1,)), ((), ())), preferred_element_type=F32
            )

    stream(proto_source(idx[0], protos, size), buf, sem, protos.shape[1] // 2 // size, step)
    for t in range(rows // 128):
        block = jnp.transpose(acc[128 * t : 128 * (t + 1), :])
        total[t : t + 1, :] = jnp.sum(block, axis=0, keepdims=True)


def student_pass(idx, own, other, protos, crops):
    rows, width = own.shape
    columns = protos.shape[1] // 2
    return call(
        functools.partial(student_kernel, crops),
        [array((rows // 128, 128)), array((rows, width))],
        [idx, own, other, protos],
        "svvh",
        scratch=[pltpu.VMEM((rows, width), BF16), pltpu.VMEM((rows, 128), F32)]
        + proto_scratch(width, columns, 2 * BN),
        flops=4 * rows * width * columns,
        traffic=2 * width * columns,
    )


def row_copies(source, dest, sems):
    return [
        pltpu.make_async_copy(
            source.at[pl.ds(128 * i, 128), :], dest.at[pl.ds(128 * i, 128), :], sems.at[i]
        )
        for i in range(source.shape[0] // 128)
    ]


def column_copies(source, dest, sems):
    return [
        pltpu.make_async_copy(
            source.at[:, pl.ds(BN * j, BN)], dest.at[:, pl.ds(BN * j, BN)], sems.at[j]
        )
        for j in range(source.shape[1] // BN)
    ]


def expo_scratch(expo, blocks):
    return [pltpu.VMEM(expo.shape, BF16), pltpu.SemaphoreType.DMA((blocks,))]


def sum_rows(crops, expo, copies_in, colscale, out):
    copies = out.shape[0]
    rows, columns = expo.shape
    per_head = columns // 128

    for i in range(rows // 128):
        copies_in[i].wait()
        head = 0 if i < 2 * crops // 128 else 1
        at = 128 * i

        def chunk(k, acc):
            e = expo[pl.ds(at, 128), pl.ds(pl.multiple_of(k * 128, 128), 128)].astype(F32)
            return acc + e * colscale[pl.ds(head * per_head + k, 1), :]

        acc = lax.fori_loop(0, per_head, chunk, jnp.zeros((128, 128), F32), unroll=8)
        sums = jnp.sum(jnp.transpose(acc), axis=0, keepdims=True)
        out[:, i : i + 1, :] = jnp.broadcast_to(sums[None], (copies, 1, 128))


def row_kernel(crops, extra, expo, colparts, *refs):
    out, colscale, buf, sems = refs[-4:]
    copies_in = row_copies(expo, buf, sems)
    for copy in copies_in:
        copy.start()
    if extra:
        total = refs[0]
        count = total.shape[0]
        out[:, count:, :] = jnp.broadcast_to(total[...][None], (out.shape[0], count, 128))
    colscale[...] = 1.0 / jnp.sum(colparts[...], axis=0)
    sum_rows(crops, buf, copies_in, colscale, out)


def row_pass(expo, colparts, total, crops, copies):
    rows, columns = expo.shape
    extra = total is not None
    return call(
        functools.partial(row_kernel, crops, extra),
        array((copies, rows // 128 * (2 if extra else 1), 128)),
        [expo, colparts] + ([total] if extra else []),
        "hvv" if extra else "hv",
        scratch=[pltpu.VMEM((2 * columns // 128, 128), F32)] + expo_scratch(expo, rows // 128),
        flops=2 * rows * columns,
        traffic=2 * rows * columns,
    )


def target_kernel(crops, idx, expo, colparts, protos, mine, theirs, target, colscale, ebuf, esem, buf, sem):
    rows, columns = expo.shape
    steps = columns // BN
    copies_in = column_copies(expo, ebuf, esem)
    for copy in copies_in:
        copy.start()
    colscale[...] = 1.0 / jnp.sum(colparts[...], axis=0)
    target[...] = jnp.zeros_like(target)

    def step(j, block):
        wnorm = unit_cols(block[...])[0]
        at = pl.multiple_of(j * BN, BN)
        pltpu.make_async_copy(
            expo.at[:, pl.ds(at, BN)], ebuf.at[:, pl.ds(at, BN)], esem.at[j]
        ).wait()
        for head, (first, last) in enumerate(((0, 2 * crops), (2 * crops, rows))):
            w = (wnorm * get_columns(j, head, colscale)).astype(BF16)
            target[first:last, :] += lax.dot_general(
                ebuf[first:last, pl.ds(at, BN)],
                w,
                (((1,), (1,)), ((), ())),
                preferred_element_type=F32,
            )

    stream(proto_source(idx[0], protos), buf, sem, steps, step)
    part_rows(crops, idx, target, mine, theirs)


def target_pass(idx, expo, colparts, protos, crops):
    rows, columns = expo.shape
    width = protos.shape[0]
    return call(
        functools.partial(target_kernel, crops),
        [array((rows // 2, width)), array((rows // 2, width))],
        [idx, expo, colparts, protos],
        "shvh",
        scratch=[pltpu.VMEM((rows, width), F32), pltpu.VMEM((2 * columns // 128, 128), F32)]
        + expo_scratch(expo, columns // BN)
        + proto_scratch(width, columns),
        flops=2 * rows * columns * width,
        traffic=2 * rows * columns,
    )


def split3(v):
    high = v.astype(BF16)
    rest = v - high.astype(F32)
    middle = rest.astype(BF16)
    low = (rest - middle.astype(F32)).astype(BF16)
    pad = jnp.zeros((13, v.shape[1]), F32)
    parts = [high.astype(F32), middle.astype(F32), low.astype(F32), pad]
    return jnp.concatenate(parts, axis=0).astype(BF16)


def column_kernel(crops, expo, rowparts, out, buf, sems):
    rows, columns = expo.shape
    copies_in = column_copies(expo, buf, sems)
    for copy in copies_in:
        copy.start()
    scale = line_up(1.0 / jnp.sum(rowparts[:, : rows // 128, :], axis=0))
    spans = [(0, 2 * crops), (2 * crops, rows)]
    lefts = [split3(scale[:, first:last]) for first, last in spans]
    for j in range(columns // BN):
        copies_in[j].wait()
        heads = []
        for left, (first, last) in zip(lefts, spans):
            sums = jnp.dot(
                left, buf[first:last, j * BN : (j + 1) * BN], preferred_element_type=F32
            )
            heads.append(sums[0:1, :] + sums[1:2, :] + sums[2:3, :])
        put_columns(j, heads, out)


def column_pass(expo, rowparts, crops, copies):
    rows, columns = expo.shape
    return call(
        functools.partial(column_kernel, crops),
        array((copies, 2 * columns // 128, 128)),
        [expo, rowparts],
        "hv",
        scratch=expo_scratch(expo, columns // BN),
        flops=2 * rows * columns,
        traffic=2 * rows * columns,
    )


def part_source(idx, ny, protos):
    columns = protos.shape[1] // 2
    part = columns // ny
    at = pl.multiple_of(idx[0] * columns + idx[3] * part, 128)
    return protos.at[:, pl.ds(at, part)]


def stream_rows(ny, here, base, half, refs, buf, sem, ready, body):
    copies = [
        pltpu.make_async_copy(ref.at[pl.ds(base, half), :], buf.at[i], sem.at[i])
        for i, ref in enumerate(refs)
    ]
    for copy in copies:
        copy.start()
    ready()
    for i, copy in enumerate(copies):
        copy.wait()
        body(i // ny, lax.rem(here + ny - i % ny, ny), buf.at[i])


def wide_teacher_kernel(ny, crops, idx, protos, *refs):
    expo_d, expo_i, w, wbuf, out, osem, buf, sem, wsem = refs[2 * ny :]
    half = buf.shape[1]
    rest = half - crops
    fetch = pltpu.make_async_copy(part_source(idx, ny, protos), wbuf, wsem)
    fetch.start()
    leaving = []

    def ready():
        fetch.wait()
        w[...] = unit_cols(wbuf[...])[0].astype(BF16)

    def body(side, y, ref):
        place = 2 * y + jnp.where(idx[0] == side, 0, 1)
        slot = len(leaving) % 4
        if len(leaving) >= 4:
            for copy in leaving[-4]:
                copy.wait()
        feats = ref[...].astype(BF16)
        for start, stop in row_blocks(0, half):
            score = jnp.dot(feats[start:stop, :], w[...], preferred_element_type=F32)
            out[slot, start:stop, :] = jnp.exp2(score * (LOG2E / TEACHER_TEMP)).astype(BF16)
        at_d = pl.multiple_of(place * crops, 128)
        at_i = pl.multiple_of(place * rest, 128)
        copies = (
            pltpu.make_async_copy(
                out.at[slot, pl.ds(0, crops), :], expo_d.at[pl.ds(at_d, crops), :], osem.at[slot, 0]
            ),
            pltpu.make_async_copy(
                out.at[slot, pl.ds(crops, rest), :], expo_i.at[pl.ds(at_i, rest), :], osem.at[slot, 1]
            ),
        )
        for copy in copies:
            copy.start()
        leaving.append(copies)

    stream_rows(ny, idx[3], 0, half, refs[: 2 * ny], buf, sem, ready, body)
    for copies in leaving[-4:]:
        for copy in copies:
            copy.wait()


def wide_teacher_pass(idx, gathered, protos, crops):
    ny = len(gathered) // 2
    rows, width = gathered[0].shape
    half = rows // 2
    part = protos.shape[1] // 2 // ny
    return call(
        functools.partial(wide_teacher_kernel, ny, crops),
        [array((2 * ny * crops, part), BF16), array((2 * ny * (half - crops), part), BF16)],
        [idx, protos, *gathered],
        "sh" + "h" * len(gathered),
        "hh",
        scratch=[
            pltpu.VMEM((width, part), BF16),
            pltpu.VMEM((width, part), BF16),
            pltpu.VMEM((4, half, part), BF16),
            pltpu.SemaphoreType.DMA((4, 2)),
            pltpu.VMEM((2 * ny, half, width), F32),
            pltpu.SemaphoreType.DMA((2 * ny,)),
            pltpu.SemaphoreType.DMA,
        ],
        flops=2 * 2 * ny * half * width * part,
        traffic=8 * ny * half * width,
    )


def wide_student_kernel(ny, crops, idx, protos, *refs):
    gathered = refs[: 2 * ny]
    refs = refs[2 * ny :]
    totals = refs[:ny]
    out, wnorm_out, turned_d, turned_i, w, wbuf, scale, left, expo, buf, sem, wsem = refs[ny:]
    half = buf.shape[1]
    rest = half - crops
    sub = totals[0].shape[0]
    fetch = pltpu.make_async_copy(part_source(idx, ny, protos), wbuf, wsem)
    fetch.start()
    for s in range(ny):
        y = lax.rem(idx[3] + ny - s, ny)
        scale[pl.ds(pl.multiple_of(y * sub, sub), sub), :] = GRAD_SCALE / totals[s][...]
    out[...] = jnp.zeros_like(out)

    def ready():
        fetch.wait()
        wnorm_out[...] = unit_cols(wbuf[...])[0]
        w[...] = wnorm_out[...].astype(BF16)

    def body(side, y, ref):
        core = jnp.where(idx[0] == side, 0, 1)
        place = 2 * y + core
        feats = ref[...].astype(BF16)
        turned = jnp.transpose(feats.astype(F32))
        turned_d[:, pl.ds(pl.multiple_of(place * crops, 128), crops)] = turned[:, :crops].astype(BF16)
        turned_i[:, pl.ds(pl.multiple_of(place * rest, 128), rest)] = turned[:, crops:].astype(BF16)
        lines = [scale[pl.ds(y * sub + core * (crops // 128) + t, 1), :] for t in range(crops // 128)]
        first = y * sub + 2 * crops // 128 + core * (rest // 128)
        lines += [scale[pl.ds(first + t, 1), :] for t in range(rest // 128)]
        left[...] = (turned * jnp.concatenate(lines, axis=1)).astype(BF16)
        for start, stop in row_blocks(0, half):
            score = jnp.dot(feats[start:stop, :], w[...], preferred_element_type=F32)
            expo[start:stop, :] = jnp.exp2(score * (LOG2E / STUDENT_TEMP)).astype(BF16)
        out[...] += jnp.dot(left[...], expo[...], preferred_element_type=F32)

    stream_rows(ny, idx[3], half, half, gathered, buf, sem, ready, body)


def wide_student_pass(idx, gathered, protos, totals, crops):
    ny = len(gathered) // 2
    rows, width = gathered[0].shape
    half = rows // 2
    part = protos.shape[1] // 2 // ny
    return call(
        functools.partial(wide_student_kernel, ny, crops),
        [
            array((width, part)),
            array((width, part)),
            array((width, 2 * ny * crops), BF16),
            array((width, 2 * ny * (half - crops)), BF16),
        ],
        [idx, protos, *gathered, *totals],
        "sh" + "h" * len(gathered) + "v" * ny,
        scratch=[
            pltpu.VMEM((width, part), BF16),
            pltpu.VMEM((width, part), BF16),
            pltpu.VMEM((ny * rows // 128, 128), F32),
            pltpu.VMEM((width, half), BF16),
            pltpu.VMEM((half, part), BF16),
            pltpu.VMEM((2 * ny, half, width), F32),
            pltpu.SemaphoreType.DMA((2 * ny,)),
            pltpu.SemaphoreType.DMA,
        ],
        flops=4 * 2 * ny * half * width * part,
        traffic=8 * ny * half * width,
    )


def weight_kernel(ny, crops, idx, prob_in, wnorm_in, turned_d_in, turned_i_in, expo_d, expo_i, colparts, rowparts, out, left_d, left_i, scales, rowscale, buf_d, buf_i, sems_d, sems_i, targets, prob, wnorm, turned_d, turned_i, sem):
    loads = [
        pltpu.make_async_copy(src, dst, sem.at[i])
        for i, (src, dst) in enumerate(
            ((turned_d_in, turned_d), (turned_i_in, turned_i), (prob_in, prob), (wnorm_in, wnorm))
        )
    ]
    for copy in loads[:2]:
        copy.start()
    copies, _, _ = out.shape
    width, part = prob.shape
    own = width // copies
    streams = []
    for expo, buf, sems in ((expo_d, buf_d, sems_d), (expo_i, buf_i, sems_i)):
        size = buf.shape[0] // sems.shape[0]
        streams.append(
            [
                pltpu.make_async_copy(
                    expo.at[pl.ds(i * size, size), :], buf.at[pl.ds(i * size, size), :], sems.at[i]
                )
                for i in range(sems.shape[0])
            ]
        )
    for copy in streams[0] + streams[1] + loads[2:]:
        copy.start()
    group = rowparts.shape[0] // ny
    sub = rowparts.shape[1]
    scales[...] = GRAD_SCALE / jnp.sum(colparts[...], axis=0)
    for y in range(ny):
        rowscale[y * sub : (y + 1) * sub, :] = 1.0 / jnp.sum(
            rowparts[y * group : (y + 1) * group], axis=0
        )
    cd = crops // 128
    ci = sub // 2 - cd
    lines_d, lines_i = [], []
    for y in range(ny):
        for core in range(2):
            for t in range(cd):
                at = y * sub + core * cd + t
                lines_d.append(rowscale[at : at + 1, :])
            for t in range(ci):
                at = y * sub + 2 * cd + core * ci + t
                lines_i.append(rowscale[at : at + 1, :])
    loads[0].wait()
    loads[1].wait()
    left_d[...] = (turned_d[...].astype(F32) * jnp.concatenate(lines_d, axis=1)).astype(BF16)
    left_i[...] = (turned_i[...].astype(F32) * jnp.concatenate(lines_i, axis=1)).astype(BF16)
    per_head = scales.shape[0] // 2
    first = idx[3] * (part // 128)
    for head, (left, buf) in enumerate(((left_d, buf_d), (left_i, buf_i))):
        size = buf.shape[0] // len(streams[head])
        for i, copy in enumerate(streams[head]):
            copy.wait()
            span = slice(i * size, (i + 1) * size)
            value = jnp.dot(left[:, span], buf[span, :], preferred_element_type=F32)
            if i == 0:
                targets[head] = value
            else:
                targets[head] += value
    loads[2].wait()
    loads[3].wait()
    for at in range(0, part, BN):
        span = slice(at, at + BN)
        wsum = prob[:, span]
        for head in range(2):
            base = head * per_head + first + at // 128
            line = [scales[pl.ds(base + t, 1), :] for t in range(BN // 128)]
            wsum = wsum - targets[head, :, span] * jnp.concatenate(line, axis=1)
        coldot = jnp.sum(wnorm[:, span] * wsum, axis=0, keepdims=True)
        for t in range(BN // 128):
            lanes = slice(128 * t, 128 * (t + 1))
            row = at // 128 + t
            for d in range(copies):
                out[d, row * own : (row + 1) * own, :] = wsum[d * own : (d + 1) * own, lanes]
            tail = part // 128 * own + row
            out[:, tail : tail + 1, :] = jnp.broadcast_to(
                coldot[:, lanes][None], (copies, 1, 128)
            )


def weight_pass(idx, prob, wnorm, turned, expo, colparts, rowparts, crops, ny, copies):
    width, part = prob.shape
    lines = part // 128 * (width // copies + 1)
    rows = turned[0].shape[1] + turned[1].shape[1]
    return call(
        functools.partial(weight_kernel, ny, crops),
        array((copies, lines, 128)),
        [idx, prob, wnorm, *turned, *expo, colparts, rowparts],
        "shhhhhhvv",
        scratch=[
            pltpu.VMEM(turned[0].shape, BF16),
            pltpu.VMEM(turned[1].shape, BF16),
            pltpu.VMEM(colparts.shape[1:], F32),
            pltpu.VMEM((ny * rowparts.shape[1], 128), F32),
            pltpu.VMEM(expo[0].shape, BF16),
            pltpu.VMEM(expo[1].shape, BF16),
            pltpu.SemaphoreType.DMA((expo[0].shape[0] // 512,)),
            pltpu.SemaphoreType.DMA((expo[1].shape[0] // 512,)),
            pltpu.VMEM((2, width, part), F32),
            pltpu.VMEM((width, part), F32),
            pltpu.VMEM((width, part), F32),
            pltpu.VMEM(turned[0].shape, BF16),
            pltpu.VMEM(turned[1].shape, BF16),
            pltpu.SemaphoreType.DMA((4,)),
        ],
        flops=2 * rows * width * part,
        traffic=2 * rows * part,
    )


def norm_kernel(protos, out, buf, sem):
    blocks, size, _ = buf.shape
    copies = [
        pltpu.make_async_copy(protos.at[pl.ds(i * size, size), :], buf.at[i], sem.at[i])
        for i in range(blocks)
    ]
    for copy in copies:
        copy.start()
    for i, copy in enumerate(copies):
        copy.wait()
        w = buf[i].astype(F32)
        part = jnp.sum(w * w, axis=0, keepdims=True)
        out[...] = part if i == 0 else out[...] + part
    out[...] = lax.rsqrt(out[...] + EPS)


def norm_pass(protos):
    width, columns = protos.shape
    return call(
        norm_kernel,
        array((1, columns)),
        [protos],
        "h",
        scratch=[pltpu.VMEM((8, width // 8, columns), BF16), pltpu.SemaphoreType.DMA((8,))],
        flops=3 * width * columns,
        traffic=2 * width * columns,
    )


def proto_kernel(nx, ny, idx, parts, protos, winv, out, rows, sem):
    own, columns = out.shape
    copies = parts.shape[0]
    part = columns // (2 * ny)
    tail = part // 128 * own
    at = pl.multiple_of(idx[2] * (2 * own), 2 * own)
    fetch = pltpu.make_async_copy(protos.at[pl.ds(at, 2 * own), :], rows, sem)
    fetch.start()
    fetch.wait()
    for y in range(ny):
        for core in range(2):
            for t in range(part // 128):
                first = core * (columns // 2) + y * part + 128 * t
                lanes = slice(first, first + 128)
                wsum = jnp.zeros((own, 128), F32)
                coldot = jnp.zeros((1, 128), F32)
                for x in range(nx):
                    source = (x * ny + y) * 2 + core
                    wsum = wsum + parts[source, t * own : (t + 1) * own, :]
                    coldot = coldot + parts[source, tail + t : tail + t + 1, :]
                inv = winv[:, lanes]
                both = rows[:, lanes].astype(F32)
                wnorm = jnp.where(idx[0] == 0, both[:own, :], both[own:, :]) * inv
                out[:, lanes] = (wsum - wnorm * coldot) * inv


def proto_pass(idx, parts, protos, winv, nx, ny):
    width, columns = protos.shape
    own = width // parts.shape[0]
    return call(
        functools.partial(proto_kernel, nx, ny),
        array((own, columns)),
        [idx, parts, protos, winv],
        "svhv",
        scratch=[pltpu.VMEM((2 * own, columns), BF16), pltpu.SemaphoreType.DMA],
    )


def spread_row(line):
    return jnp.transpose(jnp.broadcast_to(line, (128, 128)))


def scaled_kernel(crops, idx, mix, totals, mine, theirs, buf):
    rows, width = mix.shape
    prob = GRAD_SCALE / totals[...]
    for t in range(rows // 128):
        span = slice(128 * t, 128 * (t + 1))
        p = jnp.concatenate([spread_row(prob[t : t + 1, :])] * (width // 128), axis=1)
        buf[span, :] = mix[span, :] * p
    part_rows(crops, idx, buf, mine, theirs)


def part_rows(crops, idx, buf, mine, theirs):
    rest = mine.shape[0] - crops
    for side, ref in ((idx[0], mine), (1 - idx[0], theirs)):
        ref[:crops, :] = buf[pl.ds(pl.multiple_of(side * crops, crops), crops), :]
        ref[crops:, :] = buf[pl.ds(pl.multiple_of(2 * crops + side * rest, 128), rest), :]


def part_pass(idx, mix, totals, crops):
    rows, width = mix.shape
    return call(
        functools.partial(scaled_kernel, crops),
        [array((rows // 2, width)), array((rows // 2, width))],
        [idx, mix, totals],
        "svv",
        scratch=[pltpu.VMEM((rows, width), F32)],
    )


def pack_rows(nz, crops, mine, came, out):
    half = mine.shape[0]
    chunk = half // nz
    share = crops // nz
    rest = chunk - share
    for z in range(nz):
        for src, dst, size in ((z * share, z * chunk, share), (crops + z * rest, z * chunk + share, rest)):
            out[dst : dst + size, :] = mine[src : src + size, :] + came[src : src + size, :]


def halve(idx, bit, total, keep, send):
    size = total.shape[0] // 2
    side = lax.rem(idx[1] // bit, 2)
    keep[...] = total[pl.ds(pl.multiple_of(side * size, 64), size), :]
    send[...] = total[pl.ds(pl.multiple_of((1 - side) * size, 64), size), :]


def pack_half_kernel(nz, crops, idx, mine, came, keep, send, total):
    pack_rows(nz, crops, mine, came, total)
    halve(idx, nz // 2, total, keep, send)


def pack_half_pass(idx, mine, came, nz, crops):
    rows, width = mine.shape
    return call(
        functools.partial(pack_half_kernel, nz, crops),
        [array((rows // 2, width)), array((rows // 2, width))],
        [idx, mine, came],
        "svv",
        scratch=[pltpu.VMEM((rows, width), F32)],
    )


def fold_kernel(bit, idx, mine, came, keep, send, total):
    total[...] = mine[...] + came[...]
    halve(idx, bit, total, keep, send)


def fold_pass(idx, mine, came, bit):
    rows, width = mine.shape
    return call(
        functools.partial(fold_kernel, bit),
        [array((rows // 2, width)), array((rows // 2, width))],
        [idx, mine, came],
        "svv",
        scratch=[pltpu.VMEM((rows, width), F32)],
    )


def mix_kernel(nz, ny, crops, bit, idx, rowparts, target, target_came, prob, prob_came, *refs):
    scale = refs[-1]
    total = refs[-2]
    sub = rowparts.shape[1]
    group = rowparts.shape[0] // ny
    cd = crops // 128
    ci = sub // 2 - cd
    row = GRAD_SCALE / jnp.sum(rowparts[pl.ds(idx[3] * group, group), :, :], axis=0)
    low = idx[0] == 0
    for t in range(cd + ci):
        a, b = (t, cd + t) if t < cd else (cd + t, cd + ci + t)
        line = jnp.where(low, row[a : a + 1, :], row[b : b + 1, :])
        scale[128 * t : 128 * (t + 1), :] = spread_row(line)
    rows, width = target.shape
    here = nz // 2
    chunk = rows // here
    share = crops // nz
    rest = chunk - share
    first = idx[1] // here * here
    for k in range(here):
        z = first + k
        for at, src, size in ((0, z * share, share), (share, crops + z * rest, rest)):
            r = scale[pl.ds(pl.multiple_of(src, 16), size), :]
            span = slice(k * chunk + at, k * chunk + at + size)
            value = target[span, :] + target_came[span, :]
            total[span, :] = (
                prob[span, :]
                + prob_came[span, :]
                - value * jnp.concatenate([r] * (width // 128), axis=1)
            )
    if bit:
        halve(idx, bit, total, refs[0], refs[1])


def mix_pass(idx, rowparts, target, target_came, prob, prob_came, nz, ny, crops, bit):
    rows, width = target.shape
    half = rowparts.shape[1] // 2 * 128
    shapes = [array((rows // 2, width))] * 2 if bit else array((rows, width))
    return call(
        functools.partial(mix_kernel, nz, ny, crops, bit),
        shapes,
        [idx, rowparts, target, target_came, prob, prob_came],
        "svvvvv",
        scratch=([pltpu.VMEM((rows, width), F32)] if bit else []) + [pltpu.VMEM((half, 128), F32)],
    )


def feature_kernel(count, chunks, patches, idx, mask, *refs):
    pieces = refs[:count]
    all_crops, all_rows, crop_out, patch_out, masked_rows, dense, total = refs[count:]
    z = idx[1]
    masked = mask.shape[1]
    crop_share = crop_out.shape[0]
    share = patch_out.shape[0]
    value = pieces[0][...]
    for piece in pieces[1:]:
        value = value + piece[...]
    total[...] = value
    chunk = total.shape[0] // chunks
    rest = chunk - crop_share
    for side in range(chunks):
        masked_rows[side * rest : (side + 1) * rest, :] = total[
            side * chunk + crop_share : (side + 1) * chunk, :
        ]
    crop_at = pl.multiple_of(z * crop_share, 16)
    patch_at = pl.multiple_of(z * share, 128)
    start = pl.multiple_of(lax.rem(z, chunks) * chunk, 16)
    dense[...] = jnp.zeros_like(dense)
    first_row = z * share
    first_image = first_row // patches
    offset = first_row - first_image * patches
    for image in range(masked_rows.shape[0] // masked):

        def put(m, _):
            at = mask[first_image + image, m] + image * patches - offset

            @pl.when(jnp.logical_and(at >= 0, at < share))
            def _():
                dense[pl.ds(at, 1), :] = masked_rows[pl.ds(image * masked + m, 1), :]

            return 0

        lax.fori_loop(0, masked, put, 0, unroll=4)

    def back(x, d):
        xf = x.astype(F32)
        inv = lax.rsqrt(jnp.sum(xf * xf, axis=-1, keepdims=True) + EPS)
        u = xf * inv
        return (d - u * jnp.sum(u * d, axis=-1, keepdims=True)) * inv

    crop_out[...] = back(all_crops[pl.ds(crop_at, crop_share), :], total[pl.ds(start, crop_share), :])
    patch_out[...] = back(all_rows[pl.ds(patch_at, share), :], dense[...])


def feature_pass(idx, mask, pieces, all_crops, all_rows, nz, patches, pair):
    crops, width = all_crops.shape
    crop_share = crops // nz
    share = all_rows.shape[0] // nz
    rows = pieces[0].shape[0]
    return call(
        functools.partial(feature_kernel, len(pieces), 2 if pair else 1, patches),
        [array((crop_share, width)), array((share, width))],
        [idx, mask, *pieces, all_crops, all_rows],
        "ss" + "v" * len(pieces) + "vv",
        scratch=[
            pltpu.VMEM((rows - (2 if pair else 1) * crop_share, width), F32),
            pltpu.VMEM((share, width), F32),
            pltpu.VMEM((rows, width), F32),
        ],
    )


def tie(*values):
    return lax.optimization_barrier(values)


def shifted(n, s):
    return [(i, (i + s) % n) for i in range(n)]


def local(
    sizes,
    student_crops,
    teacher_crops,
    student_patches,
    teacher_patches,
    patch_mask,
    student_protos,
    teacher_protos,
):
    nx, ny, nz = sizes
    images, masked = patch_mask.shape
    patches = student_patches.shape[0] // images
    crops = student_crops.shape[0]
    ix, iy, ic, iz = (lax.axis_index(a) for a in ("x", "y", "c", "z"))
    idx = jnp.stack([ic, iz, ix * ny + iy, iy]).astype(jnp.int32)
    swap = [(0, 1), (1, 0)]

    own = prep(teacher_crops, teacher_patches, student_crops, student_patches, patch_mask)
    other = lax.ppermute(own, "c", swap)
    up, down = shifted(ny, 1), shifted(ny, ny - 1)
    from_up = lax.ppermute(own, "y", up)
    from_down = lax.ppermute(own, "y", down) if ny > 2 else None
    expo, sums = teacher_pass(idx, own, other, teacher_protos, crops, nx * ny)
    sub = 2 * (crops + images * masked) // 128

    pair = student_patches.shape[0] // nz < patches

    def across(value, bit):
        return lax.ppermute(value, "z", [(i, i ^ bit) for i in range(nz)])

    colparts = lax.all_to_all(sums, ("x", "y"), 0, 0)
    total, mix = student_pass(idx, own, other, student_protos, crops)
    colparts, total, from_up, from_down = tie(colparts, total, from_up, from_down)
    ring = [own, from_up]
    while len(ring) < ny - 1:
        ring.append(lax.ppermute(ring[-1], "y", up))
    if ny > 2:
        ring.append(from_down)
    sums = row_pass(expo, colparts, total, crops, 2 * nz)
    rowparts = lax.all_to_all(sums, ("c", "z"), 0, 0)
    later_protos, _ = tie(student_protos, sums)
    winv = norm_pass(later_protos)
    rowparts, winv = tie(rowparts, winv)
    totals = jnp.sum(rowparts[:, sub:, :], axis=0)
    sums = column_pass(expo, rowparts, crops, nx * ny)

    colparts = lax.all_to_all(sums, ("x", "y"), 0, 0)
    totals, _ = tie(totals, sums)
    all_totals = [totals] + [lax.ppermute(totals, "y", shifted(ny, s)) for s in range(1, ny)]
    mine, theirs = part_pass(idx, mix, totals, crops)
    p_keep, p_send = pack_half_pass(idx, mine, lax.ppermute(theirs, "c", swap), nz, crops)
    p_came = across(p_send, nz // 2)
    colparts, p_came = tie(colparts, p_came)
    sums = row_pass(expo, colparts, None, crops, 2 * nz)
    sums, *ring = tie(sums, *ring)
    gathered = ring + [other] + [lax.ppermute(rows, "c", swap) for rows in ring[1:]]
    rowparts = lax.all_to_all(sums, ("c", "z"), 0, 0)
    sums = column_pass(expo, rowparts, crops, nx * ny)

    colparts = lax.all_to_all(sums, ("x", "y"), 0, 0)
    *gathered, _ = tie(*gathered, sums)
    wide_expo = wide_teacher_pass(idx, gathered, teacher_protos, crops)
    wide_expo, all_totals = list(wide_expo), list(all_totals)
    colparts, *both = tie(colparts, *wide_expo, *all_totals)
    wide_expo, all_totals = both[:2], both[2:]
    target_mine, target_theirs = target_pass(idx, expo, colparts, student_protos, crops)
    colparts, target_theirs = tie(colparts, target_theirs)
    sums = row_pass(expo, colparts, None, crops, 2 * nz * ny)
    target_came = lax.ppermute(target_theirs, "c", swap)
    keep, send = pack_half_pass(idx, target_mine, target_came, nz, crops)
    sums, send = tie(sums, send)
    rowparts = lax.all_to_all(sums, ("y", "c", "z"), 0, 0)
    came = across(send, nz // 2)
    *gathered, _ = tie(*gathered, sums)
    prob, wnorm, *turned = wide_student_pass(idx, gathered, student_protos, all_totals, crops)
    prob, came = tie(prob, came)
    outgoing = weight_pass(
        idx, prob, wnorm, turned, wide_expo, colparts, rowparts, crops, ny, nx * ny * 2
    )
    parts = lax.all_to_all(outgoing, ("x", "y", "c"), 0, 0)
    proto_grad = proto_pass(idx, parts, student_protos, winv, nx, ny)
    bits = [nz >> k for k in range(2, nz.bit_length()) if nz >> k > (1 if pair else 0)]
    total = mix_pass(
        idx, rowparts, keep, came, p_keep, p_came, nz, ny, crops, bits[0] if bits else 0
    )
    pieces = [total]
    for i, bit in enumerate(bits):
        keep, send = total
        last = i + 1 == len(bits)
        pieces = [keep, across(send, bit)]
        if last and pair:
            pieces += [across(keep, 1), across(send, bit ^ 1)]
        elif not last:
            total = fold_pass(idx, *pieces, bits[i + 1])
    if pair and not bits:
        pieces.append(across(total, 1))
    crop_grad, patch_grad = feature_pass(
        idx, patch_mask, pieces, student_crops, student_patches, nz, patches, pair
    )
    return (proto_grad, crop_grad, patch_grad)


def solution(mesh):
    dp, nz = mesh.devices.shape
    nx = 4 if dp == 32 else 2
    ny = dp // (2 * nx)
    grid = Mesh(mesh.devices.reshape(nx, ny, 2, nz), ("x", "y", "c", "z"))
    rows = ("x", "y", "c")
    in_specs = (
        P(rows, None),
        P(rows, None),
        P(rows, None),
        P(rows, None),
        P(rows, None),
        P(None, "z"),
        P(None, "z"),
    )
    out_specs = (P(rows, "z"), P(rows + ("z",), None), P(rows + ("z",), None))
    return jax.shard_map(
        functools.partial(local, (nx, ny, nz)),
        mesh=grid,
        in_specs=in_specs,
        out_specs=out_specs,
        check_vma=False,
    )
```

```python
import functools

import jax
import jax.numpy as jnp
from jax import lax
from jax.experimental import pallas as pl
from jax.experimental.pallas import tpu as pltpu
from jax.sharding import Mesh, PartitionSpec as P

ITERS = 3
EPS = 1e-06
TEACHER_TEMP = 0.07
STUDENT_TEMP = 0.1
LOSS_SCALE = 256.0
GRAD_SCALE = LOSS_SCALE / STUDENT_TEMP
LOG2E = 1.4426950408889634

BN = 512
F32 = jnp.float32
BF16 = jnp.bfloat16
SMEM = pl.BlockSpec(memory_space=pltpu.SMEM)
VMEM = pl.BlockSpec(memory_space=pltpu.VMEM)
HBM = pl.BlockSpec(memory_space=pltpu.HBM)


def call(kernel, out_shape, args, specs, outs="", scratch=(), flops=0, traffic=0, limit=52):
    spaces = {"s": SMEM, "v": VMEM, "h": HBM}
    if not isinstance(out_shape, list):
        out_specs = VMEM
    else:
        out_specs = [spaces[letter] for letter in outs or "v" * len(out_shape)]
    return pl.pallas_call(
        kernel,
        out_shape=out_shape,
        out_specs=out_specs,
        in_specs=[spaces[letter] for letter in specs],
        scratch_shapes=list(scratch),
        compiler_params=pltpu.CompilerParams(vmem_limit_bytes=limit * 1024 * 1024),
        cost_estimate=pl.CostEstimate(flops=flops, bytes_accessed=traffic, transcendentals=0),
    )(*args)


def array(shape, dtype=F32):
    return jax.ShapeDtypeStruct(shape, dtype)


def stream(source, buf, sem, steps, body):
    def copy(j):
        return pltpu.make_async_copy(source(j), buf.at[j], sem.at[j])

    for j in range(steps):
        copy(j).start()

    def step(j, _):
        copy(j).wait()
        body(j, buf.at[j])
        return 0

    lax.fori_loop(0, steps, step, 0)


def unit(x):
    xf = x.astype(F32)
    return xf * lax.rsqrt(jnp.sum(xf * xf, axis=-1, keepdims=True) + EPS)


def unit_cols(w):
    wf = w.astype(F32)
    inv = lax.rsqrt(jnp.sum(wf * wf, axis=0, keepdims=True) + EPS)
    return wf * inv, inv


def prep_kernel(tcrops, tpatch, scrops, spatch, mask, out, tc, tp, sc, sp, sem):
    images, masked = mask.shape
    patches = tp.shape[0] // images
    count = tc.shape[0]
    half = out.shape[0] // 2
    copies = [
        pltpu.make_async_copy(src, dst, sem.at[i])
        for i, (src, dst) in enumerate(((tcrops, tc), (tpatch, tp), (scrops, sc), (spatch, sp)))
    ]
    for copy in copies:
        copy.start()
    for side, (crops, patch_rows) in enumerate(((tc, tp), (sc, sp))):
        copies[2 * side].wait()
        copies[2 * side + 1].wait()
        base = side * half
        out[base : base + count, :] = unit(crops[...])
        for i in range(images):
            place = lax.broadcasted_iota(jnp.int32, (patches, masked), 0)
            chosen = (place == mask[i : i + 1, :]).astype(F32).astype(BF16)
            rows = lax.dot_general(
                chosen,
                patch_rows[i * patches : (i + 1) * patches, :],
                (((0,), (0,)), ((), ())),
                preferred_element_type=F32,
            )
            at = base + count + i * masked
            out[at : at + masked, :] = unit(rows)


def prep(tcrops, tpatch, scrops, spatch, mask):
    half = tcrops.shape[0] + mask.size
    return call(
        prep_kernel,
        array((2 * half, tcrops.shape[1])),
        [tcrops, tpatch, scrops, spatch, mask],
        "hhhhv",
        limit=58,
        scratch=[pltpu.VMEM(a.shape, BF16) for a in (tcrops, tpatch, scrops, spatch)]
        + [pltpu.SemaphoreType.DMA((4,))],
    )


def place_rows(core, crops, base, half, own, other, dest):
    rest = half - crops
    for side, ref in ((core, own), (1 - core, other)):
        at = pl.multiple_of(side * crops, crops)
        dest[pl.ds(at, crops), :] = ref[base : base + crops, :].astype(dest.dtype)
        at = pl.multiple_of(2 * crops + side * rest, 128)
        dest[pl.ds(at, rest), :] = ref[base + crops : base + half, :].astype(dest.dtype)


def row_blocks(start, stop):
    return [(a, min(a + 256, stop)) for a in range(start, stop, 256)]


def proto_source(core, protos, size=BN):
    columns = protos.shape[1] // 2
    return lambda j: protos.at[:, pl.ds(pl.multiple_of(core * columns + j * size, size), size)]


def proto_scratch(width, columns, size=BN):
    steps = columns // size
    return [pltpu.VMEM((steps, width, size), BF16), pltpu.SemaphoreType.DMA((steps,))]


def put_columns(step, heads, out):
    copies = out.shape[0]
    per_head = out.shape[1] // 2
    for head in range(2):
        for t in range(BN // 128):
            piece = heads[head][:, 128 * t : 128 * (t + 1)]
            out[:, pl.ds(head * per_head + step * (BN // 128) + t, 1), :] = jnp.broadcast_to(
                piece[None], (copies, 1, 128)
            )


def get_columns(step, head, lines):
    base = head * (lines.shape[0] // 2) + step * (BN // 128)
    return jnp.concatenate([lines[pl.ds(base + t, 1), :] for t in range(BN // 128)], axis=1)


def line_up(values):
    return jnp.concatenate([values[t : t + 1, :] for t in range(values.shape[0])], axis=1)


def teacher_kernel(crops, idx, own, other, protos, expo, sums, feats, out, osem, buf, sem):
    rows, columns = expo.shape
    place_rows(idx[0], crops, 0, rows // 2, own, other, feats)
    steps = columns // BN

    def leave(j, slot):
        at = pl.multiple_of(j * BN, BN)
        return pltpu.make_async_copy(out.at[slot], expo.at[:, pl.ds(at, BN)], osem.at[slot])

    def step(j, block):
        w = unit_cols(block[...])[0].astype(BF16)
        slot = lax.rem(j, 4)

        @pl.when(j >= 4)
        def _():
            leave(j - 4, slot).wait()

        heads = []
        for first, last in ((0, 2 * crops), (2 * crops, rows)):
            part = jnp.zeros((1, BN), F32)
            for start, stop in row_blocks(first, last):
                score = jnp.dot(feats[start:stop, :], w, preferred_element_type=F32)
                e = jnp.exp2(score * (LOG2E / TEACHER_TEMP))
                out[slot, start:stop, :] = e.astype(BF16)
                part = part + jnp.sum(e, axis=0, keepdims=True)
            heads.append(part)
        leave(j, slot).start()
        put_columns(j, heads, sums)

    stream(proto_source(idx[0], protos), buf, sem, steps, step)
    for j in range(max(steps - 4, 0), steps):
        leave(j, j % 4).wait()


def teacher_pass(idx, own, other, protos, crops, copies):
    rows, width = own.shape
    columns = protos.shape[1] // 2
    return call(
        functools.partial(teacher_kernel, crops),
        [array((rows, columns), BF16), array((copies, 2 * columns // 128, 128))],
        [idx, own, other, protos],
        "svvh",
        "hv",
        scratch=[
            pltpu.VMEM((rows, width), BF16),
            pltpu.VMEM((4, rows, BN), BF16),
            pltpu.SemaphoreType.DMA((4,)),
        ]
        + proto_scratch(width, columns),
        flops=2 * rows * width * columns,
        traffic=2 * rows * columns,
    )


def student_kernel(crops, idx, own, other, protos, total, mix, feats, acc, buf, sem):
    rows = feats.shape[0]
    size = buf.shape[2]
    place_rows(idx[0], crops, rows // 2, rows // 2, own, other, feats)
    acc[...] = jnp.zeros_like(acc)
    mix[...] = jnp.zeros_like(mix)

    def step(j, block):
        w = unit_cols(block[...])[0].astype(BF16)
        for start, stop in row_blocks(0, rows):
            score = jnp.dot(feats[start:stop, :], w, preferred_element_type=F32)
            p = jnp.exp2(score * (LOG2E / STUDENT_TEMP))
            part = p[:, :128]
            for t in range(1, size // 128):
                part = part + p[:, 128 * t : 128 * (t + 1)]
            acc[start:stop, :] += part
            mix[start:stop, :] += lax.dot_general(
                p.astype(BF16), w, (((1,), (1,)), ((), ())), preferred_element_type=F32
            )

    stream(proto_source(idx[0], protos, size), buf, sem, protos.shape[1] // 2 // size, step)
    for t in range(rows // 128):
        block = jnp.transpose(acc[128 * t : 128 * (t + 1), :])
        total[t : t + 1, :] = jnp.sum(block, axis=0, keepdims=True)


def student_pass(idx, own, other, protos, crops):
    rows, width = own.shape
    columns = protos.shape[1] // 2
    return call(
        functools.partial(student_kernel, crops),
        [array((rows // 128, 128)), array((rows, width))],
        [idx, own, other, protos],
        "svvh",
        scratch=[pltpu.VMEM((rows, width), BF16), pltpu.VMEM((rows, 128), F32)]
        + proto_scratch(width, columns, 2 * BN),
        flops=4 * rows * width * columns,
        traffic=2 * width * columns,
    )


def row_copies(source, dest, sems):
    return [
        pltpu.make_async_copy(
            source.at[pl.ds(128 * i, 128), :], dest.at[pl.ds(128 * i, 128), :], sems.at[i]
        )
        for i in range(source.shape[0] // 128)
    ]


def column_copies(source, dest, sems):
    return [
        pltpu.make_async_copy(
            source.at[:, pl.ds(BN * j, BN)], dest.at[:, pl.ds(BN * j, BN)], sems.at[j]
        )
        for j in range(source.shape[1] // BN)
    ]


def expo_scratch(expo, blocks):
    return [pltpu.VMEM(expo.shape, BF16), pltpu.SemaphoreType.DMA((blocks,))]


def sum_rows(crops, expo, copies_in, colscale, out):
    copies = out.shape[0]
    rows, columns = expo.shape
    per_head = columns // 128

    for i in range(rows // 128):
        copies_in[i].wait()
        head = 0 if i < 2 * crops // 128 else 1
        at = 128 * i

        def chunk(k, acc):
            e = expo[pl.ds(at, 128), pl.ds(pl.multiple_of(k * 128, 128), 128)].astype(F32)
            return acc + e * colscale[pl.ds(head * per_head + k, 1), :]

        acc = lax.fori_loop(0, per_head, chunk, jnp.zeros((128, 128), F32), unroll=8)
        sums = jnp.sum(jnp.transpose(acc), axis=0, keepdims=True)
        out[:, i : i + 1, :] = jnp.broadcast_to(sums[None], (copies, 1, 128))


def row_kernel(crops, extra, expo, colparts, *refs):
    out, colscale, buf, sems = refs[-4:]
    copies_in = row_copies(expo, buf, sems)
    for copy in copies_in:
        copy.start()
    if extra:
        total = refs[0]
        count = total.shape[0]
        out[:, count:, :] = jnp.broadcast_to(total[...][None], (out.shape[0], count, 128))
    colscale[...] = 1.0 / jnp.sum(colparts[...], axis=0)
    sum_rows(crops, buf, copies_in, colscale, out)


def row_pass(expo, colparts, total, crops, copies):
    rows, columns = expo.shape
    extra = total is not None
    return call(
        functools.partial(row_kernel, crops, extra),
        array((copies, rows // 128 * (2 if extra else 1), 128)),
        [expo, colparts] + ([total] if extra else []),
        "hvv" if extra else "hv",
        scratch=[pltpu.VMEM((2 * columns // 128, 128), F32)] + expo_scratch(expo, rows // 128),
        flops=2 * rows * columns,
        traffic=2 * rows * columns,
    )


def target_kernel(crops, idx, expo, colparts, protos, mine, theirs, target, colscale, ebuf, esem, buf, sem):
    rows, columns = expo.shape
    steps = columns // BN
    copies_in = column_copies(expo, ebuf, esem)
    for copy in copies_in:
        copy.start()
    colscale[...] = 1.0 / jnp.sum(colparts[...], axis=0)
    target[...] = jnp.zeros_like(target)

    def step(j, block):
        wnorm = unit_cols(block[...])[0]
        at = pl.multiple_of(j * BN, BN)
        pltpu.make_async_copy(
            expo.at[:, pl.ds(at, BN)], ebuf.at[:, pl.ds(at, BN)], esem.at[j]
        ).wait()
        for head, (first, last) in enumerate(((0, 2 * crops), (2 * crops, rows))):
            w = (wnorm * get_columns(j, head, colscale)).astype(BF16)
            target[first:last, :] += lax.dot_general(
                ebuf[first:last, pl.ds(at, BN)],
                w,
                (((1,), (1,)), ((), ())),
                preferred_element_type=F32,
            )

    stream(proto_source(idx[0], protos), buf, sem, steps, step)
    part_rows(crops, idx, target, mine, theirs)


def target_pass(idx, expo, colparts, protos, crops):
    rows, columns = expo.shape
    width = protos.shape[0]
    return call(
        functools.partial(target_kernel, crops),
        [array((rows // 2, width)), array((rows // 2, width))],
        [idx, expo, colparts, protos],
        "shvh",
        scratch=[pltpu.VMEM((rows, width), F32), pltpu.VMEM((2 * columns // 128, 128), F32)]
        + expo_scratch(expo, columns // BN)
        + proto_scratch(width, columns),
        flops=2 * rows * columns * width,
        traffic=2 * rows * columns,
    )


def split3(v):
    high = v.astype(BF16)
    rest = v - high.astype(F32)
    middle = rest.astype(BF16)
    low = (rest - middle.astype(F32)).astype(BF16)
    pad = jnp.zeros((13, v.shape[1]), F32)
    parts = [high.astype(F32), middle.astype(F32), low.astype(F32), pad]
    return jnp.concatenate(parts, axis=0).astype(BF16)


def column_kernel(crops, expo, rowparts, out, buf, sems):
    rows, columns = expo.shape
    copies_in = column_copies(expo, buf, sems)
    for copy in copies_in:
        copy.start()
    scale = line_up(1.0 / jnp.sum(rowparts[:, : rows // 128, :], axis=0))
    spans = [(0, 2 * crops), (2 * crops, rows)]
    lefts = [split3(scale[:, first:last]) for first, last in spans]
    for j in range(columns // BN):
        copies_in[j].wait()
        heads = []
        for left, (first, last) in zip(lefts, spans):
            sums = jnp.dot(
                left, buf[first:last, j * BN : (j + 1) * BN], preferred_element_type=F32
            )
            heads.append(sums[0:1, :] + sums[1:2, :] + sums[2:3, :])
        put_columns(j, heads, out)


def column_pass(expo, rowparts, crops, copies):
    rows, columns = expo.shape
    return call(
        functools.partial(column_kernel, crops),
        array((copies, 2 * columns // 128, 128)),
        [expo, rowparts],
        "hv",
        scratch=expo_scratch(expo, columns // BN),
        flops=2 * rows * columns,
        traffic=2 * rows * columns,
    )


def part_source(idx, ny, protos):
    columns = protos.shape[1] // 2
    part = columns // ny
    at = pl.multiple_of(idx[0] * columns + idx[3] * part, 128)
    return protos.at[:, pl.ds(at, part)]


def stream_rows(ny, here, base, half, refs, buf, sem, ready, body):
    copies = [
        pltpu.make_async_copy(ref.at[pl.ds(base, half), :], buf.at[i], sem.at[i])
        for i, ref in enumerate(refs)
    ]
    for copy in copies:
        copy.start()
    ready()
    for i, copy in enumerate(copies):
        copy.wait()
        body(i // ny, lax.rem(here + ny - i % ny, ny), buf.at[i])


def wide_teacher_kernel(ny, crops, idx, protos, *refs):
    expo_d, expo_i, w, wbuf, out, osem, buf, sem, wsem = refs[2 * ny :]
    half = buf.shape[1]
    rest = half - crops
    fetch = pltpu.make_async_copy(part_source(idx, ny, protos), wbuf, wsem)
    fetch.start()
    leaving = []

    def ready():
        fetch.wait()
        w[...] = unit_cols(wbuf[...])[0].astype(BF16)

    def body(side, y, ref):
        place = 2 * y + jnp.where(idx[0] == side, 0, 1)
        slot = len(leaving) % 4
        if len(leaving) >= 4:
            for copy in leaving[-4]:
                copy.wait()
        feats = ref[...].astype(BF16)
        for start, stop in row_blocks(0, half):
            score = jnp.dot(feats[start:stop, :], w[...], preferred_element_type=F32)
            out[slot, start:stop, :] = jnp.exp2(score * (LOG2E / TEACHER_TEMP)).astype(BF16)
        at_d = pl.multiple_of(place * crops, 128)
        at_i = pl.multiple_of(place * rest, 128)
        copies = (
            pltpu.make_async_copy(
                out.at[slot, pl.ds(0, crops), :], expo_d.at[pl.ds(at_d, crops), :], osem.at[slot, 0]
            ),
            pltpu.make_async_copy(
                out.at[slot, pl.ds(crops, rest), :], expo_i.at[pl.ds(at_i, rest), :], osem.at[slot, 1]
            ),
        )
        for copy in copies:
            copy.start()
        leaving.append(copies)

    stream_rows(ny, idx[3], 0, half, refs[: 2 * ny], buf, sem, ready, body)
    for copies in leaving[-4:]:
        for copy in copies:
            copy.wait()


def wide_teacher_pass(idx, gathered, protos, crops):
    ny = len(gathered) // 2
    rows, width = gathered[0].shape
    half = rows // 2
    part = protos.shape[1] // 2 // ny
    return call(
        functools.partial(wide_teacher_kernel, ny, crops),
        [array((2 * ny * crops, part), BF16), array((2 * ny * (half - crops), part), BF16)],
        [idx, protos, *gathered],
        "sh" + "h" * len(gathered),
        "hh",
        scratch=[
            pltpu.VMEM((width, part), BF16),
            pltpu.VMEM((width, part), BF16),
            pltpu.VMEM((4, half, part), BF16),
            pltpu.SemaphoreType.DMA((4, 2)),
            pltpu.VMEM((2 * ny, half, width), F32),
            pltpu.SemaphoreType.DMA((2 * ny,)),
            pltpu.SemaphoreType.DMA,
        ],
        flops=2 * 2 * ny * half * width * part,
        traffic=8 * ny * half * width,
    )


def wide_student_kernel(ny, crops, idx, protos, *refs):
    gathered = refs[: 2 * ny]
    refs = refs[2 * ny :]
    totals = refs[:ny]
    out, wnorm_out, turned_d, turned_i, w, wbuf, scale, left, expo, buf, sem, wsem = refs[ny:]
    half = buf.shape[1]
    rest = half - crops
    sub = totals[0].shape[0]
    fetch = pltpu.make_async_copy(part_source(idx, ny, protos), wbuf, wsem)
    fetch.start()
    for s in range(ny):
        y = lax.rem(idx[3] + ny - s, ny)
        scale[pl.ds(pl.multiple_of(y * sub, sub), sub), :] = GRAD_SCALE / totals[s][...]
    out[...] = jnp.zeros_like(out)

    def ready():
        fetch.wait()
        wnorm_out[...] = unit_cols(wbuf[...])[0]
        w[...] = wnorm_out[...].astype(BF16)

    def body(side, y, ref):
        core = jnp.where(idx[0] == side, 0, 1)
        place = 2 * y + core
        feats = ref[...].astype(BF16)
        turned = jnp.transpose(feats.astype(F32))
        turned_d[:, pl.ds(pl.multiple_of(place * crops, 128), crops)] = turned[:, :crops].astype(BF16)
        turned_i[:, pl.ds(pl.multiple_of(place * rest, 128), rest)] = turned[:, crops:].astype(BF16)
        lines = [scale[pl.ds(y * sub + core * (crops // 128) + t, 1), :] for t in range(crops // 128)]
        first = y * sub + 2 * crops // 128 + core * (rest // 128)
        lines += [scale[pl.ds(first + t, 1), :] for t in range(rest // 128)]
        left[...] = (turned * jnp.concatenate(lines, axis=1)).astype(BF16)
        for start, stop in row_blocks(0, half):
            score = jnp.dot(feats[start:stop, :], w[...], preferred_element_type=F32)
            expo[start:stop, :] = jnp.exp2(score * (LOG2E / STUDENT_TEMP)).astype(BF16)
        out[...] += jnp.dot(left[...], expo[...], preferred_element_type=F32)

    stream_rows(ny, idx[3], half, half, gathered, buf, sem, ready, body)


def wide_student_pass(idx, gathered, protos, totals, crops):
    ny = len(gathered) // 2
    rows, width = gathered[0].shape
    half = rows // 2
    part = protos.shape[1] // 2 // ny
    return call(
        functools.partial(wide_student_kernel, ny, crops),
        [
            array((width, part)),
            array((width, part)),
            array((width, 2 * ny * crops), BF16),
            array((width, 2 * ny * (half - crops)), BF16),
        ],
        [idx, protos, *gathered, *totals],
        "sh" + "h" * len(gathered) + "v" * ny,
        scratch=[
            pltpu.VMEM((width, part), BF16),
            pltpu.VMEM((width, part), BF16),
            pltpu.VMEM((ny * rows // 128, 128), F32),
            pltpu.VMEM((width, half), BF16),
            pltpu.VMEM((half, part), BF16),
            pltpu.VMEM((2 * ny, half, width), F32),
            pltpu.SemaphoreType.DMA((2 * ny,)),
            pltpu.SemaphoreType.DMA,
        ],
        flops=4 * 2 * ny * half * width * part,
        traffic=8 * ny * half * width,
    )


def weight_kernel(ny, crops, idx, prob_in, wnorm_in, turned_d_in, turned_i_in, expo_d, expo_i, colparts, rowparts, out, left_d, left_i, scales, rowscale, buf_d, buf_i, sems_d, sems_i, targets, prob, wnorm, turned_d, turned_i, sem):
    loads = [
        pltpu.make_async_copy(src, dst, sem.at[i])
        for i, (src, dst) in enumerate(
            ((turned_d_in, turned_d), (turned_i_in, turned_i), (prob_in, prob), (wnorm_in, wnorm))
        )
    ]
    for copy in loads[:2]:
        copy.start()
    copies, _, _ = out.shape
    width, part = prob.shape
    own = width // copies
    streams = []
    for expo, buf, sems in ((expo_d, buf_d, sems_d), (expo_i, buf_i, sems_i)):
        size = buf.shape[0] // sems.shape[0]
        streams.append(
            [
                pltpu.make_async_copy(
                    expo.at[pl.ds(i * size, size), :], buf.at[pl.ds(i * size, size), :], sems.at[i]
                )
                for i in range(sems.shape[0])
            ]
        )
    for copy in streams[0] + streams[1] + loads[2:]:
        copy.start()
    group = rowparts.shape[0] // ny
    sub = rowparts.shape[1]
    scales[...] = GRAD_SCALE / jnp.sum(colparts[...], axis=0)
    for y in range(ny):
        rowscale[y * sub : (y + 1) * sub, :] = 1.0 / jnp.sum(
            rowparts[y * group : (y + 1) * group], axis=0
        )
    cd = crops // 128
    ci = sub // 2 - cd
    lines_d, lines_i = [], []
    for y in range(ny):
        for core in range(2):
            for t in range(cd):
                at = y * sub + core * cd + t
                lines_d.append(rowscale[at : at + 1, :])
            for t in range(ci):
                at = y * sub + 2 * cd + core * ci + t
                lines_i.append(rowscale[at : at + 1, :])
    loads[0].wait()
    loads[1].wait()
    left_d[...] = (turned_d[...].astype(F32) * jnp.concatenate(lines_d, axis=1)).astype(BF16)
    left_i[...] = (turned_i[...].astype(F32) * jnp.concatenate(lines_i, axis=1)).astype(BF16)
    per_head = scales.shape[0] // 2
    first = idx[3] * (part // 128)
    for head, (left, buf) in enumerate(((left_d, buf_d), (left_i, buf_i))):
        size = buf.shape[0] // len(streams[head])
        for i, copy in enumerate(streams[head]):
            copy.wait()
            span = slice(i * size, (i + 1) * size)
            value = jnp.dot(left[:, span], buf[span, :], preferred_element_type=F32)
            if i == 0:
                targets[head] = value
            else:
                targets[head] += value
    loads[2].wait()
    loads[3].wait()
    for at in range(0, part, BN):
        span = slice(at, at + BN)
        wsum = prob[:, span]
        for head in range(2):
            base = head * per_head + first + at // 128
            line = [scales[pl.ds(base + t, 1), :] for t in range(BN // 128)]
            wsum = wsum - targets[head, :, span] * jnp.concatenate(line, axis=1)
        coldot = jnp.sum(wnorm[:, span] * wsum, axis=0, keepdims=True)
        for t in range(BN // 128):
            lanes = slice(128 * t, 128 * (t + 1))
            row = at // 128 + t
            for d in range(copies):
                out[d, row * own : (row + 1) * own, :] = wsum[d * own : (d + 1) * own, lanes]
            tail = part // 128 * own + row
            out[:, tail : tail + 1, :] = jnp.broadcast_to(
                coldot[:, lanes][None], (copies, 1, 128)
            )


def weight_pass(idx, prob, wnorm, turned, expo, colparts, rowparts, crops, ny, copies):
    width, part = prob.shape
    lines = part // 128 * (width // copies + 1)
    rows = turned[0].shape[1] + turned[1].shape[1]
    return call(
        functools.partial(weight_kernel, ny, crops),
        array((copies, lines, 128)),
        [idx, prob, wnorm, *turned, *expo, colparts, rowparts],
        "shhhhhhvv",
        scratch=[
            pltpu.VMEM(turned[0].shape, BF16),
            pltpu.VMEM(turned[1].shape, BF16),
            pltpu.VMEM(colparts.shape[1:], F32),
            pltpu.VMEM((ny * rowparts.shape[1], 128), F32),
            pltpu.VMEM(expo[0].shape, BF16),
            pltpu.VMEM(expo[1].shape, BF16),
            pltpu.SemaphoreType.DMA((expo[0].shape[0] // 512,)),
            pltpu.SemaphoreType.DMA((expo[1].shape[0] // 512,)),
            pltpu.VMEM((2, width, part), F32),
            pltpu.VMEM((width, part), F32),
            pltpu.VMEM((width, part), F32),
            pltpu.VMEM(turned[0].shape, BF16),
            pltpu.VMEM(turned[1].shape, BF16),
            pltpu.SemaphoreType.DMA((4,)),
        ],
        flops=2 * rows * width * part,
        traffic=2 * rows * part,
    )


def norm_kernel(protos, out, buf, sem):
    blocks, size, _ = buf.shape
    copies = [
        pltpu.make_async_copy(protos.at[pl.ds(i * size, size), :], buf.at[i], sem.at[i])
        for i in range(blocks)
    ]
    for copy in copies:
        copy.start()
    for i, copy in enumerate(copies):
        copy.wait()
        w = buf[i].astype(F32)
        part = jnp.sum(w * w, axis=0, keepdims=True)
        out[...] = part if i == 0 else out[...] + part
    out[...] = lax.rsqrt(out[...] + EPS)


def norm_pass(protos):
    width, columns = protos.shape
    return call(
        norm_kernel,
        array((1, columns)),
        [protos],
        "h",
        scratch=[pltpu.VMEM((8, width // 8, columns), BF16), pltpu.SemaphoreType.DMA((8,))],
        flops=3 * width * columns,
        traffic=2 * width * columns,
    )


def proto_kernel(nx, ny, idx, parts, protos, winv, out, rows, sem):
    own, columns = out.shape
    copies = parts.shape[0]
    part = columns // (2 * ny)
    tail = part // 128 * own
    at = pl.multiple_of(idx[2] * (2 * own), 2 * own)
    fetch = pltpu.make_async_copy(protos.at[pl.ds(at, 2 * own), :], rows, sem)
    fetch.start()
    fetch.wait()
    for y in range(ny):
        for core in range(2):
            for t in range(part // 128):
                first = core * (columns // 2) + y * part + 128 * t
                lanes = slice(first, first + 128)
                wsum = jnp.zeros((own, 128), F32)
                coldot = jnp.zeros((1, 128), F32)
                for x in range(nx):
                    source = (x * ny + y) * 2 + core
                    wsum = wsum + parts[source, t * own : (t + 1) * own, :]
                    coldot = coldot + parts[source, tail + t : tail + t + 1, :]
                inv = winv[:, lanes]
                both = rows[:, lanes].astype(F32)
                wnorm = jnp.where(idx[0] == 0, both[:own, :], both[own:, :]) * inv
                out[:, lanes] = (wsum - wnorm * coldot) * inv


def proto_pass(idx, parts, protos, winv, nx, ny):
    width, columns = protos.shape
    own = width // parts.shape[0]
    return call(
        functools.partial(proto_kernel, nx, ny),
        array((own, columns)),
        [idx, parts, protos, winv],
        "svhv",
        scratch=[pltpu.VMEM((2 * own, columns), BF16), pltpu.SemaphoreType.DMA],
    )


def spread_row(line):
    return jnp.transpose(jnp.broadcast_to(line, (128, 128)))


def scaled_kernel(crops, idx, mix, totals, mine, theirs, buf):
    rows, width = mix.shape
    prob = GRAD_SCALE / totals[...]
    for t in range(rows // 128):
        span = slice(128 * t, 128 * (t + 1))
        p = jnp.concatenate([spread_row(prob[t : t + 1, :])] * (width // 128), axis=1)
        buf[span, :] = mix[span, :] * p
    part_rows(crops, idx, buf, mine, theirs)


def part_rows(crops, idx, buf, mine, theirs):
    rest = mine.shape[0] - crops
    for side, ref in ((idx[0], mine), (1 - idx[0], theirs)):
        ref[:crops, :] = buf[pl.ds(pl.multiple_of(side * crops, crops), crops), :]
        ref[crops:, :] = buf[pl.ds(pl.multiple_of(2 * crops + side * rest, 128), rest), :]


def part_pass(idx, mix, totals, crops):
    rows, width = mix.shape
    return call(
        functools.partial(scaled_kernel, crops),
        [array((rows // 2, width)), array((rows // 2, width))],
        [idx, mix, totals],
        "svv",
        scratch=[pltpu.VMEM((rows, width), F32)],
    )


def pack_rows(nz, crops, mine, came, out):
    half = mine.shape[0]
    chunk = half // nz
    share = crops // nz
    rest = chunk - share
    for z in range(nz):
        for src, dst, size in ((z * share, z * chunk, share), (crops + z * rest, z * chunk + share, rest)):
            out[dst : dst + size, :] = mine[src : src + size, :] + came[src : src + size, :]


def halve(idx, bit, total, keep, send):
    size = total.shape[0] // 2
    side = lax.rem(idx[1] // bit, 2)
    keep[...] = total[pl.ds(pl.multiple_of(side * size, 64), size), :]
    send[...] = total[pl.ds(pl.multiple_of((1 - side) * size, 64), size), :]


def pack_half_kernel(nz, crops, idx, mine, came, keep, send, total):
    pack_rows(nz, crops, mine, came, total)
    halve(idx, nz // 2, total, keep, send)


def pack_half_pass(idx, mine, came, nz, crops):
    rows, width = mine.shape
    return call(
        functools.partial(pack_half_kernel, nz, crops),
        [array((rows // 2, width)), array((rows // 2, width))],
        [idx, mine, came],
        "svv",
        scratch=[pltpu.VMEM((rows, width), F32)],
    )


def fold_kernel(bit, idx, mine, came, keep, send, total):
    total[...] = mine[...] + came[...]
    halve(idx, bit, total, keep, send)


def fold_pass(idx, mine, came, bit):
    rows, width = mine.shape
    return call(
        functools.partial(fold_kernel, bit),
        [array((rows // 2, width)), array((rows // 2, width))],
        [idx, mine, came],
        "svv",
        scratch=[pltpu.VMEM((rows, width), F32)],
    )


def mix_kernel(nz, ny, crops, bit, idx, rowparts, target, target_came, prob, prob_came, *refs):
    scale = refs[-1]
    total = refs[-2]
    sub = rowparts.shape[1]
    group = rowparts.shape[0] // ny
    cd = crops // 128
    ci = sub // 2 - cd
    row = GRAD_SCALE / jnp.sum(rowparts[pl.ds(idx[3] * group, group), :, :], axis=0)
    low = idx[0] == 0
    for t in range(cd + ci):
        a, b = (t, cd + t) if t < cd else (cd + t, cd + ci + t)
        line = jnp.where(low, row[a : a + 1, :], row[b : b + 1, :])
        scale[128 * t : 128 * (t + 1), :] = spread_row(line)
    rows, width = target.shape
    here = nz // 2
    chunk = rows // here
    share = crops // nz
    rest = chunk - share
    first = idx[1] // here * here
    for k in range(here):
        z = first + k
        for at, src, size in ((0, z * share, share), (share, crops + z * rest, rest)):
            r = scale[pl.ds(pl.multiple_of(src, 16), size), :]
            span = slice(k * chunk + at, k * chunk + at + size)
            value = target[span, :] + target_came[span, :]
            total[span, :] = (
                prob[span, :]
                + prob_came[span, :]
                - value * jnp.concatenate([r] * (width // 128), axis=1)
            )
    if bit:
        halve(idx, bit, total, refs[0], refs[1])


def mix_pass(idx, rowparts, target, target_came, prob, prob_came, nz, ny, crops, bit):
    rows, width = target.shape
    half = rowparts.shape[1] // 2 * 128
    shapes = [array((rows // 2, width))] * 2 if bit else array((rows, width))
    return call(
        functools.partial(mix_kernel, nz, ny, crops, bit),
        shapes,
        [idx, rowparts, target, target_came, prob, prob_came],
        "svvvvv",
        scratch=([pltpu.VMEM((rows, width), F32)] if bit else []) + [pltpu.VMEM((half, 128), F32)],
    )


def feature_kernel(count, chunks, patches, idx, mask, *refs):
    pieces = refs[:count]
    all_crops, all_rows, crop_out, patch_out, masked_rows, dense, total = refs[count:]
    z = idx[1]
    masked = mask.shape[1]
    crop_share = crop_out.shape[0]
    share = patch_out.shape[0]
    value = pieces[0][...]
    for piece in pieces[1:]:
        value = value + piece[...]
    total[...] = value
    chunk = total.shape[0] // chunks
    rest = chunk - crop_share
    for side in range(chunks):
        masked_rows[side * rest : (side + 1) * rest, :] = total[
            side * chunk + crop_share : (side + 1) * chunk, :
        ]
    crop_at = pl.multiple_of(z * crop_share, 16)
    patch_at = pl.multiple_of(z * share, 128)
    start = pl.multiple_of(lax.rem(z, chunks) * chunk, 16)
    dense[...] = jnp.zeros_like(dense)
    first_row = z * share
    first_image = first_row // patches
    offset = first_row - first_image * patches
    for image in range(masked_rows.shape[0] // masked):

        def put(m, _):
            at = mask[first_image + image, m] + image * patches - offset

            @pl.when(jnp.logical_and(at >= 0, at < share))
            def _():
                dense[pl.ds(at, 1), :] = masked_rows[pl.ds(image * masked + m, 1), :]

            return 0

        lax.fori_loop(0, masked, put, 0, unroll=4)

    def back(x, d):
        xf = x.astype(F32)
        inv = lax.rsqrt(jnp.sum(xf * xf, axis=-1, keepdims=True) + EPS)
        u = xf * inv
        return (d - u * jnp.sum(u * d, axis=-1, keepdims=True)) * inv

    crop_out[...] = back(all_crops[pl.ds(crop_at, crop_share), :], total[pl.ds(start, crop_share), :])
    patch_out[...] = back(all_rows[pl.ds(patch_at, share), :], dense[...])


def feature_pass(idx, mask, pieces, all_crops, all_rows, nz, patches, pair):
    crops, width = all_crops.shape
    crop_share = crops // nz
    share = all_rows.shape[0] // nz
    rows = pieces[0].shape[0]
    return call(
        functools.partial(feature_kernel, len(pieces), 2 if pair else 1, patches),
        [array((crop_share, width)), array((share, width))],
        [idx, mask, *pieces, all_crops, all_rows],
        "ss" + "v" * len(pieces) + "vv",
        scratch=[
            pltpu.VMEM((rows - (2 if pair else 1) * crop_share, width), F32),
            pltpu.VMEM((share, width), F32),
            pltpu.VMEM((rows, width), F32),
        ],
    )


def tie(*values):
    return lax.optimization_barrier(values)


def shifted(n, s):
    return [(i, (i + s) % n) for i in range(n)]


def local(
    sizes,
    student_crops,
    teacher_crops,
    student_patches,
    teacher_patches,
    patch_mask,
    student_protos,
    teacher_protos,
):
    nx, ny, nz = sizes
    images, masked = patch_mask.shape
    patches = student_patches.shape[0] // images
    crops = student_crops.shape[0]
    ix, iy, ic, iz = (lax.axis_index(a) for a in ("x", "y", "c", "z"))
    idx = jnp.stack([ic, iz, ix * ny + iy, iy]).astype(jnp.int32)
    swap = [(0, 1), (1, 0)]

    own = prep(teacher_crops, teacher_patches, student_crops, student_patches, patch_mask)
    other = lax.ppermute(own, "c", swap)
    up, down = shifted(ny, 1), shifted(ny, ny - 1)
    from_up = lax.ppermute(own, "y", up)
    from_down = lax.ppermute(own, "y", down) if ny > 2 else None
    expo, sums = teacher_pass(idx, own, other, teacher_protos, crops, nx * ny)
    sub = 2 * (crops + images * masked) // 128

    pair = student_patches.shape[0] // nz < patches

    def across(value, bit):
        return lax.ppermute(value, "z", [(i, i ^ bit) for i in range(nz)])

    colparts = lax.all_to_all(sums, ("x", "y"), 0, 0)
    total, mix = student_pass(idx, own, other, student_protos, crops)
    colparts, total, from_up, from_down = tie(colparts, total, from_up, from_down)
    ring = [own, from_up]
    while len(ring) < ny - 1:
        ring.append(lax.ppermute(ring[-1], "y", up))
    if ny > 2:
        ring.append(from_down)
    sums = row_pass(expo, colparts, total, crops, 2 * nz)
    rowparts = lax.all_to_all(sums, ("c", "z"), 0, 0)
    later_protos, _ = tie(student_protos, sums)
    winv = norm_pass(later_protos)
    rowparts, winv = tie(rowparts, winv)
    totals = jnp.sum(rowparts[:, sub:, :], axis=0)
    sums = column_pass(expo, rowparts, crops, nx * ny)

    colparts = lax.all_to_all(sums, ("x", "y"), 0, 0)
    totals, _ = tie(totals, sums)
    all_totals = [totals] + [lax.ppermute(totals, "y", shifted(ny, s)) for s in range(1, ny)]
    mine, theirs = part_pass(idx, mix, totals, crops)
    p_keep, p_send = pack_half_pass(idx, mine, lax.ppermute(theirs, "c", swap), nz, crops)
    p_came = across(p_send, nz // 2)
    colparts, p_came = tie(colparts, p_came)
    sums = row_pass(expo, colparts, None, crops, 2 * nz)
    sums, *ring = tie(sums, *ring)
    gathered = ring + [other] + [lax.ppermute(rows, "c", swap) for rows in ring[1:]]
    rowparts = lax.all_to_all(sums, ("c", "z"), 0, 0)
    sums = column_pass(expo, rowparts, crops, nx * ny)

    colparts = lax.all_to_all(sums, ("x", "y"), 0, 0)
    *gathered, _ = tie(*gathered, sums)
    wide_expo = wide_teacher_pass(idx, gathered, teacher_protos, crops)
    wide_expo, all_totals = list(wide_expo), list(all_totals)
    colparts, *both = tie(colparts, *wide_expo, *all_totals)
    wide_expo, all_totals = both[:2], both[2:]
    target_mine, target_theirs = target_pass(idx, expo, colparts, student_protos, crops)
    colparts, target_theirs = tie(colparts, target_theirs)
    sums = row_pass(expo, colparts, None, crops, 2 * nz * ny)
    target_came = lax.ppermute(target_theirs, "c", swap)
    keep, send = pack_half_pass(idx, target_mine, target_came, nz, crops)
    sums, send = tie(sums, send)
    rowparts = lax.all_to_all(sums, ("y", "c", "z"), 0, 0)
    came = across(send, nz // 2)
    *gathered, came, _ = tie(*gathered, came, sums)
    prob, wnorm, *turned = wide_student_pass(idx, gathered, student_protos, all_totals, crops)
    outgoing = weight_pass(
        idx, prob, wnorm, turned, wide_expo, colparts, rowparts, crops, ny, nx * ny * 2
    )
    parts = lax.all_to_all(outgoing, ("x", "y", "c"), 0, 0)
    proto_grad = proto_pass(idx, parts, student_protos, winv, nx, ny)
    bits = [nz >> k for k in range(2, nz.bit_length()) if nz >> k > (1 if pair else 0)]
    total = mix_pass(
        idx, rowparts, keep, came, p_keep, p_came, nz, ny, crops, bits[0] if bits else 0
    )
    pieces = [total]
    for i, bit in enumerate(bits):
        keep, send = total
        last = i + 1 == len(bits)
        pieces = [keep, across(send, bit)]
        if last and pair:
            pieces += [across(keep, 1), across(send, bit ^ 1)]
        elif not last:
            total = fold_pass(idx, *pieces, bits[i + 1])
    if pair and not bits:
        pieces.append(across(total, 1))
    crop_grad, patch_grad = feature_pass(
        idx, patch_mask, pieces, student_crops, student_patches, nz, patches, pair
    )
    return (proto_grad, crop_grad, patch_grad)


def solution(mesh):
    dp, nz = mesh.devices.shape
    nx = 4 if dp == 32 else 2
    ny = dp // (2 * nx)
    grid = Mesh(mesh.devices.reshape(nx, ny, 2, nz), ("x", "y", "c", "z"))
    rows = ("x", "y", "c")
    in_specs = (
        P(rows, None),
        P(rows, None),
        P(rows, None),
        P(rows, None),
        P(rows, None),
        P(None, "z"),
        P(None, "z"),
    )
    out_specs = (P(rows, "z"), P(rows + ("z",), None), P(rows + ("z",), None))
    return jax.shard_map(
        functools.partial(local, (nx, ny, nz)),
        mesh=grid,
        in_specs=in_specs,
        out_specs=out_specs,
        check_vma=False,
    )
```
